32 devices in a mesh: pb: 4 (over z), ctx: 8 (over y, x, core).
Axes of the slice: x: 2, y: 2, z: 4, core: 2. Of those that a mesh axis runs over, the one named last changes fastest.
Arguments:
- decoder_in: bfloat16 [4, 128, 768], P('pb'), may hold values from -6 to 6
- encoder_out: bfloat16 [4, 1920, 768], P('pb', 'ctx'), may hold values from -6 to 6
- self_projection: bfloat16 [768, 2304], P(('pb', 'ctx')), may hold values from -0.21875 to 0.21875
- self_output: bfloat16 [768, 768], P(('pb', 'ctx')), may hold values from -1 to 1
- cross_query: bfloat16 [768, 768], P(('pb', 'ctx')), may hold values from -0.21875 to 0.21875
- cross_memory: bfloat16 [768, 1536], P(('pb', 'ctx')), may hold values from -0.21875 to 0.21875
- cross_output: bfloat16 [768, 768], P(('pb', 'ctx')), may hold values from -6 to 6
- expand_weight: bfloat16 [768, 3072], P(('pb', 'ctx')), may hold values from -0.21875 to 0.21875
- contract_weight: bfloat16 [3072, 768], P(('pb', 'ctx')), may hold values from -0.109375 to 0.109375
- norm_gains: bfloat16 [3, 768], P(None, ('pb', 'ctx')), may hold values from 0.5 to 1.5
- bias_table: bfloat16 [32, 12], replicated, may hold values from -5 to 5
- bucket_index: int32 [128], replicated, may hold values from 0 to 31, as said below
- passage_mask: int32 [4, 1920], P('pb', 'ctx'), may hold values from 0 to 1, as said below
- target_length: int32 [4], P('pb'), may hold values from 32 to 128, as said below
- task_group: int32 [4], P('pb'), may hold values from 0 to 2
- cotangent: bfloat16 [4, 128, 768], P('pb'), may hold values from -6 to 6
Outputs:
- block_output: bfloat16 [4, 128, 768], P('pb')
- grad_decoder: bfloat16 [4, 128, 768], P('pb')
- grad_encoder: bfloat16 [4, 1920, 768], P('pb', 'ctx')
- grad_self_projection: float32 [768, 2304], P(('pb', 'ctx'))
- grad_self_output: float32 [768, 768], P(('pb', 'ctx'))
- grad_cross_query: float32 [768, 768], P(('pb', 'ctx'))
- grad_cross_memory: float32 [768, 1536], P(('pb', 'ctx'))
- grad_cross_output: float32 [768, 768], P(('pb', 'ctx'))
- grad_expand: float32 [768, 3072], P(('pb', 'ctx'))
- grad_contract: float32 [3072, 768], P(('pb', 'ctx'))
- grad_norm_gains: float32 [3, 768], P(None, ('pb', 'ctx'))
- grad_bias_table: float32 [32, 12], replicated
The draws below stay inside these ranges and needn't reach their ends.
Inputs may be any that keep to these rules, and one draw needn't show every extreme that they name: bucket_index is 0 at offset 0, equals the offset below 16, never falls, and is 31 at offset 128 - 1. `passage_mask`: each passage of 384 rows has a leading run of 96 or more real rows and padding after it; the last passage of every query is whole. `target_length`: every query with an even index has length 128.
All inputs are finite; a program needn't handle non-finite values.
Results may differ from the reference program's by a relative error of at most 0.022.
Values may be sent and summed in bfloat16 or wider, within the bound.
No kernel may reach another device: no remote copies, remote signals or barrier semaphores. Data moves between devices by JAX's collectives and lax.ppermute only.
A program may use at most 192 MiB of HBM per device.

```python
import jax
import jax.numpy as jnp
from jax import lax

D = 768
FF = 3072
HEADS = 12
HEAD_DIM = 64
BUCKETS = 32
TARGET = 128
PASSAGE = 384
QUERIES = 4
CONTEXT = 1920


def draw_bucket_index(key, part):
    key = jax.random.fold_in(key, 11)
    offsets = jnp.arange(TARGET)
    advance = jax.random.randint(key, (TARGET,), 0, 2)
    advance = jnp.where(offsets < BUCKETS // 2, 1, advance)
    advance = jnp.where(offsets == 0, 0, advance)
    running = jnp.minimum(jnp.cumsum(advance), BUCKETS - 1)
    return jnp.where(offsets == TARGET - 1, BUCKETS - 1, running).astype(jnp.int32)


def draw_passage_mask(key, part):
    key = jax.random.fold_in(key, 13)
    passages = CONTEXT // PASSAGE
    filled = jax.random.randint(key, (QUERIES, passages), PASSAGE // 4, PASSAGE + 1)
    filled = jnp.where(jnp.arange(passages)[None, :] == passages - 1, PASSAGE, filled)
    position = jnp.arange(CONTEXT) % PASSAGE
    owning = jnp.arange(CONTEXT) // PASSAGE
    bounds = jnp.take(filled, owning, axis=1)
    return (position[None, :] < bounds).astype(jnp.int32)


def draw_target_length(key, part):
    key = jax.random.fold_in(key, 12)
    lengths = jax.random.randint(key, (QUERIES,), TARGET // 4, TARGET + 1)
    leading = jnp.arange(QUERIES) % 2 == 0
    return jnp.where(leading, TARGET, lengths).astype(jnp.int32)


def plant(result, stream_key, smallest, largest):
    place = [jax.random.randint(jax.random.fold_in(stream_key, axis), (), 0, length) for axis, length in enumerate(result.shape)]
    main_axis = result.shape.index(max(result.shape))
    neighbour = place[:main_axis] + [(place[main_axis] + 1) % result.shape[main_axis]] + place[main_axis + 1:]
    return result.at[tuple(place)].set(smallest).at[tuple(neighbour)].set(largest)


def level_of(rng, shape, pieces, smallest, largest):
    gain, own = 1.0, jax.random.fold_in(rng, 6)
    for axis_at, shards_of in pieces:
        draws = jnp.exp(jax.random.uniform(jax.random.fold_in(own, axis_at), (shards_of,), jnp.float32, smallest / len(pieces), largest / len(pieces)))
        gain = gain * jnp.repeat(draws, shape[axis_at] // shards_of).reshape([-1 if axis == axis_at else 1 for axis in range(len(shape))])
    return gain


def centred(stream_key, shape, scale, most, pieces=(), held_as=jnp.bfloat16):
    level = level_of(stream_key, shape, pieces, -0.22, 0.18) if pieces else 1.0
    drawn = jax.random.normal(stream_key, shape, jnp.float32) * scale * level
    return jnp.minimum(jnp.maximum(drawn, -most), most).astype(held_as)


def setup_inputs(seed: int = 0) -> dict:
    keys = jax.random.split(jax.random.key(seed), 17)
    return {
        "decoder_in": centred(keys[0], (QUERIES, TARGET, D), 1.0, 6.0, ((0, 4),)),
        "encoder_out": centred(keys[1], (QUERIES, CONTEXT, D), 1.0, 6.0, ((0, 4), (1, 8))),
        "self_projection": centred(keys[2], (D, 3 * D), D ** -0.5, 0.21875, ((0, 32),)),
        "self_output": centred(keys[3], (D, D), 32 ** -0.5, 1.0, ((0, 32),)),
        "cross_query": centred(keys[4], (D, D), D ** -0.5, 0.21875, ((0, 32),)),
        "cross_memory": centred(keys[5], (D, 2 * D), D ** -0.5, 0.21875, ((0, 32),)),
        "cross_output": centred(keys[6], (D, D), 1.5, 6.0, ((0, 32),)),
        "expand_weight": centred(keys[7], (D, FF), D ** -0.5, 0.21875, ((0, 32),)),
        "contract_weight": centred(keys[8], (FF, D), FF ** -0.5, 0.109375, ((0, 32),)),
        "norm_gains": jnp.clip(1.0 + 0.1 * jax.random.normal(keys[9], (3, D), jnp.float32), 0.5, 1.5).astype(jnp.bfloat16),
        "bias_table": centred(keys[10], (BUCKETS, HEADS), 1.0, 5.0),
        "bucket_index": draw_bucket_index(jax.random.fold_in(keys[16], 71), 0),
        "passage_mask": draw_passage_mask(jax.random.fold_in(keys[16], 71), 0),
        "target_length": draw_target_length(jax.random.fold_in(keys[16], 71), 0),
        "task_group": plant(jax.random.randint(keys[14], (QUERIES,), 0, 3), jax.random.fold_in(keys[14], 1), 0, 2).astype(jnp.int32),
        "cotangent": centred(keys[15], (QUERIES, TARGET, D), 1.0, 6.0, ((0, 4),)),
    }


@jax.custom_vjp
def low(v):
    return lax.optimization_barrier(v.astype(jnp.bfloat16)).astype(jnp.float32)

@jax.custom_vjp
def low_back(v):
    return v

def low_keep(v):
    return (low(v), None)

def low_pass(kept, grad):
    return (grad,)

def back_keep(v):
    return (v, None)

def back_low(kept, grad):
    return (low(grad),)
low.defvjp(low_keep, low_pass)
low_back.defvjp(back_keep, back_low)
highest = lax.Precision.HIGHEST

def matmul(left, right):
    return jnp.matmul(left, right, precision=highest)

def rms_norm(values, scale):
    return values * lax.rsqrt(lax.optimization_barrier(jnp.mean(values * values, axis=-1, keepdims=True)) + 1e-06) * scale

def split_heads(values):
    return values.reshape(values.shape[0], HEADS, HEAD_DIM)

def attend(query_rows, key_rows, value_rows, added, allowed):
    scores = jnp.einsum('ihd,jhd->hij', split_heads(query_rows), split_heads(key_rows), precision=highest)
    scores = low_back(scores * HEAD_DIM ** (-0.5) + added)
    attention = jax.nn.softmax(jnp.where(allowed, scores, -1000000000.0), axis=-1)
    mixed = jnp.einsum('hij,jhd->ihd', low(attention), split_heads(value_rows), precision=highest)
    return low(low_back(mixed.reshape(mixed.shape[0], D)))

def one_query(weights, rel_bias, inputs, encoder, visible, length):
    projection, self_out, cross_in, memory_in, cross_out, expand, contract, gains = weights
    positions = jnp.arange(TARGET)
    allowed = (positions[None, :] <= positions[:, None]) & (positions[None, :] < length)
    normed_a = low(rms_norm(inputs, gains[0]))
    joined = low(low_back(matmul(normed_a, projection)))
    self_mix = attend(joined[:, :D], joined[:, D:2 * D], joined[:, 2 * D:], rel_bias, allowed)
    after_self = inputs + low_back(matmul(self_mix, self_out))
    normed_b = low(rms_norm(after_self, gains[1]))
    cross_query_rows = low(low_back(matmul(normed_b, cross_in)))
    memory = low(low_back(matmul(encoder, memory_in)))
    cross_mix = attend(cross_query_rows, memory[:, :D], memory[:, D:], 0.0, visible[None, :] > 0)
    after_cross = after_self + low_back(matmul(cross_mix, cross_out))
    normed_c = low(rms_norm(after_cross, gains[2]))
    hidden = low_back(matmul(normed_c, expand))
    active = low(jax.nn.gelu(hidden, approximate=True))
    return after_cross + low_back(matmul(active, contract))

def forward(decoder, encoder, weights, bias_grid, bucket_index, passage_mask, target_length):
    positions = jnp.arange(TARGET)
    offsets = jnp.clip(positions[:, None] - positions[None, :], 0, TARGET - 1)
    rel_bias = jnp.transpose(bias_grid[bucket_index[offsets]], (2, 0, 1))

    def single(query_item):
        return jax.checkpoint(one_query)(weights, rel_bias, query_item[0], query_item[1], query_item[2], query_item[3])
    return lax.map(single, (decoder, encoder, passage_mask, target_length))

def reference(decoder_in, encoder_out, self_projection, self_output, cross_query, cross_memory, cross_output, expand_weight, contract_weight, norm_gains, bias_table, bucket_index, passage_mask, target_length, task_group, cotangent):
    weights = tuple((entry.astype(jnp.float32) for entry in (self_projection, self_output, cross_query, cross_memory, cross_output, expand_weight, contract_weight, norm_gains)))

    def run(decoder, encoder, params, bias_grid):
        return forward(decoder, encoder, params, bias_grid, bucket_index, passage_mask, target_length)
    output, pullback = jax.vjp(run, decoder_in.astype(jnp.float32), encoder_out.astype(jnp.float32), weights, bias_table.astype(jnp.float32))
    positions = jnp.arange(TARGET)
    row_live = (positions[None, :] < target_length[:, None]).astype(jnp.float32)
    task_scale = jnp.where(task_group == 0, 1.0, jnp.where(task_group == 1, 0.5, 2.0)).astype(jnp.float32)
    seed_grad = cotangent.astype(jnp.float32) * (task_scale[:, None] * row_live)[:, :, None]
    grad_dec, grad_enc, grad_params, grad_grid = pullback(seed_grad)
    return (output.astype(jnp.bfloat16), grad_dec.astype(jnp.bfloat16), grad_enc.astype(jnp.bfloat16), grad_params[0], grad_params[1], grad_params[2], grad_params[3], grad_params[4], grad_params[5], grad_params[6], grad_params[7], grad_grid)
```

```python
import jax
import jax.numpy as jnp
from jax import lax
from jax.experimental import pallas as pl
from jax.experimental.pallas import tpu as pltpu
from jax.sharding import PartitionSpec as P

LOW, FULL = jnp.bfloat16, jnp.float32
MASKED = -1000000000.0
EPS = 1e-06
VMEM_BYTES = 56 * 1024 * 1024
HEAD = 64


def dot(left, right, left_axis=1, right_axis=0):
    return lax.dot_general(
        left,
        right,
        (((left_axis,), (right_axis,)), ((), ())),
        preferred_element_type=FULL,
    )


def dot_t(left, right):
    return dot(left, right, 1, 1)


def outer_sum(left, right):
    return dot(left, right, 0, 0)


def rms_unit(values):
    factor = lax.rsqrt(jnp.mean(values * values, axis=-1, keepdims=True) + EPS)
    return values * factor, factor


def norm_back(grad, unit, factor, gain):
    scaled = grad * gain
    return factor * (scaled - unit * jnp.mean(scaled * unit, axis=-1, keepdims=True))


def call(kernel, outs, args, scalars=0):
    spaces = [pltpu.SMEM] * scalars + [pltpu.VMEM] * (len(args) - scalars)
    return pl.pallas_call(
        kernel,
        out_shape=[jax.ShapeDtypeStruct(shape, dtype) for shape, dtype in outs],
        in_specs=[pl.BlockSpec(memory_space=space) for space in spaces],
        out_specs=[pl.BlockSpec(memory_space=pltpu.VMEM) for _ in outs],
        compiler_params=pltpu.CompilerParams(vmem_limit_bytes=VMEM_BYTES),
    )(*args)


def swap_ctx(values, mask):
    size = lax.axis_size("ctx")
    return lax.ppermute(values, "ctx", [(i, i ^ mask) for i in range(size)])


def chip_bits():
    return [b for b in range(1, 16) if (1 << b) < lax.axis_size("ctx")]


def core_groups():
    size = lax.axis_size("ctx")
    return [list(range(core, size, 2)) for core in range(2)]


def exchange(values, axis, groups=None):
    return lax.all_to_all(values, axis, 0, 0, tiled=True, axis_index_groups=groups)


def from_all(values, axis):
    size = lax.axis_size(axis)
    return exchange(jnp.broadcast_to(values[None], (size,) + values.shape), axis)


def place(core, chip, sources, widths):
    pb, ctx = lax.axis_size("pb"), lax.axis_size("ctx")
    rows = sources[0][0].shape[1]
    counts = len(sources)

    def kernel(core_ref, chip_ref, *refs):
        outs = refs[counts:]
        for ref, (array, first, chip_flip, core_flip) in zip(refs, sources):
            for z in range(array.shape[0]):
                slot = (first + z) * ctx + 2 * (chip_ref[0] ^ chip_flip) + (core_ref[0] ^ core_flip)
                at = 0
                for out, width in zip(outs, widths):
                    out[slot] = ref[z, :, at : at + width]
                    at += width

    return call(
        kernel,
        [((pb * ctx, rows, width), LOW) for width in widths],
        [core[None], chip[None]] + [array for array, _, _, _ in sources],
        scalars=2,
    )


def gather_rows(core, chip, shards):
    pb, ctx = lax.axis_size("pb"), lax.axis_size("ctx")
    rows = shards[0].shape[0]
    if rows % 8 or ctx != 8 or pb % 2:
        return [lax.all_gather(s, ("pb", "ctx"), axis=0, tiled=True) for s in shards]
    joined = jnp.concatenate(shards, axis=1) if len(shards) > 1 else shards[0]
    own = from_all(joined, "pb")
    along_x, along_y = swap_ctx(own, 2), swap_ctx(own, 4)
    low = swap_ctx(along_x[: pb // 2], 4)
    high = swap_ctx(along_y[pb // 2 :], 2)
    sources = []
    for array, first, flip in (
        (own, 0, 0),
        (along_x, 0, 1),
        (along_y, 0, 2),
        (low, 0, 3),
        (high, pb // 2, 3),
    ):
        sources.append((array, first, flip, 0))
        sources.append((swap_ctx(array, 1), first, flip, 1))
    whole = place(core, chip, sources, [s.shape[1] for s in shards])
    return [w.reshape(pb * ctx * rows, w.shape[2]) for w in whole]


def halves(values, core):
    middle = values.shape[-1] // 2
    low, high = values[..., :middle], values[..., middle:]
    return jnp.where(core == 0, low, high), jnp.where(core == 0, high, low)


def join(mine, other, core):
    return jnp.where(
        core == 0,
        jnp.concatenate([mine, other], axis=-1),
        jnp.concatenate([other, mine], axis=-1),
    )


def sum_ctx(values, core):
    mine, other = halves(values, core)
    total = mine + swap_ctx(other.astype(LOW), 1).astype(FULL)
    for bit in chip_bits():
        sent = total.astype(LOW)
        total = sent.astype(FULL) + swap_ctx(sent, 1 << bit).astype(FULL)
    sent = total.astype(LOW)
    return join(sent, swap_ctx(sent, 1), core)


def to_owners(partial):
    return jnp.sum(exchange(partial.astype(LOW), "pb").astype(FULL), axis=0)


def lane_mask(values, side):
    lanes = lax.broadcasted_iota(jnp.int32, values.shape, 1)
    middle = values.shape[1] // 2
    keep = lanes < middle if side == 0 else lanes >= middle
    return jnp.where(keep, values, jnp.zeros_like(values))


def pick(low, high):
    lanes = lax.broadcasted_iota(jnp.int32, low.shape, 1)
    return jnp.where(lanes < low.shape[1] // 2, low, high)


def self_kernel(
    length, x, proj, self_out, cross_in, gains, table, p1, probs, mix, x1, h1, h2, cq
):
    rows, width = x.shape
    heads = probs.shape[0]
    pair = 2 * (width // heads)
    inverse = (width // heads) ** (-0.5)
    xf = x[...].astype(FULL)
    unit, _ = rms_unit(xf)
    h1[...] = (unit * gains[0:1, :]).astype(LOW)
    p1[...] = dot(h1[...], proj[...]).astype(LOW)
    row = lax.broadcasted_iota(jnp.int32, (rows, rows), 0)
    col = lax.broadcasted_iota(jnp.int32, (rows, rows), 1)
    allowed = (col <= row) & (col < length[0])
    for g in range(heads // 2):
        at = g * pair
        q = p1[:, at : at + pair]
        k = p1[:, width + at : width + at + pair]
        v = p1[:, 2 * width + at : 2 * width + at + pair]
        mixed = []
        for side in range(2):
            head = 2 * g + side
            bias = pltpu.roll(
                jnp.broadcast_to(table[head : head + 1, :], (rows, rows)),
                1,
                axis=1,
                stride=1,
                stride_axis=0,
            )
            scores = jnp.where(allowed, dot_t(lane_mask(q, side), k) * inverse + bias, MASKED)
            powers = jnp.exp(scores - jnp.max(scores, axis=-1, keepdims=True))
            prob = powers / jnp.sum(powers, axis=-1, keepdims=True)
            probs[head] = prob
            mixed.append(dot(prob.astype(LOW), v))
        mix[:, at : at + pair] = pick(*mixed).astype(LOW)
    after = xf + dot(mix[...], self_out[...])
    x1[...] = after
    unit, _ = rms_unit(after)
    h2[...] = (unit * gains[1:2, :]).astype(LOW)
    cq[...] = dot(h2[...], cross_in[...]).astype(LOW)


def split_three(values):
    high = values.astype(LOW)
    rest = values - high.astype(FULL)
    middle = rest.astype(LOW)
    return high, middle, (rest - middle.astype(FULL)).astype(LOW)


def pack_stats(tops, totals):
    rows = tops[0].shape[0]
    lanes = lax.broadcasted_iota(jnp.int32, (rows, 128), 1)
    columns = jnp.zeros((rows, 128), FULL)
    for index, column in enumerate(tops + totals):
        columns = jnp.where(lanes // 3 == index, column, columns)
    high, middle, low = (part.astype(FULL) for part in split_three(columns))
    kind = lanes % 3
    return jnp.where(kind == 0, high, jnp.where(kind == 1, middle, low)).astype(LOW)


def read_stats(packed, heads):
    values = packed.astype(FULL)
    columns = [
        values[:, 3 * i : 3 * i + 1] + values[:, 3 * i + 1 : 3 * i + 2] + values[:, 3 * i + 2 : 3 * i + 3]
        for i in range(2 * heads)
    ]
    return columns[:heads], columns[heads:]


def cross_kernel(core, cq, memory, visible, mine, other):
    rows, width = cq.shape
    half = width // 2
    heads = width // HEAD
    inverse = HEAD ** (-0.5)
    seen = visible[...] > 0
    tops, totals, mixes = [], [], []
    for g in range(heads // 2):
        at = g * 2 * HEAD
        q = cq[:, at : at + 2 * HEAD]
        k = memory[:, at : at + 2 * HEAD]
        v = memory[:, width + at : width + at + 2 * HEAD]
        mixed = []
        for side in range(2):
            scores = jnp.where(seen, dot_t(lane_mask(q, side), k) * inverse, MASKED)
            top = jnp.max(scores, axis=-1, keepdims=True)
            powers = jnp.where(seen, jnp.exp(scores - top), 0.0)
            tops.append(top)
            totals.append(jnp.sum(powers, axis=-1, keepdims=True))
            mixed.append(dot(powers.astype(LOW), v))
        mixes.append(pick(*mixed).astype(LOW))
    low = jnp.concatenate(mixes[: heads // 4], axis=1)
    high = jnp.concatenate(mixes[heads // 4 :], axis=1)
    stats = pack_stats(tops, totals)
    first = core[0] == 0
    mine[:, :half] = jnp.where(first, low, high)
    other[:, :half] = jnp.where(first, high, low)
    mine[:, half:] = stats
    other[:, half:] = stats


def spread(columns):
    rows = columns[0].shape[0]
    return jnp.concatenate(
        [
            pick(
                jnp.broadcast_to(columns[g], (rows, 2 * HEAD)),
                jnp.broadcast_to(columns[g + 1], (rows, 2 * HEAD)),
            )
            for g in range(0, len(columns), 2)
        ],
        axis=1,
    )


def merge(core, order, parts, heads, final):
    ways = len(parts)
    rows, columns = parts[0].shape
    half = columns - 128

    def kernel(core_ref, order_ref, *refs):
        packed = [ref[...] for ref in refs[:ways]]
        step = 1
        while step < ways:
            flip = (order_ref[0] & step) != 0
            packed = [jnp.where(flip, packed[i ^ step], packed[i]) for i in range(ways)]
            step *= 2
        stats = [read_stats(p[:, half:], heads) for p in packed]
        first = core_ref[0] == 0
        tops, totals, scales = [], [], []
        for h in range(heads):
            top = stats[0][0][h]
            for other in stats[1:]:
                top = jnp.maximum(top, other[0][h])
            scale = [jnp.exp(s[0][h] - top) for s in stats]
            terms = [s[1][h] * w for s, w in zip(stats, scale)]
            while len(terms) > 1:
                terms = [a + b for a, b in zip(terms[0::2], terms[1::2])]
            if final:
                scale = [w / terms[0] for w in scale]
            tops.append(top)
            totals.append(terms[0])
            scales.append(scale)
        terms = []
        for i in range(ways):
            mine = [
                jnp.where(first, scales[h][i], scales[h + heads // 2][i]) for h in range(heads // 2)
            ]
            terms.append(packed[i][:, :half].astype(FULL) * spread(mine))
        while len(terms) > 1:
            terms = [a + b for a, b in zip(terms[0::2], terms[1::2])]
        refs[ways][:, :half] = terms[0].astype(LOW)
        refs[ways][:, half:] = pack_stats(tops, totals)

    return call(
        kernel, [(parts[0].shape, LOW)], [core[None], order[None]] + list(parts), scalars=2
    )[0]


def gelu_parts(values):
    slope = (2.0 / jnp.pi) ** 0.5
    square = values * values
    bent = jnp.tanh(slope * (values + 0.044715 * values * square))
    active = 0.5 * values * (1.0 + bent)
    inner = slope * (1.0 + 3 * 0.044715 * square)
    return active, 0.5 * (1.0 + bent) + 0.5 * values * (1.0 - bent * bent) * inner


def task_rows(length, task, cot):
    rows = lax.broadcasted_iota(jnp.int32, cot.shape, 0)
    weight = jnp.where(task[0] == 0, 1.0, jnp.where(task[0] == 1, 0.5, 2.0)).astype(FULL)
    return jnp.where(rows < length[0], cot[...].astype(FULL) * weight, 0.0)


def feed_kernel(
    length,
    task,
    mix,
    x1,
    cross_out,
    gains,
    expand,
    contract,
    cot,
    x2,
    h3,
    active,
    low_out,
    grad_hidden,
    grad_h3,
    part_out,
):
    after = x1[...] + dot(mix[...], cross_out[...])
    x2[...] = after
    unit, _ = rms_unit(after)
    h3[...] = (unit * gains[2:3, :]).astype(LOW)
    hidden = dot(h3[...], expand[...])
    value, slope = gelu_parts(hidden)
    active[...] = value.astype(LOW)
    low_out[...] = task_rows(length, task, cot).astype(LOW)
    grad_active = dot_t(low_out[...], contract[...])
    grad_hidden[...] = (grad_active * slope).astype(LOW)
    grad_h3[...] = dot_t(grad_hidden[...], expand[...])
    part_out[...] = dot(active[...], contract[...])


def cross_back_kernel(
    length,
    task,
    grad_h3,
    x2,
    gains,
    cot,
    cross_out,
    cq,
    memory,
    visible,
    stats,
    mix,
    dx2,
    low_cross,
    grad_cq,
    grad_memory,
    gain_grad,
):
    rows, width = x2.shape
    heads = width // HEAD
    pair = 2 * HEAD
    inverse = HEAD ** (-0.5)
    unit, factor = rms_unit(x2[...])
    grad = grad_h3[...].astype(FULL)
    gain_grad[...] = jnp.sum(grad * unit, axis=0, keepdims=True)
    back = task_rows(length, task, cot) + norm_back(grad, unit, factor, gains[2:3, :])
    dx2[...] = back
    low_cross[...] = back.astype(LOW)
    grad_mix = dot_t(low_cross[...], cross_out[...]).astype(LOW)
    seen = visible[...] > 0
    tops, totals = read_stats(stats[...], heads)
    for g in range(heads // 2):
        at = g * pair
        q = cq[:, at : at + pair]
        k = memory[:, at : at + pair]
        v = memory[:, width + at : width + at + pair]
        do = grad_mix[:, at : at + pair]
        weighed = do.astype(FULL) * mix[:, at : at + pair].astype(FULL)
        queries, keys, values = [], [], []
        for side in range(2):
            head = 2 * g + side
            qs, ds = lane_mask(q, side), lane_mask(do, side)
            scores = dot_t(qs, k) * inverse
            scores = jnp.where(seen, scores, MASKED)
            prob = jnp.where(seen, jnp.exp(scores - tops[head]) / totals[head], 0.0)
            rho = jnp.sum(lane_mask(weighed, side), axis=-1, keepdims=True)
            grad_scores = (prob * (dot_t(ds, v) - rho)).astype(LOW)
            queries.append(dot(grad_scores, k))
            keys.append(outer_sum(grad_scores, qs))
            values.append(outer_sum(prob.astype(LOW), ds))
        grad_cq[:, at : at + pair] = pick(*queries) * inverse
        grad_memory[:, at : at + pair] = ((keys[0] + keys[1]) * inverse).astype(LOW)
        grad_memory[:, width + at : width + at + pair] = (values[0] + values[1]).astype(LOW)


def self_back_kernel(
    grad_cq,
    cross_in,
    x1,
    gains,
    dx2,
    self_out,
    p1,
    probs,
    x,
    proj,
    low_self,
    grad_p1,
    grad_x,
    gain_grads,
    diagonal,
):
    rows, width = x.shape
    heads = probs.shape[0]
    pair = 2 * (width // heads)
    inverse = (width // heads) ** (-0.5)
    grad = dot_t(grad_cq[...], cross_in[...])
    unit, factor = rms_unit(x1[...])
    gain_grads[1:2, :] = jnp.sum(grad * unit, axis=0, keepdims=True)
    dx1 = dx2[...] + norm_back(grad, unit, factor, gains[1:2, :])
    low_self[...] = dx1.astype(LOW)
    row = lax.broadcasted_iota(jnp.int32, (rows, rows), 0)
    col = lax.broadcasted_iota(jnp.int32, (rows, rows), 1)
    flip = jnp.where(row + col == rows - 1, 1.0, 0.0).astype(LOW)
    grad_mix = dot_t(low_self[...], self_out[...]).astype(LOW)
    for g in range(heads // 2):
        at = g * pair
        q = p1[:, at : at + pair]
        k = p1[:, width + at : width + at + pair]
        v = p1[:, 2 * width + at : 2 * width + at + pair]
        do = grad_mix[:, at : at + pair]
        queries, keys, values = [], [], []
        for side in range(2):
            head = 2 * g + side
            ds = lane_mask(do, side)
            prob = probs[head]
            grad_probs = dot_t(ds, v)
            rho = jnp.sum(prob * grad_probs, axis=-1, keepdims=True)
            grad_scores = (prob * (grad_probs - rho)).astype(LOW)
            turned = pltpu.roll(dot(flip, grad_scores), 0, axis=1, stride=1, stride_axis=0)
            diagonal[head : head + 1, :] = jnp.sum(turned, axis=0, keepdims=True)
            queries.append(dot(grad_scores, k))
            keys.append(outer_sum(grad_scores, lane_mask(q, side)))
            values.append(outer_sum(prob.astype(LOW), ds))
        grad_p1[:, at : at + pair] = (pick(*queries) * inverse).astype(LOW)
        grad_p1[:, width + at : width + at + pair] = ((keys[0] + keys[1]) * inverse).astype(LOW)
        grad_p1[:, 2 * width + at : 2 * width + at + pair] = (values[0] + values[1]).astype(LOW)
    grad = dot_t(grad_p1[...], proj[...])
    unit, factor = rms_unit(x[...].astype(FULL))
    gain_grads[0:1, :] = jnp.sum(grad * unit, axis=0, keepdims=True)
    grad_x[...] = (dx1 + norm_back(grad, unit, factor, gains[0:1, :])).astype(LOW)


def body(
    decoder_in,
    encoder_out,
    self_projection,
    self_output,
    cross_query,
    cross_memory,
    cross_output,
    expand_weight,
    contract_weight,
    norm_gains,
    bias_table,
    bucket_index,
    passage_mask,
    target_length,
    task_group,
    cotangent,
):
    pb, ctx = lax.axis_size("pb"), lax.axis_size("ctx")
    mine_pb, mine_ctx = lax.axis_index("pb"), lax.axis_index("ctx")
    core = (mine_ctx & 1).astype(jnp.int32)
    chip = (mine_ctx >> 1).astype(jnp.int32)
    rows, width = decoder_in.shape[1:]
    passage = encoder_out.shape[1]
    buckets, heads = bias_table.shape
    share = self_projection.shape[0]
    hidden = expand_weight.shape[1]
    slab = contract_weight.shape[0]
    x = decoder_in[0]
    e = encoder_out[0]
    cot = cotangent[0]

    gain_columns = jnp.pad(norm_gains.T, ((0, 0), (0, 128 - norm_gains.shape[0])))
    proj, gain_rows = gather_rows(core, chip, [self_projection, gain_columns])
    self_out, cross_in, cross_out = gather_rows(
        core, chip, [self_output, cross_query, cross_output]
    )
    (memory_in,) = gather_rows(core, chip, [cross_memory])
    mixed = expand_weight.reshape(share, pb, ctx, slab).transpose(2, 0, 1, 3)
    mixed = exchange(mixed.reshape(ctx, share, pb * slab), "ctx")
    expand = from_all(mixed.reshape(ctx * share, pb * slab), "pb").reshape(width, pb * slab)
    contract = from_all(contract_weight, "pb").reshape(pb * slab, width)
    gains = gain_rows[:, : norm_gains.shape[0]].astype(FULL).T

    backward_bucket = bucket_index[::-1]
    hot = (jnp.arange(buckets)[:, None] == backward_bucket[None, :]).astype(LOW)
    table = outer_sum(bias_table, hot)
    table = jnp.pad(table, ((0, 16 - heads % 16 if heads % 16 else 0), (0, 0)))

    p1, probs, mix1, x1, h1, h2, cq = call(
        self_kernel,
        [
            ((rows, 3 * width), LOW),
            ((heads, rows, rows), FULL),
            ((rows, width), LOW),
            ((rows, width), FULL),
            ((rows, width), LOW),
            ((rows, width), LOW),
            ((rows, width), LOW),
        ],
        [target_length, x, proj, self_out, cross_in, gains, table],
        scalars=1,
    )
    memory = dot(e, memory_in).astype(LOW)
    mine, other = call(
        cross_kernel,
        [((rows, width // 2 + 128), LOW)] * 2,
        [core[None], cq, memory, passage_mask],
        scalars=1,
    )
    part = merge(core, core, [mine, swap_ctx(other, 1)], heads, False)
    parts = [part] + [swap_ctx(part, mask) for mask in range(2, ctx, 2)]
    part = merge(core, chip, parts, heads, True)
    stats = part[:, width // 2 :]
    part = part[:, : width // 2]
    mix2 = join(part, swap_ctx(part, 1), core)

    x2, h3, active, low_out, grad_hidden, grad_h3, part_out = call(
        feed_kernel,
        [
            ((rows, width), FULL),
            ((rows, width), LOW),
            ((rows, pb * slab), LOW),
            ((rows, width), LOW),
            ((rows, pb * slab), LOW),
            ((rows, width), FULL),
            ((rows, width), FULL),
        ],
        [target_length, task_group, mix2, x1, cross_out, gains, expand, contract, cot],
        scalars=2,
    )
    grad_h3 = sum_ctx(grad_h3, core)
    block_output = (x2 + sum_ctx(part_out, core).astype(FULL)).astype(LOW)

    block = jnp.arange(pb) * (ctx * share) + mine_ctx * share
    chosen = (block[:, None] + jnp.arange(share)[None, :]).reshape(-1)
    choose = (jnp.arange(width)[:, None] == chosen[None, :]).astype(LOW)

    def owned(left, right):
        columns = dot(left, choose).astype(LOW)
        return to_owners(outer_sum(columns, right).reshape(pb, share, right.shape[1]))

    grad_contract = to_owners(outer_sum(active, low_out).reshape(pb, slab, width))
    every_hidden = from_all(grad_hidden, "ctx")
    columns = dot(h3, choose).astype(LOW)
    partial = jnp.einsum("nf,cnh->fch", columns, every_hidden, preferred_element_type=FULL)
    summed = to_owners(partial.reshape(pb, share, ctx * pb * slab))
    grad_expand = summed.reshape(share, ctx, pb, slab).transpose(0, 2, 1, 3)
    grad_expand = grad_expand.reshape(share, hidden)

    dx2, low_cross, grad_cq, grad_memory, gain_c = call(
        cross_back_kernel,
        [
            ((rows, width), FULL),
            ((rows, width), LOW),
            ((rows, width), FULL),
            ((passage, 2 * width), LOW),
            ((1, width), FULL),
        ],
        [
            target_length,
            task_group,
            grad_h3,
            x2,
            gains,
            cot,
            cross_out,
            cq,
            memory,
            passage_mask,
            stats,
            mix2,
        ],
        scalars=2,
    )
    grad_cq = sum_ctx(grad_cq, core)
    grad_cross_output = owned(mix2, low_cross)
    grad_encoder = dot_t(grad_memory, memory_in).astype(LOW)[None]
    partial = outer_sum(e, grad_memory).reshape(pb, ctx // 2, 2, share, 2 * width)
    kept = lax.dynamic_index_in_dim(partial, core, 2, False)
    sent = lax.dynamic_index_in_dim(partial, 1 - core, 2, False).astype(LOW)
    partial = (kept + swap_ctx(sent, 1).astype(FULL)).astype(LOW).transpose(1, 0, 2, 3)
    partial = jnp.sum(exchange(partial, "ctx", core_groups()).astype(FULL), axis=0)
    grad_cross_memory = to_owners(partial)

    low_self, grad_p1, grad_x, gain_ab, diagonal = call(
        self_back_kernel,
        [
            ((rows, width), LOW),
            ((rows, 3 * width), LOW),
            ((rows, width), LOW),
            ((2, width), FULL),
            ((heads, rows), FULL),
        ],
        [grad_cq, cross_in, x1, gains, dx2, self_out, p1, probs, x, proj],
    )
    grad_cross_query = owned(h2, grad_cq)
    grad_self_output = owned(mix1, low_self)
    grad_self_projection = owned(h1, grad_p1)
    gain_grads = jnp.concatenate([gain_ab, gain_c]).reshape(-1, pb, ctx, share)
    gain_grads = lax.dynamic_index_in_dim(gain_grads, mine_ctx, 2, False).transpose(1, 0, 2)
    grad_table = lax.dot_general(
        diagonal,
        hot.astype(FULL),
        (((1,), (1,)), ((), ())),
        precision=lax.Precision.HIGHEST,
        preferred_element_type=FULL,
    )
    small = jnp.concatenate(
        [
            jnp.pad(gain_grads, ((0, 0), (0, 0), (0, 128 - share))),
            jnp.broadcast_to(
                jnp.pad(grad_table, ((0, 0), (0, 128 - buckets)))[None], (pb, heads, 128)
            ),
        ],
        axis=1,
    )
    small = jnp.sum(exchange(small, "pb"), axis=0)
    grad_norm_gains = small[: gain_grads.shape[1], :share]
    grad_table = small[gain_grads.shape[1] :, :buckets].T
    return (
        block_output[None],
        grad_x[None],
        grad_encoder,
        grad_self_projection,
        grad_self_output,
        grad_cross_query,
        grad_cross_memory,
        grad_cross_output,
        grad_expand,
        grad_contract,
        grad_norm_gains,
        grad_table,
    )


def solution(mesh):
    both = ("pb", "ctx")
    return jax.shard_map(
        body,
        mesh=mesh,
        in_specs=(
            P("pb", None, None),
            P("pb", "ctx", None),
            P(both, None),
            P(both, None),
            P(both, None),
            P(both, None),
            P(both, None),
            P(both, None),
            P(both, None),
            P(None, both),
            P(),
            P(),
            P("pb", "ctx"),
            P("pb"),
            P("pb"),
            P("pb", None, None),
        ),
        out_specs=(
            P("pb", None, None),
            P("pb", None, None),
            P("pb", "ctx", None),
            P(both, None),
            P(both, None),
            P(both, None),
            P(both, None),
            P(both, None),
            P(both, None),
            P(both, None),
            P(None, both),
            P(),
        ),
        check_vma=False,
    )
```

```python
import functools

import jax
import jax.numpy as jnp
from jax import lax
from jax.experimental import pallas as pl
from jax.experimental.pallas import tpu as pltpu
from jax.sharding import PartitionSpec as P

LOW, FULL = jnp.bfloat16, jnp.float32
MASKED = -1000000000.0
EPS = 1e-06
HEAD = 64
VMEM_BYTES = 56 * 1024 * 1024


def dot(left, right, left_axis=1, right_axis=0):
    return lax.dot_general(
        left,
        right,
        (((left_axis,), (right_axis,)), ((), ())),
        preferred_element_type=FULL,
    )


def dot_t(left, right):
    return dot(left, right, 1, 1)


def outer_sum(left, right):
    return dot(left, right, 0, 0)


def rms_unit(values):
    factor = lax.rsqrt(jnp.mean(values * values, axis=-1, keepdims=True) + EPS)
    return values * factor, factor


def norm_back(grad, unit, factor, gain):
    scaled = grad * gain
    return factor * (scaled - unit * jnp.mean(scaled * unit, axis=-1, keepdims=True))


def call(kernel, outs, args, scalars=0, scratch=()):
    spaces = [pltpu.SMEM] * scalars + [pltpu.VMEM] * (len(args) - scalars)
    return pl.pallas_call(
        kernel,
        out_shape=[jax.ShapeDtypeStruct(shape, dtype) for shape, dtype in outs],
        in_specs=[pl.BlockSpec(memory_space=space) for space in spaces],
        out_specs=[pl.BlockSpec(memory_space=pltpu.VMEM) for _ in outs],
        scratch_shapes=list(scratch),
        compiler_params=pltpu.CompilerParams(vmem_limit_bytes=VMEM_BYTES),
    )(*args)


def to_low(values):
    return values.astype(jnp.bfloat16)


def normalize(values, scale):
    factor = lax.rsqrt(jnp.mean(values * values, axis=-1, keepdims=True) + 1e-06)
    return (values * factor * scale, values * factor, factor)


def gelu_tanh(values):
    return jax.nn.gelu(values, approximate=True)


def fetch(shards):
    return (
        lax.all_gather(shards[0], ("pb", "ctx"), axis=0, tiled=True),
        lax.all_gather(shards[1], ("pb", "ctx"), axis=0, tiled=True),
        lax.all_gather(shards[2], ("pb", "ctx"), axis=0, tiled=True),
        lax.all_gather(shards[3], ("pb", "ctx"), axis=0, tiled=True),
        lax.all_gather(shards[4], ("pb", "ctx"), axis=0, tiled=True),
        lax.all_gather(shards[5], ("pb", "ctx"), axis=0, tiled=True),
        lax.all_gather(shards[6], ("pb", "ctx"), axis=0, tiled=True),
        lax.all_gather(shards[7], ("pb", "ctx"), axis=1, tiled=True),
    )


def run_forward(params, decoder, encoder, allowed, visible, rel_bias):
    projection, self_out, cross_in, memory_in, cross_out, expand, contract, gains = params
    scale_gain = gains.astype(jnp.float32)
    count, length, width = decoder.shape
    heads = rel_bias.shape[0]
    head_dim = width // heads
    inverse = head_dim ** (-0.5)
    residual = decoder.astype(jnp.float32).reshape(count * length, width)
    normed_a, unit_a, factor_a = normalize(residual, scale_gain[0])
    normed_a = to_low(normed_a)
    joined = to_low(dot(normed_a, projection)).reshape(count, length, 3, heads, head_dim)
    query_rows, key_rows, value_rows = (joined[:, :, 0], joined[:, :, 1], joined[:, :, 2])
    self_scores = (
        jnp.einsum("nihd,njhd->nhij", query_rows, key_rows, preferred_element_type=jnp.float32)
        * inverse
        + rel_bias[None]
    )
    self_probs = jax.nn.softmax(jnp.where(allowed, self_scores, -1000000000.0), axis=-1)
    self_mixed = jnp.einsum(
        "nhij,njhd->nihd", to_low(self_probs), value_rows, preferred_element_type=jnp.float32
    )
    self_mix = to_low(self_mixed.reshape(count * length, width))
    after_self = residual + dot(self_mix, self_out)
    normed_b, unit_b, factor_b = normalize(after_self, scale_gain[1])
    normed_b = to_low(normed_b)
    cross_rows = to_low(dot(normed_b, cross_in)).reshape(count, length, heads, head_dim)
    ctx_rows = encoder.shape[1]
    memory = to_low(dot(encoder.reshape(count * ctx_rows, width), memory_in)).reshape(
        count, ctx_rows, 2, heads, head_dim
    )
    cross_keys, cross_vals = (memory[:, :, 0], memory[:, :, 1])
    cross_scores = (
        jnp.einsum("nihd,njhd->nhij", cross_rows, cross_keys, preferred_element_type=jnp.float32)
        * inverse
    )
    masked = jnp.where(visible, cross_scores, -1000000000.0)
    highest_score = lax.pmax(jnp.max(masked, axis=-1), "ctx")
    total = lax.psum(
        jnp.sum(jnp.where(visible, jnp.exp(masked - highest_score[..., None]), 0.0), axis=-1), "ctx"
    )
    cross_probs = (
        jnp.where(visible, jnp.exp(masked - highest_score[..., None]), 0.0) / total[..., None]
    )
    partial_mix = jnp.einsum(
        "nhij,njhd->nihd", to_low(cross_probs), cross_vals, preferred_element_type=jnp.float32
    )
    cross_mixed = lax.psum(partial_mix, "ctx")
    cross_mix = to_low(cross_mixed.reshape(count * length, width))
    after_cross = after_self + dot(cross_mix, cross_out)
    normed_c, unit_c, factor_c = normalize(after_cross, scale_gain[2])
    normed_c = to_low(normed_c)
    hidden = dot(normed_c, expand)
    active = to_low(gelu_tanh(hidden))
    output = after_cross + dot(active, contract)
    saved = (
        normed_a,
        unit_a,
        factor_a,
        query_rows,
        key_rows,
        value_rows,
        self_probs,
        self_mix,
        normed_b,
        unit_b,
        factor_b,
        cross_rows,
        cross_keys,
        cross_vals,
        cross_probs,
        cross_mix,
        normed_c,
        unit_c,
        factor_c,
        hidden,
        active,
        scale_gain,
    )
    return (output, saved)


def plain_body(
    decoder_in,
    encoder_out,
    self_projection,
    self_output,
    cross_query,
    cross_memory,
    cross_output,
    expand_weight,
    contract_weight,
    norm_gains,
    bias_table,
    bucket_index,
    passage_mask,
    target_length,
    task_group,
    cotangent,
):
    shards = (
        self_projection,
        self_output,
        cross_query,
        cross_memory,
        cross_output,
        expand_weight,
        contract_weight,
        norm_gains,
    )
    count, length, width = decoder_in.shape
    ctx_rows = encoder_out.shape[1]
    buckets, heads = bias_table.shape
    head_dim = width // heads
    inverse = head_dim ** (-0.5)
    positions = jnp.arange(length)
    offsets = jnp.clip(positions[:, None] - positions[None, :], 0, length - 1)
    pair_bucket = jnp.take(bucket_index, offsets.reshape(-1))
    one_hot = (pair_bucket[:, None] == jnp.arange(buckets)[None, :]).astype(jnp.bfloat16)
    rel_bias = dot(one_hot, bias_table).T.reshape(heads, length, length)
    causal = positions[None, :] <= positions[:, None]
    allowed = (causal[None] & (positions[None, None, :] < target_length[:, None, None]))[:, None]
    visible = (passage_mask > 0)[:, None, None, :]
    params = fetch(shards)
    output, saved = run_forward(params, decoder_in, encoder_out, allowed, visible, rel_bias)
    projection, self_out, cross_in, memory_in, cross_out, expand, contract, gains = params
    (
        normed_a,
        unit_a,
        factor_a,
        query_rows,
        key_rows,
        value_rows,
        self_probs,
        self_mix,
        normed_b,
        unit_b,
        factor_b,
        cross_rows,
        cross_keys,
        cross_vals,
        cross_probs,
        cross_mix,
        normed_c,
        unit_c,
        factor_c,
        hidden,
        active,
        scale_gain,
    ) = saved
    rows_total = count * length
    share = rows_total // lax.axis_size("ctx")
    start = lax.axis_index("ctx") * share

    def sliced(values):
        return lax.dynamic_slice_in_dim(values, start, share, 0)

    task_scale = jnp.where(task_group == 0, 1.0, jnp.where(task_group == 1, 0.5, 2.0)).astype(
        jnp.float32
    )
    row_live = (positions[None, :] < target_length[:, None]).astype(jnp.float32)
    grad_out = (
        cotangent.astype(jnp.float32) * (task_scale[:, None] * row_live)[:, :, None]
    ).reshape(rows_total, width)
    low_out = to_low(grad_out)
    grad_active = dot_t(low_out, contract)
    unused_value, gelu_pull = jax.vjp(gelu_tanh, hidden)
    grad_hidden = to_low(gelu_pull(grad_active)[0])
    grad_normed_c = dot_t(grad_hidden, expand)
    gain_c = jnp.sum(sliced(grad_normed_c * unit_c), axis=0)
    grad_after_cross = grad_out + norm_back(grad_normed_c, unit_c, factor_c, scale_gain[2])
    low_cross = to_low(grad_after_cross)
    grad_mix = to_low(dot_t(low_cross, cross_out)).reshape(count, length, heads, head_dim)
    grad_probs = jnp.einsum(
        "nihd,njhd->nhij", grad_mix, cross_vals, preferred_element_type=jnp.float32
    )
    row_dot = lax.psum(jnp.sum(grad_probs * cross_probs, axis=-1), "ctx")
    grad_scores = to_low(cross_probs * (grad_probs - row_dot[..., None]))
    partial_query = (
        jnp.einsum("nhij,njhd->nihd", grad_scores, cross_keys, preferred_element_type=jnp.float32)
        * inverse
    )
    grad_query = to_low(lax.psum(partial_query, "ctx")).reshape(rows_total, width)
    grad_key = (
        jnp.einsum("nhij,nihd->njhd", grad_scores, cross_rows, preferred_element_type=jnp.float32)
        * inverse
    )
    grad_value = jnp.einsum(
        "nhij,nihd->njhd", to_low(cross_probs), grad_mix, preferred_element_type=jnp.float32
    )
    grad_memory = to_low(jnp.stack([grad_key, grad_value], axis=2)).reshape(
        count * ctx_rows, 2 * width
    )
    encoder_rows = encoder_out.reshape(count * ctx_rows, width)
    grad_cross_memory = outer_sum(encoder_rows, grad_memory)
    grad_encoder = to_low(dot_t(grad_memory, memory_in)).reshape(count, ctx_rows, width)
    grad_normed_b = dot_t(grad_query, cross_in)
    gain_b = jnp.sum(sliced(grad_normed_b * unit_b), axis=0)
    grad_after_self = grad_after_cross + norm_back(grad_normed_b, unit_b, factor_b, scale_gain[1])
    low_self = to_low(grad_after_self)
    grad_self_mix = to_low(dot_t(low_self, self_out)).reshape(count, length, heads, head_dim)
    grad_probs_self = jnp.einsum(
        "nihd,njhd->nhij", grad_self_mix, value_rows, preferred_element_type=jnp.float32
    )
    self_dot = jnp.sum(grad_probs_self * self_probs, axis=-1, keepdims=True)
    grad_scores_self = to_low(self_probs * (grad_probs_self - self_dot))
    pair_grad = jnp.sum(grad_scores_self.astype(jnp.float32), axis=0).reshape(
        heads, length * length
    )
    pair_count = length * length // lax.axis_size("ctx")
    pair_start = lax.axis_index("ctx") * pair_count
    pair_slice = lax.dynamic_slice_in_dim(pair_grad, pair_start, pair_count, 1)
    hot_slice = lax.dynamic_slice_in_dim(one_hot.astype(jnp.float32), pair_start, pair_count, 0)
    table_term = lax.dot_general(
        hot_slice,
        pair_slice,
        (((0,), (1,)), ((), ())),
        precision=lax.Precision.HIGHEST,
        preferred_element_type=jnp.float32,
    )
    grad_table = lax.psum(table_term, ("pb", "ctx"))
    grad_q = (
        jnp.einsum(
            "nhij,njhd->nihd", grad_scores_self, key_rows, preferred_element_type=jnp.float32
        )
        * inverse
    )
    grad_k = (
        jnp.einsum(
            "nhij,nihd->njhd", grad_scores_self, query_rows, preferred_element_type=jnp.float32
        )
        * inverse
    )
    grad_v = jnp.einsum(
        "nhij,nihd->njhd", to_low(self_probs), grad_self_mix, preferred_element_type=jnp.float32
    )
    grad_joined = to_low(jnp.stack([grad_q, grad_k, grad_v], axis=2)).reshape(rows_total, 3 * width)
    grad_normed_a = dot_t(grad_joined, projection)
    gain_a = jnp.sum(sliced(grad_normed_a * unit_a), axis=0)
    grad_decoder = to_low(
        grad_after_self + norm_back(grad_normed_a, unit_a, factor_a, scale_gain[0])
    ).reshape(count, length, width)
    gain_grads = jnp.stack([gain_a, gain_b, gain_c])
    pairs = (
        (normed_a, grad_joined),
        (self_mix, low_self),
        (normed_b, grad_query),
        (cross_mix, low_cross),
        (normed_c, grad_hidden),
        (active, low_out),
    )
    partials = tuple((outer_sum(sliced(left), sliced(right)) for left, right in pairs))
    summed = (
        lax.psum_scatter(partials[0], ("pb", "ctx"), scatter_dimension=0, tiled=True),
        lax.psum_scatter(partials[1], ("pb", "ctx"), scatter_dimension=0, tiled=True),
        lax.psum_scatter(partials[2], ("pb", "ctx"), scatter_dimension=0, tiled=True),
        lax.psum_scatter(grad_cross_memory, ("pb", "ctx"), scatter_dimension=0, tiled=True),
        lax.psum_scatter(partials[3], ("pb", "ctx"), scatter_dimension=0, tiled=True),
        lax.psum_scatter(partials[4], ("pb", "ctx"), scatter_dimension=0, tiled=True),
        lax.psum_scatter(partials[5], ("pb", "ctx"), scatter_dimension=0, tiled=True),
        lax.psum_scatter(gain_grads, ("pb", "ctx"), scatter_dimension=1, tiled=True),
    )
    block_output = to_low(output).reshape(count, length, width)
    return (
        block_output,
        grad_decoder,
        grad_encoder,
        summed[0],
        summed[1],
        summed[2],
        summed[3],
        summed[4],
        summed[5],
        summed[6],
        summed[7],
        grad_table,
    )


def swap_ctx(values, mask):
    size = lax.axis_size("ctx")
    return lax.ppermute(values, "ctx", [(i, i ^ mask) for i in range(size)])


def swap_pb(values, mask):
    size = lax.axis_size("pb")
    return lax.ppermute(values, "pb", [(i, i ^ mask) for i in range(size)])


def exchange(values, axis):
    return lax.all_to_all(values, axis, 0, 0, tiled=True)


def from_all(values, axis):
    size = lax.axis_size(axis)
    return exchange(jnp.broadcast_to(values[None], (size,) + values.shape), axis)


def all_chips(values):
    return [values] + [swap_ctx(values, mask) for mask in range(2, lax.axis_size("ctx"), 2)]


def tree(terms):
    while len(terms) > 1:
        terms = [a + b for a, b in zip(terms[0::2], terms[1::2])]
    return terms[0]


def sum_chips(values):
    return tree([part.astype(FULL) for part in all_chips(values)]).astype(LOW)


def to_owners(parts):
    return [parts[0]] + [swap_pb(part, r) for r, part in enumerate(parts) if r]


def pick(low, high):
    lanes = lax.broadcasted_iota(jnp.int32, low.shape, 1)
    return jnp.where(lanes < low.shape[1] // 2, low, high)


def lane_mask(values, side):
    zeros = jnp.zeros_like(values)
    return pick(values, zeros) if side == 0 else pick(zeros, values)


def join(first, mine, other, axis=1):
    return jnp.where(
        first,
        jnp.concatenate([mine, other], axis=axis),
        jnp.concatenate([other, mine], axis=axis),
    )


def half_of(first, values, axis=1):
    middle = values.shape[axis] // 2
    if axis == 0:
        return jnp.where(first, values[:middle], values[middle:])
    return jnp.where(first, values[:, :middle], values[:, middle:])


CORE, CHIP, PB, CTX = range(4)


def place_kernel(sources, widths, rows, ctx, here, *refs):
    ins, outs = refs[: 2 * len(sources)], refs[2 * len(sources) :]
    first = here[CORE] == 0
    for i, (begin, flip) in enumerate(sources):
        mine, other = ins[2 * i], ins[2 * i + 1]
        chip = here[CHIP] ^ flip
        for z in range(mine.shape[0]):
            both = join(first, mine[z], other[z], 0)
            slot = pl.multiple_of(((begin + z) * (ctx // 2) + chip) * 2 * rows, 16)
            at = 0
            for out, width in zip(outs, widths):
                out[pl.ds(slot, 2 * rows), :] = both[:, at : at + width]
                at += width


def gather_rows(here, shards):
    pb, ctx = lax.axis_size("pb"), lax.axis_size("ctx")
    rows = shards[0].shape[0]
    widths = [s.shape[1] for s in shards]
    own = from_all(jnp.concatenate(shards, axis=1), "pb")
    along_x, along_y = swap_ctx(own, 2), swap_ctx(own, 4)
    low = swap_ctx(along_x[: pb // 2], 4)
    high = swap_ctx(along_y[pb // 2 :], 2)
    arrays = [own, along_x, along_y, low, high]
    sources = [(0, 0), (0, 1), (0, 2), (0, 3), (pb // 2, 3)]
    args = []
    for array in arrays:
        args += [array, swap_ctx(array, 1)]
    return call(
        functools.partial(place_kernel, sources, widths, rows, ctx),
        [((pb * ctx * rows, width), LOW) for width in widths],
        [here] + args,
        scalars=1,
    ), own


def self_kernel(
    here, length, x, proj, self_out, cross_in, gains, table, p1, probs, mix, x1, h1, h2, cq
):
    rows, width = x.shape
    heads = width // HEAD
    pair = 2 * HEAD
    inverse = HEAD ** (-0.5)
    xf = x[...].astype(FULL)
    unit, _ = rms_unit(xf)
    normed = (unit * gains[0:1, :]).astype(LOW)
    h1[...] = normed
    joined = dot(normed, proj[...]).astype(LOW)
    p1[...] = joined
    row = lax.broadcasted_iota(jnp.int32, (rows, rows), 0)
    col = lax.broadcasted_iota(jnp.int32, (rows, rows), 1)
    allowed = (col <= row) & (col < length[0])
    mixes = []
    for g in range(heads // 2):
        at = g * pair
        q = joined[:, at : at + pair]
        k = joined[:, width + at : width + at + pair]
        v = joined[:, 2 * width + at : 2 * width + at + pair]
        mixed = []
        for side in range(2):
            head = 2 * g + side
            bias = pltpu.roll(
                jnp.broadcast_to(table[head : head + 1, :], (rows, rows)),
                1,
                axis=1,
                stride=1,
                stride_axis=0,
            )
            scores = jnp.where(allowed, dot_t(lane_mask(q, side), k) * inverse + bias, MASKED)
            powers = jnp.exp(scores - jnp.max(scores, axis=-1, keepdims=True))
            prob = powers / jnp.sum(powers, axis=-1, keepdims=True)
            probs[head] = prob
            mixed.append(dot(prob.astype(LOW), v))
        mixes.append(pick(*mixed).astype(LOW))
    mixes = jnp.concatenate(mixes, axis=1)
    mix[...] = mixes
    after = xf + dot(mixes, self_out[...])
    x1[...] = after
    unit, _ = rms_unit(after)
    normed = (unit * gains[1:2, :]).astype(LOW)
    h2[...] = normed
    cq[...] = dot(normed, half_of(here[CORE] == 0, cross_in[...])).astype(LOW)


def memory_kernel(here, mine, other, memory_in, memory):
    first = here[CORE] == 0
    width = mine.shape[1]
    keys = half_of(first, memory_in[:, :width])
    values = half_of(first, memory_in[:, width:])
    weight = jnp.concatenate([keys, values], axis=1)
    rows = mine.shape[0]
    memory[:rows] = dot(mine[...], weight).astype(LOW)
    memory[rows:] = dot(other[...], weight).astype(LOW)


def pack_stats(tops, totals):
    rows = tops[0].shape[0]
    lanes = lax.broadcasted_iota(jnp.int32, (rows, 128), 1)
    columns = jnp.zeros((rows, 128), FULL)
    for index, column in enumerate(tops + totals):
        columns = jnp.where(lanes // 3 == index, column, columns)
    high = columns.astype(LOW).astype(FULL)
    middle = (columns - high).astype(LOW).astype(FULL)
    kind = lanes % 3
    return jnp.where(kind == 0, high, jnp.where(kind == 1, middle, columns - high - middle)).astype(
        LOW
    )


def read_stats(packed, heads):
    values = packed.astype(FULL)
    columns = [
        values[:, i : i + 1] + values[:, i + 1 : i + 2] + values[:, i + 2 : i + 3]
        for i in range(0, 6 * heads, 3)
    ]
    return columns[:heads], columns[heads:]


def cross_kernel(cq, memory, visible, packed):
    half = cq.shape[1]
    pair = 2 * HEAD
    inverse = HEAD ** (-0.5)
    seen = visible[...] > 0
    tops, totals, mixes = [], [], []
    for at in range(0, half, pair):
        q = cq[:, at : at + pair]
        k = memory[:, at : at + pair]
        v = memory[:, half + at : half + at + pair]
        mixed = []
        for side in range(2):
            scores = jnp.where(seen, dot_t(lane_mask(q, side), k) * inverse, MASKED)
            top = jnp.max(scores, axis=-1, keepdims=True)
            powers = jnp.where(seen, jnp.exp(scores - top), 0.0)
            tops.append(top)
            totals.append(jnp.sum(powers, axis=-1, keepdims=True))
            mixed.append(dot(powers.astype(LOW), v))
        mixes.append(pick(*mixed).astype(LOW))
    packed[...] = jnp.concatenate(mixes + [pack_stats(tops, totals)], axis=1)


def spread(columns):
    shape = (columns[0].shape[0], 2 * HEAD)
    return jnp.concatenate(
        [
            pick(jnp.broadcast_to(a, shape), jnp.broadcast_to(b, shape))
            for a, b in zip(columns[0::2], columns[1::2])
        ],
        axis=1,
    )


def merge_kernel(here, *refs):
    ins, mix, stats = refs[:-2], refs[-2], refs[-1]
    half = mix.shape[1]
    heads = half // HEAD
    packed = [ref[...] for ref in ins]
    step = 1
    while step < len(packed):
        flip = (here[CHIP] & step) != 0
        packed = [jnp.where(flip, packed[i ^ step], packed[i]) for i in range(len(packed))]
        step *= 2
    read = [read_stats(p[:, half:], heads) for p in packed]
    tops, totals, scales = [], [], []
    for h in range(heads):
        top = read[0][0][h]
        for other in read[1:]:
            top = jnp.maximum(top, other[0][h])
        scale = [jnp.exp(r[0][h] - top) for r in read]
        total = tree([r[1][h] * w for r, w in zip(read, scale)])
        tops.append(top)
        totals.append(total)
        scales.append([w / total for w in scale])
    terms = [
        p[:, :half].astype(FULL) * spread([scale[i] for scale in scales])
        for i, p in enumerate(packed)
    ]
    mix[...] = tree(terms).astype(LOW)
    stats[...] = pack_stats(tops, totals)


def gelu_parts(values):
    slope = (2.0 / jnp.pi) ** 0.5
    square = values * values
    bent = jnp.tanh(slope * (values + 0.044715 * values * square))
    active = 0.5 * values * (1.0 + bent)
    inner = slope * (1.0 + 3 * 0.044715 * square)
    return active, 0.5 * (1.0 + bent) + 0.5 * values * (1.0 - bent * bent) * inner


def task_rows(length, task, cot):
    rows = lax.broadcasted_iota(jnp.int32, cot.shape, 0)
    weight = jnp.where(task[0] == 0, 1.0, jnp.where(task[0] == 1, 0.5, 2.0)).astype(FULL)
    return jnp.where(rows < length[0], cot[...].astype(FULL) * weight, 0.0)


def feed_weights(packed, width):
    pb = packed.shape[0]
    side = (packed.shape[2] - width) // 2
    expand = []
    for z in range(pb):
        expand += [packed[z, :, width : width + side], packed[z, :, width + side :]]
    contract = [packed[z, :, :width] for z in range(pb)]
    return jnp.concatenate(expand, axis=0), jnp.concatenate(contract, axis=0)


def feed_kernel(
    here,
    length,
    task,
    mix_mine,
    mix_other,
    x1,
    cross_out,
    gains,
    feed_mine,
    feed_other,
    cot,
    x2,
    h3,
    active,
    low_out,
    grad_hidden,
    partial,
):
    first = here[CORE] == 0
    width = x1.shape[1]
    after = x1[...] + dot(join(first, mix_mine[...], mix_other[...]), cross_out[...])
    x2[...] = after
    unit, _ = rms_unit(after)
    normed = (unit * gains[2:3, :]).astype(LOW)
    h3[...] = normed
    low = task_rows(length, task, cot).astype(LOW)
    low_out[...] = low
    mine, other = feed_weights(feed_mine, width), feed_weights(feed_other, width)
    expand = jnp.concatenate([mine[0], other[0]], axis=1)
    contract = jnp.concatenate([mine[1], other[1]], axis=0)
    value, slope = gelu_parts(dot(normed, expand))
    value = value.astype(LOW)
    grad = (dot_t(low, contract) * slope).astype(LOW)
    units = active.shape[1]
    active[...] = value[:, :units]
    grad_hidden[...] = grad[:, :units]
    partial[:, : width // 2] = dot_t(grad, half_of(first, expand, 0)).astype(LOW)
    partial[:, width // 2 :] = dot(value, half_of(first, contract)).astype(LOW)


def feed_grad_kernel(here, active, low_out, h3, grad_hidden, *refs):
    outs, contract, expand = refs[:-2], refs[-2], refs[-1]
    contract[...] = outer_sum(active[...], low_out[...])
    expand[...] = outer_sum(h3[...], grad_hidden[...])
    slab = contract.shape[0] // len(outs)
    block = expand.shape[0] // len(outs)
    for r, out in enumerate(outs):
        z = here[PB] ^ r
        out[:slab] = contract[pl.ds(pl.multiple_of(z * slab, 16), slab)].astype(LOW)
        at = pl.multiple_of(z * block, 16)
        low = expand[pl.ds(at, block // 2)]
        high = expand[pl.ds(at + block // 2, block // 2)]
        out[slab:] = jnp.concatenate([low, high], axis=1).astype(LOW)


def cross_back_kernel(
    here,
    length,
    task,
    sums_mine,
    sums_other,
    x2,
    gains,
    cot,
    cross_out,
    cq,
    memory,
    visible,
    stats,
    mix,
    dx2,
    low_cross,
    grad_cq,
    grad_memory,
    gain_grad,
    output,
):
    first = here[CORE] == 0
    half = mix.shape[1]
    heads = half // HEAD
    pair = 2 * HEAD
    inverse = HEAD ** (-0.5)
    after = x2[...]
    unit, factor = rms_unit(after)
    sums = [join(first, sums_mine[:, a : a + half], sums_other[:, a : a + half]) for a in (0, half)]
    grad = sums[0].astype(FULL)
    output[...] = (after + sums[1].astype(FULL)).astype(LOW)
    gain_grad[...] = jnp.sum(grad * unit, axis=0, keepdims=True)
    back = task_rows(length, task, cot) + norm_back(grad, unit, factor, gains[2:3, :])
    dx2[...] = back
    low = back.astype(LOW)
    low_cross[...] = low
    grad_mix = dot_t(low, half_of(first, cross_out[...], 0)).astype(LOW)
    seen = visible[...] > 0
    tops, totals = read_stats(stats[...], heads)
    for g in range(heads // 2):
        at = g * pair
        q = cq[:, at : at + pair]
        k = memory[:, at : at + pair]
        v = memory[:, half + at : half + at + pair]
        do = grad_mix[:, at : at + pair]
        weighed = do.astype(FULL) * mix[:, at : at + pair].astype(FULL)
        queries, keys, values = [], [], []
        for side in range(2):
            head = 2 * g + side
            qs, ds = lane_mask(q, side), lane_mask(do, side)
            scores = jnp.where(seen, dot_t(qs, k) * inverse, MASKED)
            prob = jnp.where(seen, jnp.exp(scores - tops[head]) * (1.0 / totals[head]), 0.0)
            rho = jnp.sum(lane_mask(weighed, side), axis=-1, keepdims=True)
            grad_scores = (prob * (dot_t(ds, v) - rho)).astype(LOW)
            queries.append(dot(grad_scores, k))
            keys.append(outer_sum(grad_scores, qs))
            values.append(outer_sum(prob.astype(LOW), ds))
        grad_cq[:, at : at + pair] = (pick(*queries) * inverse).astype(LOW)
        grad_memory[:, at : at + pair] = ((keys[0] + keys[1]) * inverse).astype(LOW)
        grad_memory[:, half + at : half + at + pair] = (values[0] + values[1]).astype(LOW)


def memory_grad_kernel(here, mine, other, grad_memory, *refs):
    outs, whole = refs[:-1], refs[-1]
    rows = mine.shape[0]
    whole[...] = outer_sum(mine[...], grad_memory[:rows]) + outer_sum(other[...], grad_memory[rows:])
    share = outs[0].shape[1]
    for r, out in enumerate(outs):
        chip = here[CHIP] ^ r
        for z in range(out.shape[0]):
            at = pl.multiple_of((z * len(outs) + chip) * share, 16)
            out[z] = whole[pl.ds(at, share)].astype(LOW)


def encoder_grad_kernel(here, mine, other, memory_in, grad):
    first = here[CORE] == 0
    half = mine.shape[1] // 2
    keys = join(first, mine[:, :half], other[:, :half])
    values = join(first, mine[:, half:], other[:, half:])
    grad[...] = dot_t(jnp.concatenate([keys, values], axis=1), memory_in[...]).astype(LOW)


def owned(left, choose):
    return dot(left, choose).astype(LOW)


def cross_grad_kernel(
    count, here, mix_mine, mix_other, low_cross, h2, cq_mine, cq_other, choose, *refs
):
    pieces, outs, first_sum, second_sum = refs[:count], refs[count:-2], refs[-2], refs[-1]
    first = here[CORE] == 0
    chosen = choose[...]
    mix = join(first, mix_mine[...], mix_other[...])
    first_sum[...] = outer_sum(owned(mix, chosen), low_cross[...])
    cq = join(first, cq_mine[...], cq_other[...])
    second_sum[...] = outer_sum(owned(h2[...], chosen), cq)
    share = first_sum.shape[0] // len(outs)
    both = pieces[0].shape[1]
    for r, out in enumerate(outs):
        z = here[PB] ^ r
        out[:both] = tree([piece[z].astype(FULL) for piece in pieces]).astype(LOW)
        at = pl.multiple_of(z * share, 8)
        out[both:] = jnp.concatenate(
            [first_sum[pl.ds(at, share)], second_sum[pl.ds(at, share)]], axis=0
        ).astype(LOW)


def self_back_kernel(
    here,
    cq_mine,
    cq_other,
    cross_in,
    x1,
    gains,
    dx2,
    self_out,
    p1,
    probs,
    x,
    proj,
    gain_grad,
    low_self,
    grad_p1,
    grad_x,
    small,
):
    rows, width = x.shape
    heads = width // HEAD
    pair = 2 * HEAD
    inverse = HEAD ** (-0.5)
    grad = dot_t(join(here[CORE] == 0, cq_mine[...], cq_other[...]), cross_in[...])
    unit, factor = rms_unit(x1[...])
    small[...] = jnp.zeros_like(small)
    small[1:2, :] = jnp.sum(grad * unit, axis=0, keepdims=True)
    small[2:3, :] = gain_grad[...]
    dx1 = dx2[...] + norm_back(grad, unit, factor, gains[1:2, :])
    low = dx1.astype(LOW)
    low_self[...] = low
    row = lax.broadcasted_iota(jnp.int32, (rows, rows), 0)
    col = lax.broadcasted_iota(jnp.int32, (rows, rows), 1)
    flip = jnp.where(row + col == rows - 1, 1.0, 0.0).astype(LOW)
    grad_mix = dot_t(low, self_out[...]).astype(LOW)
    parts = [[], [], []]
    for g in range(heads // 2):
        at = g * pair
        q = p1[:, at : at + pair]
        k = p1[:, width + at : width + at + pair]
        v = p1[:, 2 * width + at : 2 * width + at + pair]
        do = grad_mix[:, at : at + pair]
        queries, keys, values = [], [], []
        for side in range(2):
            head = 2 * g + side
            ds = lane_mask(do, side)
            prob = probs[head]
            grad_probs = dot_t(ds, v)
            rho = jnp.sum(prob * grad_probs, axis=-1, keepdims=True)
            grad_scores = (prob * (grad_probs - rho)).astype(LOW)
            turned = pltpu.roll(dot(flip, grad_scores), 0, axis=1, stride=1, stride_axis=0)
            small[3 + head : 4 + head, :rows] = jnp.sum(turned, axis=0, keepdims=True)
            queries.append(dot(grad_scores, k))
            keys.append(outer_sum(grad_scores, lane_mask(q, side)))
            values.append(outer_sum(prob.astype(LOW), ds))
        parts[0].append((pick(*queries) * inverse).astype(LOW))
        parts[1].append(((keys[0] + keys[1]) * inverse).astype(LOW))
        parts[2].append((values[0] + values[1]).astype(LOW))
    joined = jnp.concatenate(parts[0] + parts[1] + parts[2], axis=1)
    grad_p1[...] = joined
    grad = dot_t(joined, proj[...])
    unit, factor = rms_unit(x[...].astype(FULL))
    small[0:1, :] = jnp.sum(grad * unit, axis=0, keepdims=True)
    grad_x[...] = (dx1 + norm_back(grad, unit, factor, gains[0:1, :])).astype(LOW)


def self_grad_kernel(here, mix, low_self, h1, grad_p1, small, choose, *refs):
    outs, sums = refs[:-1], refs[-1]
    chosen = choose[...]
    width = mix.shape[1]
    sums[:, :width] = outer_sum(owned(mix[...], chosen), low_self[...])
    sums[:, width:] = outer_sum(owned(h1[...], chosen), grad_p1[...])
    share = sums.shape[0] // len(outs)
    for r, out in enumerate(outs):
        at = pl.multiple_of((here[PB] ^ r) * share, 8)
        mine = sums[pl.ds(at, share)]
        blocks = [mine[:, a : a + width] for a in range(0, sums.shape[1], width)]
        out[...] = jnp.concatenate(blocks + [small[...]], axis=0).astype(LOW)


def total_of(refs):
    return tree([ref[...].astype(FULL) for ref in refs])


def feed_total_kernel(*refs):
    parts, contract, expand = refs[:-2], refs[-2], refs[-1]
    total = total_of(parts)
    slab = contract.shape[0]
    contract[...] = total[:slab]
    rows = total[slab:].astype(LOW).astype(FULL)
    share, units = expand.shape[1:]
    for c in range(expand.shape[0]):
        side, at = divmod(c * share, rows.shape[0])
        expand[c] = rows[at : at + share, side * units : (side + 1) * units].astype(LOW)


def cross_total_kernel(share, here, *refs):
    parts, mine, other, out_grad, query_grad = refs[:-4], *refs[-4:]
    total = total_of(parts)
    first = here[CORE] == 0
    mine[...] = half_of(first, total[: 2 * share], 0)
    other[...] = half_of(jnp.logical_not(first), total[: 2 * share], 0)
    out_grad[...] = total[2 * share : 3 * share]
    query_grad[...] = total[3 * share :]


def self_total_kernel(here, *refs):
    parts, hot, out_grad, proj_grad, gain_grad, table = refs[:-5], *refs[-5:]
    total = total_of(parts)
    share, width = out_grad.shape
    blocks = [total[a : a + share] for a in range(0, 4 * share, share)]
    out_grad[...] = blocks[0]
    proj_grad[...] = jnp.concatenate(blocks[1:], axis=1)
    small = total[4 * share :]
    gains = gain_grad.shape[0]
    rows = hot.shape[1]
    shape = (width, share)
    mine = lax.broadcasted_iota(jnp.int32, shape, 1) + (here[PB] * here[4] + here[CTX]) * share
    chosen = jnp.where(lax.broadcasted_iota(jnp.int32, shape, 0) == mine, 1.0, 0.0)
    highest = lax.Precision.HIGHEST
    gain_grad[...] = jnp.dot(small, chosen, precision=highest, preferred_element_type=FULL)[:gains]
    heads = table.shape[1]
    whole = lax.dot_general(
        hot[...].astype(FULL),
        small[:, :rows],
        (((1,), (1,)), ((), ())),
        precision=highest,
        preferred_element_type=FULL,
    )
    table[...] = whole[:, gains : gains + heads]


def fast_body(
    decoder_in,
    encoder_out,
    self_projection,
    self_output,
    cross_query,
    cross_memory,
    cross_output,
    expand_weight,
    contract_weight,
    norm_gains,
    bias_table,
    bucket_index,
    passage_mask,
    target_length,
    task_group,
    cotangent,
):
    pb, ctx = lax.axis_size("pb"), lax.axis_size("ctx")
    mine_pb, mine_ctx = lax.axis_index("pb"), lax.axis_index("ctx")
    here = jnp.stack([mine_ctx & 1, mine_ctx >> 1, mine_pb, mine_ctx, jnp.int32(ctx)])
    here = here.astype(jnp.int32)
    rows, width = decoder_in.shape[1:]
    half = width // 2
    passage = encoder_out.shape[1]
    buckets, heads = bias_table.shape
    share = self_projection.shape[0]
    hidden = expand_weight.shape[1]
    slab = contract_weight.shape[0]
    units = pb * slab
    chips = ctx // 2
    x, e, cot = decoder_in[0], encoder_out[0], cotangent[0]

    late = jnp.concatenate([cross_memory, cross_output], axis=1)
    late = lax.all_gather(late, ("pb", "ctx"), axis=0, tiled=True)
    memory_in, cross_out = late[:, : 2 * width], late[:, 2 * width :]
    gain_columns = jnp.pad(norm_gains.T, ((0, 0), (0, 128 - norm_gains.shape[0])))
    (proj, self_out, cross_in, gain_rows), arrived = gather_rows(
        here, [self_projection, self_output, cross_query, gain_columns]
    )
    gains = gain_rows[:, : norm_gains.shape[0]].astype(FULL).T
    e_other = swap_ctx(e, 1)
    visible = jnp.concatenate([passage_mask, swap_ctx(passage_mask, 1)], axis=1)

    expand_weight, _ = lax.optimization_barrier((expand_weight, arrived))
    mixed = expand_weight.reshape(share, pb, ctx, slab).transpose(2, 0, 1, 3)
    mixed = exchange(mixed.reshape(ctx, share, units), "ctx").reshape(2, ctx * share // 2, units)
    feed = from_all(jnp.concatenate([contract_weight, mixed[0], mixed[1]], axis=1), "pb")
    feed_other = swap_ctx(feed, 1)

    hot = (jnp.arange(buckets)[:, None] == bucket_index[::-1][None, :]).astype(LOW)
    table = outer_sum(bias_table, hot)

    p1, probs, mix1, x1, h1, h2, cq = call(
        self_kernel,
        [
            ((rows, 3 * width), LOW),
            ((heads, rows, rows), FULL),
            ((rows, width), LOW),
            ((rows, width), FULL),
            ((rows, width), LOW),
            ((rows, width), LOW),
            ((rows, half), LOW),
        ],
        [here, target_length, x, proj, self_out, cross_in, gains, table],
        scalars=2,
    )
    (memory,) = call(
        memory_kernel, [((2 * passage, width), LOW)], [here, e, e_other, memory_in], scalars=1
    )
    (packed,) = call(cross_kernel, [((rows, half + 128), LOW)], [cq, memory, visible])
    mix2, stats = call(
        merge_kernel,
        [((rows, half), LOW), ((rows, 128), LOW)],
        [here] + all_chips(packed),
        scalars=1,
    )
    mix2_other = swap_ctx(mix2, 1)

    x2, h3, active, low_out, grad_hidden, partial = call(
        feed_kernel,
        [
            ((rows, width), FULL),
            ((rows, width), LOW),
            ((rows, units), LOW),
            ((rows, width), LOW),
            ((rows, units), LOW),
            ((rows, width), LOW),
        ],
        [
            here,
            target_length,
            task_group,
            mix2,
            mix2_other,
            x1,
            cross_out,
            gains,
            feed,
            feed_other,
            cot,
        ],
        scalars=3,
    )
    sums = sum_chips(partial)
    sums_other = swap_ctx(sums, 1)
    feed_grads = call(
        feed_grad_kernel,
        [((2 * slab, width), LOW)] * pb,
        [here, active, low_out, h3, grad_hidden],
        scalars=1,
        scratch=[pltpu.VMEM((units, width), FULL), pltpu.VMEM((width, units), FULL)],
    )
    grad_contract, expand_rows = call(
        feed_total_kernel,
        [((slab, width), FULL), ((ctx, share, units), LOW)],
        to_owners(feed_grads),
    )
    grad_expand = exchange(expand_rows, "ctx").astype(FULL).reshape(ctx, share, pb, slab)
    grad_expand = grad_expand.transpose(1, 2, 0, 3).reshape(share, hidden)

    dx2, low_cross, grad_cq, grad_memory, gain_grad, block_output = call(
        cross_back_kernel,
        [
            ((rows, width), FULL),
            ((rows, width), LOW),
            ((rows, half), LOW),
            ((2 * passage, width), LOW),
            ((1, width), FULL),
            ((rows, width), LOW),
        ],
        [
            here,
            target_length,
            task_group,
            sums,
            sums_other,
            x2,
            gains,
            cot,
            cross_out,
            cq,
            memory,
            visible,
            stats,
            mix2,
        ],
        scalars=3,
    )
    grad_cq = sum_chips(grad_cq)
    cq_other = swap_ctx(grad_cq, 1)
    pieces = call(
        memory_grad_kernel,
        [((pb, 2 * share, width), LOW)] * chips,
        [here, e, e_other, grad_memory],
        scalars=1,
        scratch=[pltpu.VMEM((width, width), FULL)],
    )
    pieces = [pieces[0]] + [swap_ctx(pieces[r], 2 * r) for r in range(1, chips)]
    (grad_encoder,) = call(
        encoder_grad_kernel,
        [((passage, width), LOW)],
        [here, grad_memory[:passage], swap_ctx(grad_memory[passage:], 1), memory_in],
        scalars=1,
    )

    low_self, grad_p1, grad_x, small = call(
        self_back_kernel,
        [
            ((rows, width), LOW),
            ((rows, 3 * width), LOW),
            ((rows, width), LOW),
            ((16, width), FULL),
        ],
        [
            here,
            grad_cq,
            cq_other,
            cross_in,
            x1,
            gains,
            dx2,
            self_out,
            p1,
            probs,
            x,
            proj,
            gain_grad,
        ],
        scalars=1,
    )

    block = jnp.arange(pb) * (ctx * share) + mine_ctx * share
    chosen = (block[:, None] + jnp.arange(share)[None, :]).reshape(-1)
    choose = (jnp.arange(width)[:, None] == chosen[None, :]).astype(LOW)
    cross_grads = call(
        functools.partial(cross_grad_kernel, chips),
        [((4 * share, width), LOW)] * pb,
        [here, mix2, mix2_other, low_cross, h2, grad_cq, cq_other, choose] + pieces,
        scalars=1,
        scratch=[pltpu.VMEM((pb * share, width), FULL)] * 2,
    )
    self_grads = call(
        self_grad_kernel,
        [((4 * share + 16, width), LOW)] * pb,
        [here, mix1, low_self, h1, grad_p1, small, choose],
        scalars=1,
        scratch=[pltpu.VMEM((pb * share, 4 * width), FULL)],
    )
    mine, other, grad_cross_output, grad_cross_query = call(
        functools.partial(cross_total_kernel, share),
        [((share, width), FULL)] * 4,
        [here] + to_owners(cross_grads),
        scalars=1,
    )
    other = swap_ctx(other, 1)
    first = (mine_ctx & 1) == 0
    grad_cross_memory = jnp.concatenate(
        [join(first, mine[:, :half], other[:, :half]), join(first, mine[:, half:], other[:, half:])],
        axis=1,
    )
    grad_self_output, grad_self_projection, grad_norm_gains, grad_table = call(
        self_total_kernel,
        [
            ((share, width), FULL),
            ((share, 3 * width), FULL),
            (norm_gains.shape[:1] + (share,), FULL),
            (bias_table.shape, FULL),
        ],
        [here] + to_owners(self_grads) + [hot],
        scalars=1,
    )
    return (
        block_output[None],
        grad_x[None],
        grad_encoder[None],
        grad_self_projection,
        grad_self_output,
        grad_cross_query,
        grad_cross_memory,
        grad_cross_output,
        grad_expand,
        grad_contract,
        grad_norm_gains,
        grad_table,
    )


def body(*args):
    decoder_in, encoder_out, self_projection = args[:3]
    contract_weight = args[8]
    fits = (
        lax.axis_size("ctx") == 8
        and lax.axis_size("pb") == 4
        and decoder_in.shape[0] == 1
        and decoder_in.shape[1] == 128
        and self_projection.shape[0] % 8 == 0
        and contract_weight.shape[0] * 2 == self_projection.shape[0] * lax.axis_size("ctx")
        and encoder_out.shape[1] % 16 == 0
    )
    return (fast_body if fits else plain_body)(*args)


def solution(mesh):
    return jax.shard_map(
        body,
        mesh=mesh,
        in_specs=(
            P("pb", None, None),
            P("pb", "ctx", None),
            P(("pb", "ctx"), None),
            P(("pb", "ctx"), None),
            P(("pb", "ctx"), None),
            P(("pb", "ctx"), None),
            P(("pb", "ctx"), None),
            P(("pb", "ctx"), None),
            P(("pb", "ctx"), None),
            P(None, ("pb", "ctx")),
            P(),
            P(),
            P("pb", "ctx"),
            P("pb"),
            P("pb"),
            P("pb", None, None),
        ),
        out_specs=(
            P("pb", None, None),
            P("pb", None, None),
            P("pb", "ctx", None),
            P(("pb", "ctx"), None),
            P(("pb", "ctx"), None),
            P(("pb", "ctx"), None),
            P(("pb", "ctx"), None),
            P(("pb", "ctx"), None),
            P(("pb", "ctx"), None),
            P(("pb", "ctx"), None),
            P(None, ("pb", "ctx")),
            P(),
        ),
        check_vma=False,
    )
```

```python
import functools

import jax
import jax.numpy as jnp
from jax import lax
from jax.experimental import pallas as pl
from jax.experimental.pallas import tpu as pltpu
from jax.sharding import PartitionSpec as P

LOW, FULL = jnp.bfloat16, jnp.float32
MASKED = -1000000000.0
EPS = 1e-06
HEAD = 64
VMEM_BYTES = 56 * 1024 * 1024


def dot(left, right, left_axis=1, right_axis=0):
    return lax.dot_general(
        left,
        right,
        (((left_axis,), (right_axis,)), ((), ())),
        preferred_element_type=FULL,
    )


def dot_t(left, right):
    return dot(left, right, 1, 1)


def outer_sum(left, right):
    return dot(left, right, 0, 0)


def rms_unit(values):
    factor = lax.rsqrt(jnp.mean(values * values, axis=-1, keepdims=True) + EPS)
    return values * factor, factor


def norm_back(grad, unit, factor, gain):
    scaled = grad * gain
    return factor * (scaled - unit * jnp.mean(scaled * unit, axis=-1, keepdims=True))


def call(kernel, outs, args, scalars=0, scratch=()):
    arrays, specs, grid = [], [], ()
    for index, arg in enumerate(args):
        if isinstance(arg, tuple):
            arg, shape, place = arg
            specs.append(pl.BlockSpec(shape, lambda i, place=place: place))
            grid = (1,)
        else:
            specs.append(pl.BlockSpec(memory_space=pltpu.SMEM if index < scalars else pltpu.VMEM))
        arrays.append(arg)
    return pl.pallas_call(
        kernel,
        grid=grid,
        out_shape=[jax.ShapeDtypeStruct(shape, dtype) for shape, dtype in outs],
        in_specs=specs,
        out_specs=[pl.BlockSpec(memory_space=pltpu.VMEM) for _ in outs],
        scratch_shapes=list(scratch),
        compiler_params=pltpu.CompilerParams(vmem_limit_bytes=VMEM_BYTES),
    )(*arrays)


def to_low(values):
    return values.astype(jnp.bfloat16)


def normalize(values, scale):
    factor = lax.rsqrt(jnp.mean(values * values, axis=-1, keepdims=True) + 1e-06)
    return (values * factor * scale, values * factor, factor)


def gelu_tanh(values):
    return jax.nn.gelu(values, approximate=True)


def fetch(shards):
    return (
        lax.all_gather(shards[0], ("pb", "ctx"), axis=0, tiled=True),
        lax.all_gather(shards[1], ("pb", "ctx"), axis=0, tiled=True),
        lax.all_gather(shards[2], ("pb", "ctx"), axis=0, tiled=True),
        lax.all_gather(shards[3], ("pb", "ctx"), axis=0, tiled=True),
        lax.all_gather(shards[4], ("pb", "ctx"), axis=0, tiled=True),
        lax.all_gather(shards[5], ("pb", "ctx"), axis=0, tiled=True),
        lax.all_gather(shards[6], ("pb", "ctx"), axis=0, tiled=True),
        lax.all_gather(shards[7], ("pb", "ctx"), axis=1, tiled=True),
    )


def run_forward(params, decoder, encoder, allowed, visible, rel_bias):
    projection, self_out, cross_in, memory_in, cross_out, expand, contract, gains = params
    scale_gain = gains.astype(jnp.float32)
    count, length, width = decoder.shape
    heads = rel_bias.shape[0]
    head_dim = width // heads
    inverse = head_dim ** (-0.5)
    residual = decoder.astype(jnp.float32).reshape(count * length, width)
    normed_a, unit_a, factor_a = normalize(residual, scale_gain[0])
    normed_a = to_low(normed_a)
    joined = to_low(dot(normed_a, projection)).reshape(count, length, 3, heads, head_dim)
    query_rows, key_rows, value_rows = (joined[:, :, 0], joined[:, :, 1], joined[:, :, 2])
    self_scores = (
        jnp.einsum("nihd,njhd->nhij", query_rows, key_rows, preferred_element_type=jnp.float32)
        * inverse
        + rel_bias[None]
    )
    self_probs = jax.nn.softmax(jnp.where(allowed, self_scores, -1000000000.0), axis=-1)
    self_mixed = jnp.einsum(
        "nhij,njhd->nihd", to_low(self_probs), value_rows, preferred_element_type=jnp.float32
    )
    self_mix = to_low(self_mixed.reshape(count * length, width))
    after_self = residual + dot(self_mix, self_out)
    normed_b, unit_b, factor_b = normalize(after_self, scale_gain[1])
    normed_b = to_low(normed_b)
    cross_rows = to_low(dot(normed_b, cross_in)).reshape(count, length, heads, head_dim)
    ctx_rows = encoder.shape[1]
    memory = to_low(dot(encoder.reshape(count * ctx_rows, width), memory_in)).reshape(
        count, ctx_rows, 2, heads, head_dim
    )
    cross_keys, cross_vals = (memory[:, :, 0], memory[:, :, 1])
    cross_scores = (
        jnp.einsum("nihd,njhd->nhij", cross_rows, cross_keys, preferred_element_type=jnp.float32)
        * inverse
    )
    masked = jnp.where(visible, cross_scores, -1000000000.0)
    highest_score = lax.pmax(jnp.max(masked, axis=-1), "ctx")
    total = lax.psum(
        jnp.sum(jnp.where(visible, jnp.exp(masked - highest_score[..., None]), 0.0), axis=-1), "ctx"
    )
    cross_probs = (
        jnp.where(visible, jnp.exp(masked - highest_score[..., None]), 0.0) / total[..., None]
    )
    partial_mix = jnp.einsum(
        "nhij,njhd->nihd", to_low(cross_probs), cross_vals, preferred_element_type=jnp.float32
    )
    cross_mixed = lax.psum(partial_mix, "ctx")
    cross_mix = to_low(cross_mixed.reshape(count * length, width))
    after_cross = after_self + dot(cross_mix, cross_out)
    normed_c, unit_c, factor_c = normalize(after_cross, scale_gain[2])
    normed_c = to_low(normed_c)
    hidden = dot(normed_c, expand)
    active = to_low(gelu_tanh(hidden))
    output = after_cross + dot(active, contract)
    saved = (
        normed_a,
        unit_a,
        factor_a,
        query_rows,
        key_rows,
        value_rows,
        self_probs,
        self_mix,
        normed_b,
        unit_b,
        factor_b,
        cross_rows,
        cross_keys,
        cross_vals,
        cross_probs,
        cross_mix,
        normed_c,
        unit_c,
        factor_c,
        hidden,
        active,
        scale_gain,
    )
    return (output, saved)


def plain_body(
    decoder_in,
    encoder_out,
    self_projection,
    self_output,
    cross_query,
    cross_memory,
    cross_output,
    expand_weight,
    contract_weight,
    norm_gains,
    bias_table,
    bucket_index,
    passage_mask,
    target_length,
    task_group,
    cotangent,
):
    shards = (
        self_projection,
        self_output,
        cross_query,
        cross_memory,
        cross_output,
        expand_weight,
        contract_weight,
        norm_gains,
    )
    count, length, width = decoder_in.shape
    ctx_rows = encoder_out.shape[1]
    buckets, heads = bias_table.shape
    head_dim = width // heads
    inverse = head_dim ** (-0.5)
    positions = jnp.arange(length)
    offsets = jnp.clip(positions[:, None] - positions[None, :], 0, length - 1)
    pair_bucket = jnp.take(bucket_index, offsets.reshape(-1))
    one_hot = (pair_bucket[:, None] == jnp.arange(buckets)[None, :]).astype(jnp.bfloat16)
    rel_bias = dot(one_hot, bias_table).T.reshape(heads, length, length)
    causal = positions[None, :] <= positions[:, None]
    allowed = (causal[None] & (positions[None, None, :] < target_length[:, None, None]))[:, None]
    visible = (passage_mask > 0)[:, None, None, :]
    params = fetch(shards)
    output, saved = run_forward(params, decoder_in, encoder_out, allowed, visible, rel_bias)
    projection, self_out, cross_in, memory_in, cross_out, expand, contract, gains = params
    (
        normed_a,
        unit_a,
        factor_a,
        query_rows,
        key_rows,
        value_rows,
        self_probs,
        self_mix,
        normed_b,
        unit_b,
        factor_b,
        cross_rows,
        cross_keys,
        cross_vals,
        cross_probs,
        cross_mix,
        normed_c,
        unit_c,
        factor_c,
        hidden,
        active,
        scale_gain,
    ) = saved
    rows_total = count * length
    share = rows_total // lax.axis_size("ctx")
    start = lax.axis_index("ctx") * share

    def sliced(values):
        return lax.dynamic_slice_in_dim(values, start, share, 0)

    task_scale = jnp.where(task_group == 0, 1.0, jnp.where(task_group == 1, 0.5, 2.0)).astype(
        jnp.float32
    )
    row_live = (positions[None, :] < target_length[:, None]).astype(jnp.float32)
    grad_out = (
        cotangent.astype(jnp.float32) * (task_scale[:, None] * row_live)[:, :, None]
    ).reshape(rows_total, width)
    low_out = to_low(grad_out)
    grad_active = dot_t(low_out, contract)
    unused_value, gelu_pull = jax.vjp(gelu_tanh, hidden)
    grad_hidden = to_low(gelu_pull(grad_active)[0])
    grad_normed_c = dot_t(grad_hidden, expand)
    gain_c = jnp.sum(sliced(grad_normed_c * unit_c), axis=0)
    grad_after_cross = grad_out + norm_back(grad_normed_c, unit_c, factor_c, scale_gain[2])
    low_cross = to_low(grad_after_cross)
    grad_mix = to_low(dot_t(low_cross, cross_out)).reshape(count, length, heads, head_dim)
    grad_probs = jnp.einsum(
        "nihd,njhd->nhij", grad_mix, cross_vals, preferred_element_type=jnp.float32
    )
    row_dot = lax.psum(jnp.sum(grad_probs * cross_probs, axis=-1), "ctx")
    grad_scores = to_low(cross_probs * (grad_probs - row_dot[..., None]))
    partial_query = (
        jnp.einsum("nhij,njhd->nihd", grad_scores, cross_keys, preferred_element_type=jnp.float32)
        * inverse
    )
    grad_query = to_low(lax.psum(partial_query, "ctx")).reshape(rows_total, width)
    grad_key = (
        jnp.einsum("nhij,nihd->njhd", grad_scores, cross_rows, preferred_element_type=jnp.float32)
        * inverse
    )
    grad_value = jnp.einsum(
        "nhij,nihd->njhd", to_low(cross_probs), grad_mix, preferred_element_type=jnp.float32
    )
    grad_memory = to_low(jnp.stack([grad_key, grad_value], axis=2)).reshape(
        count * ctx_rows, 2 * width
    )
    encoder_rows = encoder_out.reshape(count * ctx_rows, width)
    grad_cross_memory = outer_sum(encoder_rows, grad_memory)
    grad_encoder = to_low(dot_t(grad_memory, memory_in)).reshape(count, ctx_rows, width)
    grad_normed_b = dot_t(grad_query, cross_in)
    gain_b = jnp.sum(sliced(grad_normed_b * unit_b), axis=0)
    grad_after_self = grad_after_cross + norm_back(grad_normed_b, unit_b, factor_b, scale_gain[1])
    low_self = to_low(grad_after_self)
    grad_self_mix = to_low(dot_t(low_self, self_out)).reshape(count, length, heads, head_dim)
    grad_probs_self = jnp.einsum(
        "nihd,njhd->nhij", grad_self_mix, value_rows, preferred_element_type=jnp.float32
    )
    self_dot = jnp.sum(grad_probs_self * self_probs, axis=-1, keepdims=True)
    grad_scores_self = to_low(self_probs * (grad_probs_self - self_dot))
    pair_grad = jnp.sum(grad_scores_self.astype(jnp.float32), axis=0).reshape(
        heads, length * length
    )
    pair_count = length * length // lax.axis_size("ctx")
    pair_start = lax.axis_index("ctx") * pair_count
    pair_slice = lax.dynamic_slice_in_dim(pair_grad, pair_start, pair_count, 1)
    hot_slice = lax.dynamic_slice_in_dim(one_hot.astype(jnp.float32), pair_start, pair_count, 0)
    table_term = lax.dot_general(
        hot_slice,
        pair_slice,
        (((0,), (1,)), ((), ())),
        precision=lax.Precision.HIGHEST,
        preferred_element_type=jnp.float32,
    )
    grad_table = lax.psum(table_term, ("pb", "ctx"))
    grad_q = (
        jnp.einsum(
            "nhij,njhd->nihd", grad_scores_self, key_rows, preferred_element_type=jnp.float32
        )
        * inverse
    )
    grad_k = (
        jnp.einsum(
            "nhij,nihd->njhd", grad_scores_self, query_rows, preferred_element_type=jnp.float32
        )
        * inverse
    )
    grad_v = jnp.einsum(
        "nhij,nihd->njhd", to_low(self_probs), grad_self_mix, preferred_element_type=jnp.float32
    )
    grad_joined = to_low(jnp.stack([grad_q, grad_k, grad_v], axis=2)).reshape(rows_total, 3 * width)
    grad_normed_a = dot_t(grad_joined, projection)
    gain_a = jnp.sum(sliced(grad_normed_a * unit_a), axis=0)
    grad_decoder = to_low(
        grad_after_self + norm_back(grad_normed_a, unit_a, factor_a, scale_gain[0])
    ).reshape(count, length, width)
    gain_grads = jnp.stack([gain_a, gain_b, gain_c])
    pairs = (
        (normed_a, grad_joined),
        (self_mix, low_self),
        (normed_b, grad_query),
        (cross_mix, low_cross),
        (normed_c, grad_hidden),
        (active, low_out),
    )
    partials = tuple((outer_sum(sliced(left), sliced(right)) for left, right in pairs))
    summed = (
        lax.psum_scatter(partials[0], ("pb", "ctx"), scatter_dimension=0, tiled=True),
        lax.psum_scatter(partials[1], ("pb", "ctx"), scatter_dimension=0, tiled=True),
        lax.psum_scatter(partials[2], ("pb", "ctx"), scatter_dimension=0, tiled=True),
        lax.psum_scatter(grad_cross_memory, ("pb", "ctx"), scatter_dimension=0, tiled=True),
        lax.psum_scatter(partials[3], ("pb", "ctx"), scatter_dimension=0, tiled=True),
        lax.psum_scatter(partials[4], ("pb", "ctx"), scatter_dimension=0, tiled=True),
        lax.psum_scatter(partials[5], ("pb", "ctx"), scatter_dimension=0, tiled=True),
        lax.psum_scatter(gain_grads, ("pb", "ctx"), scatter_dimension=1, tiled=True),
    )
    block_output = to_low(output).reshape(count, length, width)
    return (
        block_output,
        grad_decoder,
        grad_encoder,
        summed[0],
        summed[1],
        summed[2],
        summed[3],
        summed[4],
        summed[5],
        summed[6],
        summed[7],
        grad_table,
    )


def swap_ctx(values, mask):
    size = lax.axis_size("ctx")
    return lax.ppermute(values, "ctx", [(i, i ^ mask) for i in range(size)])


def swap_pb(values, mask):
    size = lax.axis_size("pb")
    return lax.ppermute(values, "pb", [(i, i ^ mask) for i in range(size)])


def exchange(values, axis):
    return lax.all_to_all(values, axis, 0, 0, tiled=True)


def all_pb(values):
    size = lax.axis_size("pb")
    return [values] + [swap_pb(values, r) for r in range(1, size)]


def after(values, earlier):
    return lax.optimization_barrier((values, earlier))[0]


def all_chips(values):
    return [values] + [swap_ctx(values, mask) for mask in range(2, lax.axis_size("ctx"), 2)]


def tree(terms):
    while len(terms) > 1:
        terms = [a + b for a, b in zip(terms[0::2], terms[1::2])]
    return terms[0]


def sum_chips(values):
    return tree([part.astype(FULL) for part in all_chips(values)]).astype(LOW)


def to_owners(parts):
    return [parts[0]] + [swap_pb(part, r) for r, part in enumerate(parts) if r]


def pick(low, high):
    lanes = lax.broadcasted_iota(jnp.int32, low.shape, 1)
    return jnp.where(lanes < low.shape[1] // 2, low, high)


def lane_mask(values, side):
    zeros = jnp.zeros_like(values)
    return pick(values, zeros) if side == 0 else pick(zeros, values)


def join(first, mine, other, axis=1):
    return jnp.where(
        first,
        jnp.concatenate([mine, other], axis=axis),
        jnp.concatenate([other, mine], axis=axis),
    )


def half_of(first, values, axis=1):
    middle = values.shape[axis] // 2
    if axis == 0:
        return jnp.where(first, values[:middle], values[middle:])
    return jnp.where(first, values[:, :middle], values[:, middle:])


CORE, CHIP, PB, CTX = range(4)


def prepare_kernel(proj, self_out, cross_in, gains, out):
    count = gains.shape[0]
    row = lax.broadcasted_iota(jnp.int32, (count, 128), 0)
    lane = lax.broadcasted_iota(jnp.int32, (count, 128), 1)
    columns = outer_sum(gains[...], jnp.where(row == lane, 1.0, 0.0).astype(LOW)).astype(LOW)
    at = 0
    for part in (proj[...], self_out[...], cross_in[...], columns):
        out[:, at : at + part.shape[1]] = part
        at += part.shape[1]


def place(here, ins, outs, ctx):
    first = here[CORE] == 0
    pb, rows = ins[0].shape[:2]
    for i, (begin, flip) in enumerate([(0, 0), (0, 1), (0, 2), (0, 3), (pb // 2, 3)]):
        mine, other = ins[2 * i], ins[2 * i + 1]
        chip = here[CHIP] ^ flip
        for z in range(mine.shape[0]):
            both = join(first, mine[z], other[z], 0)
            owner = (begin + z) ^ here[PB]
            slot = pl.multiple_of((owner * (ctx // 2) + chip) * 2 * rows, 16)
            at = 0
            for out in outs:
                width = out.shape[1]
                out[pl.ds(slot, 2 * rows), :] = both[:, at : at + width]
                at += width


def first_hop(own):
    return swap_ctx(own, 2), swap_ctx(own, 4)


def second_hop(own, along):
    middle = own.shape[0] // 2
    low = swap_ctx(along[0][:middle], 4)
    high = swap_ctx(along[1][middle:], 2)
    blocks = []
    for array in (own, *along, low, high):
        blocks += [array, swap_ctx(array, 1)]
    return blocks


def self_kernel(ctx, here, length, x, table, *refs):
    blocks, refs = refs[:-12], refs[-12:]
    proj, self_out, cross_in, gains_out, p1, probs, mix, x1, h1, h2, cq, columns = refs
    rows, width = x.shape
    heads = width // HEAD
    pair = 2 * HEAD
    inverse = HEAD ** (-0.5)
    place(here, blocks, [proj, self_out, cross_in, columns], ctx)
    gains = columns[...].astype(FULL).T
    gains_out[...] = gains[: gains_out.shape[0]]
    xf = x[...].astype(FULL)
    unit, _ = rms_unit(xf)
    normed = (unit * gains[0:1, :]).astype(LOW)
    h1[...] = normed
    joined = dot(normed, proj[...]).astype(LOW)
    p1[...] = joined
    row = lax.broadcasted_iota(jnp.int32, (rows, rows), 0)
    col = lax.broadcasted_iota(jnp.int32, (rows, rows), 1)
    allowed = (col <= row) & (col < length[0])
    mixes = []
    for g in range(heads // 2):
        at = g * pair
        q = joined[:, at : at + pair]
        k = joined[:, width + at : width + at + pair]
        v = joined[:, 2 * width + at : 2 * width + at + pair]
        mixed = []
        for side in range(2):
            head = 2 * g + side
            bias = pltpu.roll(
                jnp.broadcast_to(table[head : head + 1, :], (rows, rows)),
                1,
                axis=1,
                stride=1,
                stride_axis=0,
            )
            scores = jnp.where(allowed, dot_t(lane_mask(q, side), k) * inverse + bias, MASKED)
            powers = jnp.exp(scores - jnp.max(scores, axis=-1, keepdims=True))
            prob = powers / jnp.sum(powers, axis=-1, keepdims=True)
            probs[head] = prob
            mixed.append(dot(prob.astype(LOW), v))
        mixes.append(pick(*mixed).astype(LOW))
    mixes = jnp.concatenate(mixes, axis=1)
    mix[...] = mixes
    after_self = xf + dot(mixes, self_out[...])
    x1[...] = after_self
    unit, _ = rms_unit(after_self)
    normed = (unit * gains[1:2, :]).astype(LOW)
    h2[...] = normed
    cq[...] = dot(normed, half_of(here[CORE] == 0, cross_in[...])).astype(LOW)


def memory_kernel(ctx, here, mine, other, *refs):
    blocks, (memory_in, memory) = refs[:-2], refs[-2:]
    place(here, blocks, [memory_in], ctx)
    first = here[CORE] == 0
    width = mine.shape[1]
    keys = half_of(first, memory_in[:, :width])
    values = half_of(first, memory_in[:, width:])
    weight = jnp.concatenate([keys, values], axis=1)
    rows = mine.shape[0]
    memory[:rows] = dot(mine[...], weight).astype(LOW)
    memory[rows:] = dot(other[...], weight).astype(LOW)


def pack_stats(tops, totals):
    rows = tops[0].shape[0]
    lanes = lax.broadcasted_iota(jnp.int32, (rows, 128), 1)
    columns = jnp.zeros((rows, 128), FULL)
    for index, column in enumerate(tops + totals):
        columns = jnp.where(lanes // 3 == index, column, columns)
    high = columns.astype(LOW).astype(FULL)
    middle = (columns - high).astype(LOW).astype(FULL)
    kind = lanes % 3
    return jnp.where(kind == 0, high, jnp.where(kind == 1, middle, columns - high - middle)).astype(
        LOW
    )


def read_stats(packed, heads):
    values = packed.astype(FULL)
    columns = [
        values[:, i : i + 1] + values[:, i + 1 : i + 2] + values[:, i + 2 : i + 3]
        for i in range(0, 6 * heads, 3)
    ]
    return columns[:heads], columns[heads:]


def cross_kernel(cq, memory, visible, packed):
    half = cq.shape[1]
    pair = 2 * HEAD
    inverse = HEAD ** (-0.5)
    seen = visible[...] > 0
    tops, totals, mixes = [], [], []
    for at in range(0, half, pair):
        q = cq[:, at : at + pair]
        k = memory[:, at : at + pair]
        v = memory[:, half + at : half + at + pair]
        mixed = []
        for side in range(2):
            scores = jnp.where(seen, dot_t(lane_mask(q, side), k) * inverse, MASKED)
            top = jnp.max(scores, axis=-1, keepdims=True)
            powers = jnp.where(seen, jnp.exp(scores - top), 0.0)
            tops.append(top)
            totals.append(jnp.sum(powers, axis=-1, keepdims=True))
            mixed.append(dot(powers.astype(LOW), v))
        mixes.append(pick(*mixed).astype(LOW))
    packed[...] = jnp.concatenate(mixes + [pack_stats(tops, totals)], axis=1)


def spread(columns):
    shape = (columns[0].shape[0], 2 * HEAD)
    return jnp.concatenate(
        [
            pick(jnp.broadcast_to(a, shape), jnp.broadcast_to(b, shape))
            for a, b in zip(columns[0::2], columns[1::2])
        ],
        axis=1,
    )


def merge_kernel(here, *refs):
    ins, mix, stats = refs[:-2], refs[-2], refs[-1]
    half = mix.shape[1]
    heads = half // HEAD
    packed = [ref[...] for ref in ins]
    step = 1
    while step < len(packed):
        flip = (here[CHIP] & step) != 0
        packed = [jnp.where(flip, packed[i ^ step], packed[i]) for i in range(len(packed))]
        step *= 2
    read = [read_stats(p[:, half:], heads) for p in packed]
    tops, totals, scales = [], [], []
    for h in range(heads):
        top = read[0][0][h]
        for other in read[1:]:
            top = jnp.maximum(top, other[0][h])
        scale = [jnp.exp(r[0][h] - top) for r in read]
        total = tree([r[1][h] * w for r, w in zip(read, scale)])
        tops.append(top)
        totals.append(total)
        scales.append([w / total for w in scale])
    terms = [
        p[:, :half].astype(FULL) * spread([scale[i] for scale in scales])
        for i, p in enumerate(packed)
    ]
    mix[...] = tree(terms).astype(LOW)
    stats[...] = pack_stats(tops, totals)


def gelu_parts(values):
    slope = (2.0 / jnp.pi) ** 0.5
    square = values * values
    bent = jnp.tanh(slope * (values + 0.044715 * values * square))
    active = 0.5 * values * (1.0 + bent)
    inner = slope * (1.0 + 3 * 0.044715 * square)
    return active, 0.5 * (1.0 + bent) + 0.5 * values * (1.0 - bent * bent) * inner


def task_rows(length, task, cot):
    rows = lax.broadcasted_iota(jnp.int32, cot.shape, 0)
    weight = jnp.where(task[0] == 0, 1.0, jnp.where(task[0] == 1, 0.5, 2.0)).astype(FULL)
    return jnp.where(rows < length[0], cot[...].astype(FULL) * weight, 0.0)


def feed_weights(here, mine, other, expand, contract):
    first = here[CORE] == 0
    width = contract.shape[1]
    slab = mine.shape[1]
    share = slab // 4
    for z in range(mine.shape[0]):
        owner = z
        contract[pl.ds(pl.multiple_of(2 * owner * slab, 16), 2 * slab), :] = join(
            first, mine[z, :, :width], other[z, :, :width], 0
        )
        for r in range(4):
            rows = slice(r * share, (r + 1) * share)
            both = join(first, mine[z, rows, width:], other[z, rows, width:], 0)
            at = pl.multiple_of((owner * 4 + (here[CHIP] ^ r)) * 2 * share, 16)
            expand[pl.ds(at, 2 * share), :] = both


def feed_kernel(
    ctx,
    here,
    length,
    task,
    mix_mine,
    mix_other,
    x1,
    gains,
    feed_mine,
    feed_other,
    cot,
    *refs,
):
    blocks, outs = refs[:-10], refs[-10:]
    place(here, blocks, [outs[0]], ctx)
    feed_step(
        here, length, task, mix_mine, mix_other, x1, gains, feed_mine, feed_other, cot, *outs
    )


def feed_step(
    here,
    length,
    task,
    mix_mine,
    mix_other,
    x1,
    gains,
    feed_mine,
    feed_other,
    cot,
    cross_out,
    x2,
    h3,
    active,
    low_out,
    grad_hidden,
    partial,
    part_out,
    expand,
    contract,
):
    first = here[CORE] == 0
    after_cross = x1[...] + dot(join(first, mix_mine[...], mix_other[...]), cross_out[...])
    x2[...] = after_cross
    unit, _ = rms_unit(after_cross)
    normed = (unit * gains[2:3, :]).astype(LOW)
    h3[...] = normed
    low = task_rows(length, task, cot).astype(LOW)
    low_out[...] = low
    feed_weights(here, feed_mine, feed_other, expand, contract)
    value, slope = gelu_parts(dot(normed, expand[...]))
    value = value.astype(LOW)
    grad = (dot_t(low, contract[...]) * slope).astype(LOW)
    active[...] = value
    grad_hidden[...] = grad
    partial[...] = dot_t(grad, half_of(first, expand[...], 0)).astype(LOW)
    part_out[...] = dot(value, half_of(first, contract[...])).astype(LOW)


def feed_grad_kernel(share, here, active, low_out, h3, grad_hidden, out, contract, expand):
    contract[...] = outer_sum(active[...], low_out[...])
    expand[...] = outer_sum(h3[...], grad_hidden[...])
    pb = out.shape[0]
    slab = contract.shape[0] // pb // 2
    block = expand.shape[0] // pb
    for z in range(pb):
        at = pl.multiple_of((2 * z + here[CORE]) * slab, 16)
        out[z, :slab] = contract[pl.ds(at, slab)].astype(LOW)
        rows = [
            expand[pl.ds(pl.multiple_of(z * block + at + here[CORE] * share, 8), share)]
            for at in range(0, block, 2 * share)
        ]
        out[z, slab:] = jnp.concatenate(rows, axis=0).astype(LOW)


def cross_back_kernel(
    here,
    length,
    task,
    sums_mine,
    sums_other,
    x2,
    gains,
    cot,
    cross_out,
    cq,
    memory,
    visible,
    stats,
    mix,
    dx2,
    low_cross,
    grad_cq,
    grad_mine,
    grad_other,
    gain_grad,
):
    first = here[CORE] == 0
    half = mix.shape[1]
    heads = half // HEAD
    pair = 2 * HEAD
    inverse = HEAD ** (-0.5)
    unit, factor = rms_unit(x2[...])
    grad = join(first, sums_mine[...], sums_other[...]).astype(FULL)
    gain_grad[...] = jnp.sum(grad * unit, axis=0, keepdims=True)
    back = task_rows(length, task, cot) + norm_back(grad, unit, factor, gains[2:3, :])
    dx2[...] = back
    low = back.astype(LOW)
    low_cross[...] = low
    grad_mix = dot_t(low, half_of(first, cross_out[...], 0)).astype(LOW)
    seen = visible[...] > 0
    tops, totals = read_stats(stats[...], heads)
    for g in range(heads // 2):
        at = g * pair
        q = cq[:, at : at + pair]
        k = memory[:, at : at + pair]
        v = memory[:, half + at : half + at + pair]
        do = grad_mix[:, at : at + pair]
        weighed = do.astype(FULL) * mix[:, at : at + pair].astype(FULL)
        queries, keys, values = [], [], []
        for side in range(2):
            head = 2 * g + side
            qs, ds = lane_mask(q, side), lane_mask(do, side)
            scores = jnp.where(seen, dot_t(qs, k) * inverse, MASKED)
            prob = jnp.where(seen, jnp.exp(scores - tops[head]) * (1.0 / totals[head]), 0.0)
            rho = jnp.sum(lane_mask(weighed, side), axis=-1, keepdims=True)
            grad_scores = (prob * (dot_t(ds, v) - rho)).astype(LOW)
            queries.append(dot(grad_scores, k))
            keys.append(outer_sum(grad_scores, qs))
            values.append(outer_sum(prob.astype(LOW), ds))
        grad_cq[:, at : at + pair] = (pick(*queries) * inverse).astype(LOW)
        keys = ((keys[0] + keys[1]) * inverse).astype(LOW)
        values = (values[0] + values[1]).astype(LOW)
        passage = grad_mine.shape[0]
        for ref, begin in ((grad_mine, 0), (grad_other, passage)):
            ref[:, at : at + pair] = keys[begin : begin + passage]
            ref[:, half + at : half + at + pair] = values[begin : begin + passage]


def memory_grad_kernel(pb, here, mine, other, grad_mine, grad_other, *refs):
    outs, whole = refs[:-1], refs[-1]
    whole[...] = outer_sum(mine[...], grad_mine[...]) + outer_sum(other[...], grad_other[...])
    share = whole.shape[0] // pb // len(outs)
    for r, out in enumerate(outs):
        chip = here[CHIP] ^ r
        for z in range(pb):
            at = pl.multiple_of((z * len(outs) + chip) * share, 16)
            out[z * share : (z + 1) * share] = whole[pl.ds(at, share)].astype(LOW)


def encoder_grad_kernel(here, mine, other, memory_in, grad):
    first = here[CORE] == 0
    half = mine.shape[1] // 2
    keys = join(first, mine[:, :half], other[:, :half])
    values = join(first, mine[:, half:], other[:, half:])
    grad[...] = dot_t(jnp.concatenate([keys, values], axis=1), memory_in[...]).astype(LOW)


def owned(left, choose):
    return dot(left, choose).astype(LOW)


def self_back_kernel(
    here,
    cq_mine,
    cq_other,
    cross_in,
    x1,
    gains,
    dx2,
    self_out,
    p1,
    probs,
    x,
    proj,
    gain_grad,
    low_self,
    grad_p1,
    grad_x,
    small,
):
    rows, width = x.shape
    heads = width // HEAD
    pair = 2 * HEAD
    inverse = HEAD ** (-0.5)
    grad = dot_t(join(here[CORE] == 0, cq_mine[...], cq_other[...]), cross_in[...])
    unit, factor = rms_unit(x1[...])
    small[...] = jnp.zeros_like(small)
    small[1:2, :] = jnp.sum(grad * unit, axis=0, keepdims=True)
    small[2:3, :] = gain_grad[...]
    dx1 = dx2[...] + norm_back(grad, unit, factor, gains[1:2, :])
    low = dx1.astype(LOW)
    low_self[...] = low
    row = lax.broadcasted_iota(jnp.int32, (rows, rows), 0)
    col = lax.broadcasted_iota(jnp.int32, (rows, rows), 1)
    flip = jnp.where(row + col == rows - 1, 1.0, 0.0).astype(LOW)
    grad_mix = dot_t(low, self_out[...]).astype(LOW)
    parts = [[], [], []]
    for g in range(heads // 2):
        at = g * pair
        q = p1[:, at : at + pair]
        k = p1[:, width + at : width + at + pair]
        v = p1[:, 2 * width + at : 2 * width + at + pair]
        do = grad_mix[:, at : at + pair]
        queries, keys, values = [], [], []
        for side in range(2):
            head = 2 * g + side
            ds = lane_mask(do, side)
            prob = probs[head]
            grad_probs = dot_t(ds, v)
            rho = jnp.sum(prob * grad_probs, axis=-1, keepdims=True)
            grad_scores = (prob * (grad_probs - rho)).astype(LOW)
            turned = pltpu.roll(dot(flip, grad_scores), 0, axis=1, stride=1, stride_axis=0)
            small[3 + head : 4 + head, :rows] = jnp.sum(turned, axis=0, keepdims=True)
            queries.append(dot(grad_scores, k))
            keys.append(outer_sum(grad_scores, lane_mask(q, side)))
            values.append(outer_sum(prob.astype(LOW), ds))
        parts[0].append((pick(*queries) * inverse).astype(LOW))
        parts[1].append(((keys[0] + keys[1]) * inverse).astype(LOW))
        parts[2].append((values[0] + values[1]).astype(LOW))
    joined = jnp.concatenate(parts[0] + parts[1] + parts[2], axis=1)
    grad_p1[...] = joined
    grad = dot_t(joined, proj[...])
    unit, factor = rms_unit(x[...].astype(FULL))
    small[0:1, :] = jnp.sum(grad * unit, axis=0, keepdims=True)
    grad_x[...] = (dx1 + norm_back(grad, unit, factor, gains[0:1, :])).astype(LOW)


def feed_total_kernel(here, parts, contract, *refs):
    outs, rows = refs[:-1], refs[-1]
    total = tree([parts[z].astype(FULL) for z in range(parts.shape[0])])
    slab = contract.shape[0]
    contract[...] = total[:slab]
    rows[...] = total[slab:]
    share = outs[0].shape[0]
    for r, out in enumerate(outs):
        out[...] = rows[pl.ds(pl.multiple_of((here[CHIP] ^ r) * share, 8), share)].astype(LOW)


def expand_total_kernel(pb, here, *refs):
    parts, out = [ref[...].astype(FULL) for ref in refs[:-1]], refs[-1]
    step = 1
    while step < len(parts):
        flip = (here[CHIP] & step) != 0
        parts = [jnp.where(flip, parts[i ^ step], parts[i]) for i in range(len(parts))]
        step *= 2
    units = parts[0].shape[1] // pb
    out[...] = jnp.concatenate(
        [part[:, q * units : (q + 1) * units] for q in range(pb) for part in parts], axis=1
    )


def attention_grad_kernel(
    count,
    here,
    mix_mine,
    mix_other,
    low_cross,
    h2,
    cq_mine,
    cq_other,
    mix1,
    low_self,
    h1,
    grad_p1,
    small,
    *refs,
):
    pieces, out, choose, sums = refs[:count], *refs[count:]
    first = here[CORE] == 0
    pb = out.shape[0]
    width = mix1.shape[1]
    share = sums.shape[0] // pb
    lane = lax.broadcasted_iota(jnp.int32, choose.shape, 1)
    row = lax.broadcasted_iota(jnp.int32, choose.shape, 0)
    mine = lane // share * (width // pb) + here[CTX] * share + lane % share
    choose[...] = jnp.where(row == mine, 1.0, 0.0).astype(LOW)

    def owned(left, right):
        return outer_sum(dot(left, choose[...]).astype(LOW), right)

    sums[:, : 3 * width] = owned(h1[...], grad_p1[...])
    sums[:, 3 * width : 4 * width] = owned(mix1[...], low_self[...])
    cq = join(first, cq_mine[...], cq_other[...])
    sums[:, 4 * width : 5 * width] = owned(h2[...], cq)
    mix2 = join(first, mix_mine[...], mix_other[...])
    sums[:, 5 * width :] = owned(mix2, low_cross[...])
    total = tree([piece[...].astype(FULL) for piece in pieces])
    both = 2 * share
    for z in range(pb):
        rows = sums[z * share : (z + 1) * share]
        blocks = [rows[:, a : a + width] for a in range(0, 6 * width, width)]
        blocks += [total[z * both : (z + 1) * both], small[...]]
        out[z] = jnp.concatenate(blocks, axis=0).astype(LOW)


def attention_total_kernel(
    here, parts, hot, proj_grad, out_grad, query_grad, cross_grad, mine, other, gain_grad, table
):
    total = tree([parts[z].astype(FULL) for z in range(parts.shape[0])])
    first = here[CORE] == 0
    share, width = out_grad.shape
    blocks = [total[a : a + share] for a in range(0, 8 * share, share)]
    proj_grad[...] = jnp.concatenate(blocks[:3], axis=1)
    out_grad[...] = blocks[3]
    query_grad[...] = blocks[4]
    cross_grad[...] = blocks[5]
    mine[...] = jnp.where(first, blocks[6], blocks[7])
    other[...] = jnp.where(first, blocks[7], blocks[6])
    small = total[8 * share :]
    gains = gain_grad.shape[0]
    rows = hot.shape[1]
    shape = (width, share)
    place_of = lax.broadcasted_iota(jnp.int32, shape, 1) + (here[PB] * here[4] + here[CTX]) * share
    chosen = jnp.where(lax.broadcasted_iota(jnp.int32, shape, 0) == place_of, 1.0, 0.0)
    highest = lax.Precision.HIGHEST
    gain_grad[...] = jnp.dot(small, chosen, precision=highest, preferred_element_type=FULL)[:gains]
    heads = table.shape[0]
    whole = lax.dot_general(
        small[:, :rows],
        hot[...].astype(FULL),
        (((1,), (1,)), ((), ())),
        precision=highest,
        preferred_element_type=FULL,
    )
    table[...] = whole[gains : gains + heads]


def fast_body(
    decoder_in,
    encoder_out,
    self_projection,
    self_output,
    cross_query,
    cross_memory,
    cross_output,
    expand_weight,
    contract_weight,
    norm_gains,
    bias_table,
    bucket_index,
    passage_mask,
    target_length,
    task_group,
    cotangent,
):
    pb, ctx = lax.axis_size("pb"), lax.axis_size("ctx")
    mine_pb, mine_ctx = lax.axis_index("pb"), lax.axis_index("ctx")
    here = jnp.stack([mine_ctx & 1, mine_ctx >> 1, mine_pb, mine_ctx, jnp.int32(ctx)])
    here = here.astype(jnp.int32)
    rows, width = decoder_in.shape[1:]
    half = width // 2
    passage = encoder_out.shape[1]
    buckets, heads = bias_table.shape
    share = self_projection.shape[0]
    hidden = expand_weight.shape[1]
    slab = contract_weight.shape[0]
    units = pb * slab
    chips = ctx // 2
    x, e, cot = decoder_in[0], encoder_out[0], cotangent[0]

    (columns,) = call(
        prepare_kernel,
        [((share, 5 * width + 128), LOW)],
        [self_projection, self_output, cross_query, norm_gains],
    )
    columns = jnp.stack(all_pb(columns))
    mixed = expand_weight.reshape(share, pb, chips, 2 * slab).transpose(2, 0, 1, 3)
    mixed = mixed.reshape(chips, share, 2 * units)
    chip = mine_ctx >> 1
    mixed = [lax.dynamic_index_in_dim(mixed, chip ^ r, 0, False) for r in range(chips)]
    mixed = jnp.concatenate([mixed[0]] + [swap_ctx(mixed[r], 2 * r) for r in range(1, chips)])
    e_other = swap_ctx(e, 1)
    visible = jnp.concatenate([passage_mask, swap_ctx(passage_mask, 1)], axis=1)
    columns = after(columns, (e_other, visible, mixed))
    early = first_hop(columns)
    proj_blocks = second_hop(columns, early)
    others = jnp.concatenate([cross_memory, cross_output], axis=1)
    others = jnp.stack(all_pb(after(others, columns)))
    others_early = first_hop(after(others, early))
    x = after(x, others_early)
    feed = jnp.concatenate([contract_weight, mixed], axis=1)
    feed = jnp.broadcast_to(after(feed, others)[None], (pb,) + feed.shape)
    feed = exchange(feed, "pb")

    hot = (jnp.arange(buckets)[:, None] == bucket_index[::-1][None, :]).astype(LOW)
    table = outer_sum(bias_table, hot)

    proj, self_out, cross_in, gains, p1, probs, mix1, x1, h1, h2, cq = call(
        functools.partial(self_kernel, ctx),
        [
            ((width, 3 * width), LOW),
            ((width, width), LOW),
            ((width, width), LOW),
            ((norm_gains.shape[0], width), FULL),
            ((rows, 3 * width), LOW),
            ((heads, rows, rows), FULL),
            ((rows, width), LOW),
            ((rows, width), FULL),
            ((rows, width), LOW),
            ((rows, width), LOW),
            ((rows, half), LOW),
        ],
        [here, target_length, x, table] + proj_blocks,
        scalars=2,
        scratch=[pltpu.VMEM((width, 128), LOW)],
    )
    others_blocks = second_hop(others, others_early)

    def part(size, index):
        return [(b, b.shape[:2] + (size * width,), (0, 0, index)) for b in others_blocks]

    feed = after(feed, cq)
    feed_other = swap_ctx(feed, 1)
    memory_in, memory = call(
        functools.partial(memory_kernel, ctx),
        [((width, 2 * width), LOW), ((2 * passage, width), LOW)],
        [here, e, e_other] + part(2, 0),
        scalars=1,
    )
    (packed,) = call(cross_kernel, [((rows, half + 128), LOW)], [cq, memory, visible])
    mix2, stats = call(
        merge_kernel,
        [((rows, half), LOW), ((rows, 128), LOW)],
        [here] + all_chips(packed),
        scalars=1,
    )
    mix2_other = swap_ctx(mix2, 1)

    cross_out, x2, h3, active, low_out, grad_hidden, partial, part_out = call(
        functools.partial(feed_kernel, ctx),
        [
            ((width, width), LOW),
            ((rows, width), FULL),
            ((rows, width), LOW),
            ((rows, 2 * units), LOW),
            ((rows, width), LOW),
            ((rows, 2 * units), LOW),
            ((rows, half), LOW),
            ((rows, half), LOW),
        ],
        [
            here,
            target_length,
            task_group,
            mix2,
            mix2_other,
            x1,
            gains,
            feed,
            feed_other,
            cot,
        ]
        + part(1, 2),
        scalars=3,
        scratch=[pltpu.VMEM((width, 2 * units), LOW), pltpu.VMEM((2 * units, width), LOW)],
    )
    sums = sum_chips(partial)
    sums_other = swap_ctx(sums, 1)
    (feed_grads,) = call(
        functools.partial(feed_grad_kernel, share),
        [((pb, 2 * slab, width), LOW)],
        [here, active, low_out, h3, grad_hidden],
        scalars=1,
        scratch=[pltpu.VMEM((2 * units, width), FULL), pltpu.VMEM((width, 2 * units), FULL)],
    )
    feed_grads = exchange(feed_grads, "pb")

    dx2, low_cross, grad_cq, grad_mine, grad_other, gain_grad = call(
        cross_back_kernel,
        [
            ((rows, width), FULL),
            ((rows, width), LOW),
            ((rows, half), LOW),
            ((passage, width), LOW),
            ((passage, width), LOW),
            ((1, width), FULL),
        ],
        [
            here,
            target_length,
            task_group,
            sums,
            sums_other,
            x2,
            gains,
            cot,
            cross_out,
            cq,
            memory,
            visible,
            stats,
            mix2,
        ],
        scalars=3,
    )
    grad_cq = sum_chips(grad_cq)
    cq_other = swap_ctx(grad_cq, 1)
    pieces = call(
        functools.partial(memory_grad_kernel, pb),
        [((pb * 2 * share, width), LOW)] * chips,
        [here, e, e_other, grad_mine, grad_other],
        scalars=1,
        scratch=[pltpu.VMEM((width, width), FULL)],
    )
    pieces = [pieces[0]] + [swap_ctx(pieces[r], 2 * r) for r in range(1, chips)]
    memory_other = swap_ctx(grad_other, 1)

    low_self, grad_p1, grad_x, small = call(
        self_back_kernel,
        [
            ((rows, width), LOW),
            ((rows, 3 * width), LOW),
            ((rows, width), LOW),
            ((16, width), FULL),
        ],
        [
            here,
            grad_cq,
            cq_other,
            cross_in,
            x1,
            gains,
            dx2,
            self_out,
            p1,
            probs,
            x,
            proj,
            gain_grad,
        ],
        scalars=1,
    )

    (grads,) = call(
        functools.partial(attention_grad_kernel, chips),
        [((pb, 8 * share + 16, width), LOW)],
        [
            here,
            mix2,
            mix2_other,
            low_cross,
            h2,
            grad_cq,
            cq_other,
            mix1,
            low_self,
            h1,
            grad_p1,
            small,
        ]
        + pieces,
        scalars=1,
        scratch=[pltpu.VMEM((width, pb * share), LOW), pltpu.VMEM((pb * share, 6 * width), FULL)],
    )
    output = sum_chips(after(part_out, grads))
    grads = exchange(grads, "pb")
    (grad_encoder,) = call(
        encoder_grad_kernel,
        [((passage, width), LOW)],
        [here, after(grad_mine, grad_p1), memory_other, memory_in],
        scalars=1,
    )
    grad_contract, *expand_rows = call(
        feed_total_kernel,
        [((slab, width), FULL)] + [((share, 2 * units), LOW)] * chips,
        [here, after(feed_grads, grad_p1)],
        scalars=1,
        scratch=[pltpu.VMEM((chips * share, 2 * units), FULL)],
    )
    expand_rows = [expand_rows[0]] + [swap_ctx(expand_rows[r], 2 * r) for r in range(1, chips)]
    (grad_expand,) = call(
        functools.partial(expand_total_kernel, pb),
        [((share, hidden), FULL)],
        [here] + expand_rows,
        scalars=1,
    )
    first = (mine_ctx & 1) == 0
    block_output = (x2 + join(first, output, swap_ctx(output, 1)).astype(FULL)).astype(LOW)
    (
        grad_self_projection,
        grad_self_output,
        grad_cross_query,
        grad_cross_output,
        mine,
        other,
        grad_norm_gains,
        grad_table,
    ) = call(
        attention_total_kernel,
        [((share, 3 * width), FULL)]
        + [((share, width), FULL)] * 5
        + [(norm_gains.shape[:1] + (share,), FULL), ((heads, buckets), FULL)],
        [here, grads, hot],
        scalars=1,
    )
    other = swap_ctx(other, 1)
    grad_cross_memory = jnp.concatenate(
        [join(first, mine[:, :half], other[:, :half]), join(first, mine[:, half:], other[:, half:])],
        axis=1,
    )
    return (
        block_output[None],
        grad_x[None],
        grad_encoder[None],
        grad_self_projection,
        grad_self_output,
        grad_cross_query,
        grad_cross_memory,
        grad_cross_output,
        grad_expand,
        grad_contract,
        grad_norm_gains,
        grad_table.T,
    )


def body(*args):
    decoder_in, encoder_out, self_projection = args[:3]
    contract_weight = args[8]
    fits = (
        lax.axis_size("ctx") == 8
        and lax.axis_size("pb") == 4
        and decoder_in.shape[0] == 1
        and decoder_in.shape[1] == 128
        and self_projection.shape[0] % 8 == 0
        and contract_weight.shape[0] * 2 == self_projection.shape[0] * lax.axis_size("ctx")
        and encoder_out.shape[1] % 16 == 0
    )
    return (fast_body if fits else plain_body)(*args)


def solution(mesh):
    return jax.shard_map(
        body,
        mesh=mesh,
        in_specs=(
            P("pb", None, None),
            P("pb", "ctx", None),
            P(("pb", "ctx"), None),
            P(("pb", "ctx"), None),
            P(("pb", "ctx"), None),
            P(("pb", "ctx"), None),
            P(("pb", "ctx"), None),
            P(("pb", "ctx"), None),
            P(("pb", "ctx"), None),
            P(None, ("pb", "ctx")),
            P(),
            P(),
            P("pb", "ctx"),
            P("pb"),
            P("pb"),
            P("pb", None, None),
        ),
        out_specs=(
            P("pb", None, None),
            P("pb", None, None),
            P("pb", "ctx", None),
            P(("pb", "ctx"), None),
            P(("pb", "ctx"), None),
            P(("pb", "ctx"), None),
            P(("pb", "ctx"), None),
            P(("pb", "ctx"), None),
            P(("pb", "ctx"), None),
            P(("pb", "ctx"), None),
            P(None, ("pb", "ctx")),
            P(),
        ),
        check_vma=False,
    )
```

```python
import functools
import math

import jax
import jax.numpy as jnp
from jax import lax
from jax.experimental import pallas as pl
from jax.experimental.pallas import tpu as pltpu
from jax.sharding import PartitionSpec as P

LOW, FULL = jnp.bfloat16, jnp.float32
MASKED = -1000000000.0
EPS = 1e-06
HEAD = 64
SPARE_BYTES = 6 * 1024 * 1024


def dot(left, right, left_axis=1, right_axis=0):
    return lax.dot_general(
        left,
        right,
        (((left_axis,), (right_axis,)), ((), ())),
        preferred_element_type=FULL,
    )


def dot_t(left, right):
    return dot(left, right, 1, 1)


def outer_sum(left, right):
    return dot(left, right, 0, 0)


def rms_unit(values):
    factor = lax.rsqrt(jnp.mean(values * values, axis=-1, keepdims=True) + EPS)
    return values * factor, factor


def norm_back(grad, unit, factor, gain):
    scaled = grad * gain
    return factor * (scaled - unit * jnp.mean(scaled * unit, axis=-1, keepdims=True))


def call(kernel, outs, args, scalars=0, scratch=(), spare=SPARE_BYTES):
    arrays, specs, grid = [], [], ()
    held = [(arg[1], arg[0].dtype) if isinstance(arg, tuple) else (arg.shape, arg.dtype) for arg in args]
    held += list(outs) + [(one.shape, one.dtype) for one in scratch]
    size = sum(math.prod(shape) * jnp.dtype(dtype).itemsize for shape, dtype in held)
    for index, arg in enumerate(args):
        if isinstance(arg, tuple):
            arg, shape, place = arg
            specs.append(pl.BlockSpec(shape, lambda i, place=place: place))
            grid = (1,)
        else:
            specs.append(pl.BlockSpec(memory_space=pltpu.SMEM if index < scalars else pltpu.VMEM))
        arrays.append(arg)
    return pl.pallas_call(
        kernel,
        grid=grid,
        out_shape=[jax.ShapeDtypeStruct(shape, dtype) for shape, dtype in outs],
        in_specs=specs,
        out_specs=[pl.BlockSpec(memory_space=pltpu.VMEM) for _ in outs],
        scratch_shapes=list(scratch),
        compiler_params=pltpu.CompilerParams(vmem_limit_bytes=size + spare),
    )(*arrays)


def to_low(values):
    return values.astype(jnp.bfloat16)


def normalize(values, scale):
    factor = lax.rsqrt(jnp.mean(values * values, axis=-1, keepdims=True) + 1e-06)
    return (values * factor * scale, values * factor, factor)


def gelu_tanh(values):
    return jax.nn.gelu(values, approximate=True)


def fetch(shards):
    return (
        lax.all_gather(shards[0], ("pb", "ctx"), axis=0, tiled=True),
        lax.all_gather(shards[1], ("pb", "ctx"), axis=0, tiled=True),
        lax.all_gather(shards[2], ("pb", "ctx"), axis=0, tiled=True),
        lax.all_gather(shards[3], ("pb", "ctx"), axis=0, tiled=True),
        lax.all_gather(shards[4], ("pb", "ctx"), axis=0, tiled=True),
        lax.all_gather(shards[5], ("pb", "ctx"), axis=0, tiled=True),
        lax.all_gather(shards[6], ("pb", "ctx"), axis=0, tiled=True),
        lax.all_gather(shards[7], ("pb", "ctx"), axis=1, tiled=True),
    )


def run_forward(params, decoder, encoder, allowed, visible, rel_bias):
    projection, self_out, cross_in, memory_in, cross_out, expand, contract, gains = params
    scale_gain = gains.astype(jnp.float32)
    count, length, width = decoder.shape
    heads = rel_bias.shape[0]
    head_dim = width // heads
    inverse = head_dim ** (-0.5)
    residual = decoder.astype(jnp.float32).reshape(count * length, width)
    normed_a, unit_a, factor_a = normalize(residual, scale_gain[0])
    normed_a = to_low(normed_a)
    joined = to_low(dot(normed_a, projection)).reshape(count, length, 3, heads, head_dim)
    query_rows, key_rows, value_rows = (joined[:, :, 0], joined[:, :, 1], joined[:, :, 2])
    self_scores = (
        jnp.einsum("nihd,njhd->nhij", query_rows, key_rows, preferred_element_type=jnp.float32)
        * inverse
        + rel_bias[None]
    )
    self_probs = jax.nn.softmax(jnp.where(allowed, self_scores, -1000000000.0), axis=-1)
    self_mixed = jnp.einsum(
        "nhij,njhd->nihd", to_low(self_probs), value_rows, preferred_element_type=jnp.float32
    )
    self_mix = to_low(self_mixed.reshape(count * length, width))
    after_self = residual + dot(self_mix, self_out)
    normed_b, unit_b, factor_b = normalize(after_self, scale_gain[1])
    normed_b = to_low(normed_b)
    cross_rows = to_low(dot(normed_b, cross_in)).reshape(count, length, heads, head_dim)
    ctx_rows = encoder.shape[1]
    memory = to_low(dot(encoder.reshape(count * ctx_rows, width), memory_in)).reshape(
        count, ctx_rows, 2, heads, head_dim
    )
    cross_keys, cross_vals = (memory[:, :, 0], memory[:, :, 1])
    cross_scores = (
        jnp.einsum("nihd,njhd->nhij", cross_rows, cross_keys, preferred_element_type=jnp.float32)
        * inverse
    )
    masked = jnp.where(visible, cross_scores, -1000000000.0)
    highest_score = lax.pmax(jnp.max(masked, axis=-1), "ctx")
    total = lax.psum(
        jnp.sum(jnp.where(visible, jnp.exp(masked - highest_score[..., None]), 0.0), axis=-1), "ctx"
    )
    cross_probs = (
        jnp.where(visible, jnp.exp(masked - highest_score[..., None]), 0.0) / total[..., None]
    )
    partial_mix = jnp.einsum(
        "nhij,njhd->nihd", to_low(cross_probs), cross_vals, preferred_element_type=jnp.float32
    )
    cross_mixed = lax.psum(partial_mix, "ctx")
    cross_mix = to_low(cross_mixed.reshape(count * length, width))
    after_cross = after_self + dot(cross_mix, cross_out)
    normed_c, unit_c, factor_c = normalize(after_cross, scale_gain[2])
    normed_c = to_low(normed_c)
    hidden = dot(normed_c, expand)
    active = to_low(gelu_tanh(hidden))
    output = after_cross + dot(active, contract)
    saved = (
        normed_a,
        unit_a,
        factor_a,
        query_rows,
        key_rows,
        value_rows,
        self_probs,
        self_mix,
        normed_b,
        unit_b,
        factor_b,
        cross_rows,
        cross_keys,
        cross_vals,
        cross_probs,
        cross_mix,
        normed_c,
        unit_c,
        factor_c,
        hidden,
        active,
        scale_gain,
    )
    return (output, saved)


def plain_body(
    decoder_in,
    encoder_out,
    self_projection,
    self_output,
    cross_query,
    cross_memory,
    cross_output,
    expand_weight,
    contract_weight,
    norm_gains,
    bias_table,
    bucket_index,
    passage_mask,
    target_length,
    task_group,
    cotangent,
):
    shards = (
        self_projection,
        self_output,
        cross_query,
        cross_memory,
        cross_output,
        expand_weight,
        contract_weight,
        norm_gains,
    )
    count, length, width = decoder_in.shape
    ctx_rows = encoder_out.shape[1]
    buckets, heads = bias_table.shape
    head_dim = width // heads
    inverse = head_dim ** (-0.5)
    positions = jnp.arange(length)
    offsets = jnp.clip(positions[:, None] - positions[None, :], 0, length - 1)
    pair_bucket = jnp.take(bucket_index, offsets.reshape(-1))
    one_hot = (pair_bucket[:, None] == jnp.arange(buckets)[None, :]).astype(jnp.bfloat16)
    rel_bias = dot(one_hot, bias_table).T.reshape(heads, length, length)
    causal = positions[None, :] <= positions[:, None]
    allowed = (causal[None] & (positions[None, None, :] < target_length[:, None, None]))[:, None]
    visible = (passage_mask > 0)[:, None, None, :]
    params = fetch(shards)
    output, saved = run_forward(params, decoder_in, encoder_out, allowed, visible, rel_bias)
    projection, self_out, cross_in, memory_in, cross_out, expand, contract, gains = params
    (
        normed_a,
        unit_a,
        factor_a,
        query_rows,
        key_rows,
        value_rows,
        self_probs,
        self_mix,
        normed_b,
        unit_b,
        factor_b,
        cross_rows,
        cross_keys,
        cross_vals,
        cross_probs,
        cross_mix,
        normed_c,
        unit_c,
        factor_c,
        hidden,
        active,
        scale_gain,
    ) = saved
    rows_total = count * length
    share = rows_total // lax.axis_size("ctx")
    start = lax.axis_index("ctx") * share

    def sliced(values):
        return lax.dynamic_slice_in_dim(values, start, share, 0)

    task_scale = jnp.where(task_group == 0, 1.0, jnp.where(task_group == 1, 0.5, 2.0)).astype(
        jnp.float32
    )
    row_live = (positions[None, :] < target_length[:, None]).astype(jnp.float32)
    grad_out = (
        cotangent.astype(jnp.float32) * (task_scale[:, None] * row_live)[:, :, None]
    ).reshape(rows_total, width)
    low_out = to_low(grad_out)
    grad_active = dot_t(low_out, contract)
    unused_value, gelu_pull = jax.vjp(gelu_tanh, hidden)
    grad_hidden = to_low(gelu_pull(grad_active)[0])
    grad_normed_c = dot_t(grad_hidden, expand)
    gain_c = jnp.sum(sliced(grad_normed_c * unit_c), axis=0)
    grad_after_cross = grad_out + norm_back(grad_normed_c, unit_c, factor_c, scale_gain[2])
    low_cross = to_low(grad_after_cross)
    grad_mix = to_low(dot_t(low_cross, cross_out)).reshape(count, length, heads, head_dim)
    grad_probs = jnp.einsum(
        "nihd,njhd->nhij", grad_mix, cross_vals, preferred_element_type=jnp.float32
    )
    row_dot = lax.psum(jnp.sum(grad_probs * cross_probs, axis=-1), "ctx")
    grad_scores = to_low(cross_probs * (grad_probs - row_dot[..., None]))
    partial_query = (
        jnp.einsum("nhij,njhd->nihd", grad_scores, cross_keys, preferred_element_type=jnp.float32)
        * inverse
    )
    grad_query = to_low(lax.psum(partial_query, "ctx")).reshape(rows_total, width)
    grad_key = (
        jnp.einsum("nhij,nihd->njhd", grad_scores, cross_rows, preferred_element_type=jnp.float32)
        * inverse
    )
    grad_value = jnp.einsum(
        "nhij,nihd->njhd", to_low(cross_probs), grad_mix, preferred_element_type=jnp.float32
    )
    grad_memory = to_low(jnp.stack([grad_key, grad_value], axis=2)).reshape(
        count * ctx_rows, 2 * width
    )
    encoder_rows = encoder_out.reshape(count * ctx_rows, width)
    grad_cross_memory = outer_sum(encoder_rows, grad_memory)
    grad_encoder = to_low(dot_t(grad_memory, memory_in)).reshape(count, ctx_rows, width)
    grad_normed_b = dot_t(grad_query, cross_in)
    gain_b = jnp.sum(sliced(grad_normed_b * unit_b), axis=0)
    grad_after_self = grad_after_cross + norm_back(grad_normed_b, unit_b, factor_b, scale_gain[1])
    low_self = to_low(grad_after_self)
    grad_self_mix = to_low(dot_t(low_self, self_out)).reshape(count, length, heads, head_dim)
    grad_probs_self = jnp.einsum(
        "nihd,njhd->nhij", grad_self_mix, value_rows, preferred_element_type=jnp.float32
    )
    self_dot = jnp.sum(grad_probs_self * self_probs, axis=-1, keepdims=True)
    grad_scores_self = to_low(self_probs * (grad_probs_self - self_dot))
    pair_grad = jnp.sum(grad_scores_self.astype(jnp.float32), axis=0).reshape(
        heads, length * length
    )
    pair_count = length * length // lax.axis_size("ctx")
    pair_start = lax.axis_index("ctx") * pair_count
    pair_slice = lax.dynamic_slice_in_dim(pair_grad, pair_start, pair_count, 1)
    hot_slice = lax.dynamic_slice_in_dim(one_hot.astype(jnp.float32), pair_start, pair_count, 0)
    table_term = lax.dot_general(
        hot_slice,
        pair_slice,
        (((0,), (1,)), ((), ())),
        precision=lax.Precision.HIGHEST,
        preferred_element_type=jnp.float32,
    )
    grad_table = lax.psum(table_term, ("pb", "ctx"))
    grad_q = (
        jnp.einsum(
            "nhij,njhd->nihd", grad_scores_self, key_rows, preferred_element_type=jnp.float32
        )
        * inverse
    )
    grad_k = (
        jnp.einsum(
            "nhij,nihd->njhd", grad_scores_self, query_rows, preferred_element_type=jnp.float32
        )
        * inverse
    )
    grad_v = jnp.einsum(
        "nhij,nihd->njhd", to_low(self_probs), grad_self_mix, preferred_element_type=jnp.float32
    )
    grad_joined = to_low(jnp.stack([grad_q, grad_k, grad_v], axis=2)).reshape(rows_total, 3 * width)
    grad_normed_a = dot_t(grad_joined, projection)
    gain_a = jnp.sum(sliced(grad_normed_a * unit_a), axis=0)
    grad_decoder = to_low(
        grad_after_self + norm_back(grad_normed_a, unit_a, factor_a, scale_gain[0])
    ).reshape(count, length, width)
    gain_grads = jnp.stack([gain_a, gain_b, gain_c])
    pairs = (
        (normed_a, grad_joined),
        (self_mix, low_self),
        (normed_b, grad_query),
        (cross_mix, low_cross),
        (normed_c, grad_hidden),
        (active, low_out),
    )
    partials = tuple((outer_sum(sliced(left), sliced(right)) for left, right in pairs))
    summed = (
        lax.psum_scatter(partials[0], ("pb", "ctx"), scatter_dimension=0, tiled=True),
        lax.psum_scatter(partials[1], ("pb", "ctx"), scatter_dimension=0, tiled=True),
        lax.psum_scatter(partials[2], ("pb", "ctx"), scatter_dimension=0, tiled=True),
        lax.psum_scatter(grad_cross_memory, ("pb", "ctx"), scatter_dimension=0, tiled=True),
        lax.psum_scatter(partials[3], ("pb", "ctx"), scatter_dimension=0, tiled=True),
        lax.psum_scatter(partials[4], ("pb", "ctx"), scatter_dimension=0, tiled=True),
        lax.psum_scatter(partials[5], ("pb", "ctx"), scatter_dimension=0, tiled=True),
        lax.psum_scatter(gain_grads, ("pb", "ctx"), scatter_dimension=1, tiled=True),
    )
    block_output = to_low(output).reshape(count, length, width)
    return (
        block_output,
        grad_decoder,
        grad_encoder,
        summed[0],
        summed[1],
        summed[2],
        summed[3],
        summed[4],
        summed[5],
        summed[6],
        summed[7],
        grad_table,
    )


def swap_ctx(values, mask):
    size = lax.axis_size("ctx")
    return lax.ppermute(values, "ctx", [(i, i ^ mask) for i in range(size)])


def swap_pb(values, mask):
    size = lax.axis_size("pb")
    return lax.ppermute(values, "pb", [(i, i ^ mask) for i in range(size)])


def exchange(values, axis):
    return lax.all_to_all(values, axis, 0, 0, tiled=True)


def all_pb(values):
    size = lax.axis_size("pb")
    return [values] + [swap_pb(values, r) for r in range(1, size)]


def after(values, earlier):
    return lax.optimization_barrier((values, earlier))[0]


def all_chips(values):
    return [values] + [swap_ctx(values, mask) for mask in range(2, lax.axis_size("ctx"), 2)]


def tree(terms):
    while len(terms) > 1:
        terms = [a + b for a, b in zip(terms[0::2], terms[1::2])]
    return terms[0]


def sum_chips(values):
    return tree([part.astype(FULL) for part in all_chips(values)]).astype(LOW)


def to_owners(parts):
    return [parts[0]] + [swap_pb(part, r) for r, part in enumerate(parts) if r]


def pick(low, high):
    lanes = lax.broadcasted_iota(jnp.int32, low.shape, 1)
    return jnp.where(lanes < low.shape[1] // 2, low, high)


def lane_mask(values, side):
    zeros = jnp.zeros_like(values)
    return pick(values, zeros) if side == 0 else pick(zeros, values)


def both_heads(values):
    return jnp.concatenate([lane_mask(values, 0), lane_mask(values, 1)], axis=0)


def pick_rows(values):
    middle = values.shape[0] // 2
    return pick(values[:middle], values[middle:])


def join(first, mine, other, axis=1):
    return jnp.where(
        first,
        jnp.concatenate([mine, other], axis=axis),
        jnp.concatenate([other, mine], axis=axis),
    )


def half_of(first, values, axis=1):
    middle = values.shape[axis] // 2
    if axis == 0:
        return jnp.where(first, values[:middle], values[middle:])
    return jnp.where(first, values[:, :middle], values[:, middle:])


CORE, CHIP, PB, CTX = range(4)


def prepare_kernel(proj, self_out, cross_in, gains, out):
    count = gains.shape[0]
    row = lax.broadcasted_iota(jnp.int32, (count, 128), 0)
    lane = lax.broadcasted_iota(jnp.int32, (count, 128), 1)
    columns = outer_sum(gains[...], jnp.where(row == lane, 1.0, 0.0).astype(LOW)).astype(LOW)
    at = 0
    for part in (proj[...], self_out[...], cross_in[...], columns):
        out[:, at : at + part.shape[1]] = part
        at += part.shape[1]


def block_places(pb):
    middle = pb // 2
    return [
        [(0, 0), (0, 1), (0, 2)],
        [(r, 0) for r in range(1, pb)],
        [(r, 1) for r in range(1, pb)],
        [(r, 2) for r in range(1, pb)],
        [(r, 3) for r in range(middle)],
        [(r, 3) for r in range(middle, pb)],
    ]


def place(here, ins, outs, ctx):
    first = here[CORE] == 0
    pb = ins[2].shape[0] + 1
    rows = ins[0].shape[1]
    for i, places in enumerate(block_places(pb)):
        mine, other = ins[2 * i], ins[2 * i + 1]
        for k, (z, flip) in enumerate(places):
            both = join(first, mine[k], other[k], 0)
            owner = (z ^ here[PB]) * (ctx // 2) + (here[CHIP] ^ flip)
            slot = pl.multiple_of(owner * 2 * rows, 16)
            at = 0
            for out in outs:
                width = out.shape[1]
                out[pl.ds(slot, 2 * rows), :] = both[:, at : at + width]
                at += width


def first_hops(own):
    return swap_ctx(own, 2), swap_ctx(own, 4)


def gather_rows(own, along, far, far_along):
    middle = (far.shape[0] + 1) // 2
    low = jnp.concatenate([along[0][None], far_along[0][: middle - 1]])
    low = swap_ctx(low, 4)
    high = swap_ctx(far_along[1][middle - 1 :], 2)
    blocks = []
    for array in (jnp.stack([own, *along]), far, *far_along, low, high):
        blocks += [array, swap_ctx(array, 1)]
    return blocks, (low, high)


def self_kernel(ctx, here, length, x, table, *refs):
    blocks, refs = refs[:-12], refs[-12:]
    proj, self_out, cross_in, gains_out, p1, probs, mix, x1, h1, h2, cq, columns = refs
    rows, width = x.shape
    heads = width // HEAD
    pair = 2 * HEAD
    inverse = jnp.asarray(HEAD ** (-0.5), LOW)
    place(here, blocks, [proj, self_out, cross_in, columns], ctx)
    gains = columns[...].astype(FULL).T
    gains_out[...] = gains[: gains_out.shape[0]]
    xf = x[...].astype(FULL)
    unit, _ = rms_unit(xf)
    normed = (unit * gains[0:1, :]).astype(LOW)
    h1[...] = normed
    joined = dot(normed, proj[...]).astype(LOW)
    p1[...] = joined
    row = lax.broadcasted_iota(jnp.int32, (rows, rows), 0)
    col = lax.broadcasted_iota(jnp.int32, (rows, rows), 1)
    allowed = (col <= row) & (col < length[0])
    barred = jnp.where(allowed, 0.0, MASKED)
    mixes = []
    for g in range(heads // 2):
        at = g * pair
        q = both_heads(joined[:, at : at + pair] * inverse)
        k = joined[:, width + at : width + at + pair]
        v = joined[:, 2 * width + at : 2 * width + at + pair]
        bias = [
            pltpu.roll(
                jnp.broadcast_to(table[head : head + 1, :], (rows, rows)),
                1,
                axis=1,
                stride=1,
                stride_axis=0,
            )
            + barred
            for head in (2 * g, 2 * g + 1)
        ]
        scores = dot_t(q, k) + jnp.concatenate(bias, axis=0)
        powers = jnp.exp(scores - jnp.max(scores, axis=-1, keepdims=True))
        prob = powers * (1.0 / jnp.sum(powers, axis=-1, keepdims=True))
        probs[g] = prob
        mixes.append(pick_rows(dot(prob.astype(LOW), v)).astype(LOW))
    mixes = jnp.concatenate(mixes, axis=1)
    mix[...] = mixes
    after_self = xf + dot(mixes, self_out[...])
    x1[...] = after_self
    unit, _ = rms_unit(after_self)
    normed = (unit * gains[1:2, :]).astype(LOW)
    h2[...] = normed
    cq[...] = dot(normed, half_of(here[CORE] == 0, cross_in[...])).astype(LOW)


def memory_kernel(ctx, here, mine, other, *refs):
    blocks, (memory_in, memory) = refs[:-2], refs[-2:]
    place(here, blocks, [memory_in], ctx)
    first = here[CORE] == 0
    width = mine.shape[1]
    keys = half_of(first, memory_in[:, :width])
    values = half_of(first, memory_in[:, width:])
    weight = jnp.concatenate([keys, values], axis=1)
    rows = mine.shape[0]
    memory[:rows] = dot(mine[...], weight).astype(LOW)
    memory[rows:] = dot(other[...], weight).astype(LOW)


def pack_stats(tops, totals):
    rows = tops[0].shape[0]
    lanes = lax.broadcasted_iota(jnp.int32, (rows, 128), 1)
    columns = jnp.zeros((rows, 128), FULL)
    for index, column in enumerate(tops + totals):
        columns = jnp.where(lanes // 3 == index, column, columns)
    high = columns.astype(LOW).astype(FULL)
    middle = (columns - high).astype(LOW).astype(FULL)
    kind = lanes % 3
    return jnp.where(kind == 0, high, jnp.where(kind == 1, middle, columns - high - middle)).astype(
        LOW
    )


def read_stats(packed):
    values = packed.astype(FULL)
    return values + pltpu.roll(values, 127, axis=1) + pltpu.roll(values, 126, axis=1)


def cross_kernel(cq, memory, visible, packed):
    rows, half = cq.shape
    pair = 2 * HEAD
    inverse = jnp.asarray(HEAD ** (-0.5), LOW)
    barred = jnp.where(visible[...] > 0, 0.0, MASKED)
    tops, totals, mixes = [], [], []
    for at in range(0, half, pair):
        q = both_heads(cq[:, at : at + pair] * inverse)
        k = memory[:, at : at + pair]
        v = memory[:, half + at : half + at + pair]
        scores = dot_t(q, k) + barred
        top = jnp.max(scores, axis=-1, keepdims=True)
        powers = jnp.exp(scores - top)
        total = jnp.sum(powers, axis=-1, keepdims=True)
        tops += [top[:rows], top[rows:]]
        totals += [total[:rows], total[rows:]]
        mixes.append(pick_rows(dot(powers.astype(LOW), v)).astype(LOW))
    packed[...] = jnp.concatenate(mixes + [pack_stats(tops, totals)], axis=1)


def spread(columns):
    shape = (columns[0].shape[0], 2 * HEAD)
    return jnp.concatenate(
        [
            pick(jnp.broadcast_to(a, shape), jnp.broadcast_to(b, shape))
            for a, b in zip(columns[0::2], columns[1::2])
        ],
        axis=1,
    )


def merge_kernel(here, *refs):
    ins, mix, stats = refs[:-2], refs[-2], refs[-1]
    half = mix.shape[1]
    heads = half // HEAD
    packed = [ref[...] for ref in ins]
    step = 1
    while step < len(packed):
        flip = (here[CHIP] & step) != 0
        packed = [jnp.where(flip, packed[i ^ step], packed[i]) for i in range(len(packed))]
        step *= 2
    read = [read_stats(p[:, half:]) for p in packed]
    top = read[0]
    for other in read[1:]:
        top = jnp.maximum(top, other)
    lanes = lax.broadcasted_iota(jnp.int32, top.shape, 1)
    is_top = lanes < 3 * heads
    scales = [jnp.exp(jnp.where(is_top, r - top, 0.0)) for r in read]
    total = tree([r * pltpu.roll(w, 3 * heads, axis=1) for r, w in zip(read, scales)])
    share = 1.0 / pltpu.roll(total, 128 - 3 * heads, axis=1)
    weights = [w * share for w in scales]
    terms = [
        p[:, :half].astype(FULL) * spread([w[:, 3 * h : 3 * h + 1] for h in range(heads)])
        for p, w in zip(packed, weights)
    ]
    mix[...] = tree(terms).astype(LOW)
    stats[...] = jnp.where(is_top, top, total)


def gelu_parts(values):
    slope = (2.0 / jnp.pi) ** 0.5
    square = values * values
    bent = jnp.tanh(slope * (values + 0.044715 * values * square))
    active = 0.5 * values * (1.0 + bent)
    inner = slope * (1.0 + 3 * 0.044715 * square)
    return active, 0.5 * (1.0 + bent) + 0.5 * values * (1.0 - bent * bent) * inner


def task_rows(length, task, cot):
    rows = lax.broadcasted_iota(jnp.int32, cot.shape, 0)
    weight = jnp.where(task[0] == 0, 1.0, jnp.where(task[0] == 1, 0.5, 2.0)).astype(FULL)
    return jnp.where(rows < length[0], cot[...].astype(FULL) * weight, 0.0)


def feed_weights(here, mine, other, expand, contract):
    first = here[CORE] == 0
    width = contract.shape[1]
    slab = mine.shape[1]
    share = slab // 4
    for z in range(mine.shape[0]):
        owner = z
        contract[pl.ds(pl.multiple_of(2 * owner * slab, 16), 2 * slab), :] = join(
            first, mine[z, :, :width], other[z, :, :width], 0
        )
        for r in range(4):
            rows = slice(r * share, (r + 1) * share)
            both = join(first, mine[z, rows, width:], other[z, rows, width:], 0)
            at = pl.multiple_of((owner * 4 + (here[CHIP] ^ r)) * 2 * share, 16)
            expand[pl.ds(at, 2 * share), :] = both


def feed_kernel(
    ctx,
    here,
    length,
    task,
    mix_mine,
    mix_other,
    x1,
    gains,
    feed_mine,
    feed_other,
    cot,
    *refs,
):
    blocks, outs = refs[:-10], refs[-10:]
    place(here, blocks, [outs[0]], ctx)
    feed_step(
        here, length, task, mix_mine, mix_other, x1, gains, feed_mine, feed_other, cot, *outs
    )


def feed_step(
    here,
    length,
    task,
    mix_mine,
    mix_other,
    x1,
    gains,
    feed_mine,
    feed_other,
    cot,
    cross_out,
    x2,
    h3,
    active,
    low_out,
    grad_hidden,
    partial,
    part_out,
    expand,
    contract,
):
    first = here[CORE] == 0
    after_cross = x1[...] + dot(join(first, mix_mine[...], mix_other[...]), cross_out[...])
    x2[...] = after_cross
    unit, _ = rms_unit(after_cross)
    normed = (unit * gains[2:3, :]).astype(LOW)
    h3[...] = normed
    low = task_rows(length, task, cot).astype(LOW)
    low_out[...] = low
    feed_weights(here, feed_mine, feed_other, expand, contract)
    value, slope = gelu_parts(dot(normed, expand[...]))
    value = value.astype(LOW)
    grad = (dot_t(low, contract[...]) * slope).astype(LOW)
    active[...] = value
    grad_hidden[...] = grad
    partial[...] = dot_t(grad, half_of(first, expand[...], 0)).astype(LOW)
    part_out[...] = dot(value, half_of(first, contract[...])).astype(LOW)


def feed_grad_kernel(share, here, active, low_out, h3, grad_hidden, out, contract, expand):
    contract[...] = outer_sum(active[...], low_out[...])
    expand[...] = outer_sum(h3[...], grad_hidden[...])
    pb = out.shape[0]
    slab = contract.shape[0] // pb // 2
    block = expand.shape[0] // pb
    for z in range(pb):
        at = pl.multiple_of((2 * z + here[CORE]) * slab, 16)
        out[z, :slab] = contract[pl.ds(at, slab)].astype(LOW)
        rows = [
            expand[pl.ds(pl.multiple_of(z * block + at + here[CORE] * share, 8), share)]
            for at in range(0, block, 2 * share)
        ]
        out[z, slab:] = jnp.concatenate(rows, axis=0).astype(LOW)


def cross_back_kernel(
    here,
    length,
    task,
    sums_mine,
    sums_other,
    x2,
    gains,
    cot,
    cross_out,
    cq,
    memory,
    visible,
    stats,
    mix,
    dx2,
    low_cross,
    grad_cq,
    grad_mine,
    grad_other,
    gain_grad,
):
    first = here[CORE] == 0
    half = mix.shape[1]
    heads = half // HEAD
    pair = 2 * HEAD
    inverse = jnp.asarray(HEAD ** (-0.5), LOW)
    unit, factor = rms_unit(x2[...])
    grad = join(first, sums_mine[...], sums_other[...]).astype(FULL)
    gain_grad[...] = jnp.sum(grad * unit, axis=0, keepdims=True)
    back = task_rows(length, task, cot) + norm_back(grad, unit, factor, gains[2:3, :])
    dx2[...] = back
    low = back.astype(LOW)
    low_cross[...] = low
    grad_mix = dot_t(low, half_of(first, cross_out[...], 0)).astype(LOW)
    barred = jnp.where(visible[...] > 0, 0.0, MASKED)
    shares = 1.0 / stats[...]
    passage = grad_mine.shape[0]
    for g in range(heads // 2):
        at = g * pair
        q = both_heads(cq[:, at : at + pair] * inverse)
        do = both_heads(grad_mix[:, at : at + pair])
        k = memory[:, at : at + pair]
        v = memory[:, half + at : half + at + pair]
        mixed = mix[:, at : at + pair].astype(FULL)
        top, scale = [
            jnp.concatenate([a[:, c : c + 1], a[:, c + 3 : c + 4]], axis=0)
            for a, c in ((stats, 6 * g), (shares, 3 * heads + 6 * g))
        ]
        rho = jnp.sum(
            do.astype(FULL) * jnp.concatenate([mixed, mixed], axis=0), axis=-1, keepdims=True
        )
        prob = jnp.exp(dot_t(q, k) + barred - top) * scale
        grad_scores = (prob * (dot_t(do, v) - rho)).astype(LOW)
        grad_cq[:, at : at + pair] = (pick_rows(dot(grad_scores, k)) * HEAD ** (-0.5)).astype(LOW)
        keys = outer_sum(grad_scores, q).astype(LOW)
        values = outer_sum(prob.astype(LOW), do).astype(LOW)
        for ref, begin in ((grad_mine, 0), (grad_other, passage)):
            ref[:, at : at + pair] = keys[begin : begin + passage]
            ref[:, half + at : half + at + pair] = values[begin : begin + passage]


def memory_grad_kernel(pb, here, mine, other, grad_mine, grad_other, *refs):
    outs, whole = refs[:-1], refs[-1]
    whole[...] = outer_sum(mine[...], grad_mine[...]) + outer_sum(other[...], grad_other[...])
    share = whole.shape[0] // pb // len(outs)
    for r, out in enumerate(outs):
        chip = here[CHIP] ^ r
        for z in range(pb):
            at = pl.multiple_of((z * len(outs) + chip) * share, 16)
            out[z * share : (z + 1) * share] = whole[pl.ds(at, share)].astype(LOW)


def encoder_grad_kernel(here, mine, other, memory_in, grad):
    first = here[CORE] == 0
    half = mine.shape[1] // 2
    keys = join(first, mine[:, :half], other[:, :half])
    values = join(first, mine[:, half:], other[:, half:])
    grad[...] = dot_t(jnp.concatenate([keys, values], axis=1), memory_in[...]).astype(LOW)


def owned(left, choose):
    return dot(left, choose).astype(LOW)


def self_back_kernel(
    here,
    cq_mine,
    cq_other,
    cross_in,
    x1,
    gains,
    dx2,
    self_out,
    p1,
    probs,
    x,
    proj,
    gain_grad,
    low_self,
    grad_p1,
    grad_x,
    small,
):
    rows, width = x.shape
    heads = width // HEAD
    pair = 2 * HEAD
    inverse = jnp.asarray(HEAD ** (-0.5), LOW)
    grad = dot_t(join(here[CORE] == 0, cq_mine[...], cq_other[...]), cross_in[...])
    unit, factor = rms_unit(x1[...])
    small[...] = jnp.zeros_like(small)
    small[1:2, :] = jnp.sum(grad * unit, axis=0, keepdims=True)
    small[2:3, :] = gain_grad[...]
    dx1 = dx2[...] + norm_back(grad, unit, factor, gains[1:2, :])
    low = dx1.astype(LOW)
    low_self[...] = low
    row = lax.broadcasted_iota(jnp.int32, (rows, rows), 0)
    col = lax.broadcasted_iota(jnp.int32, (rows, rows), 1)
    flip = jnp.where(row + col == rows - 1, 1.0, 0.0).astype(LOW)
    grad_mix = dot_t(low, self_out[...]).astype(LOW)
    parts = [[], [], []]
    for g in range(heads // 2):
        at = g * pair
        q = both_heads(p1[:, at : at + pair] * inverse)
        k = p1[:, width + at : width + at + pair]
        v = p1[:, 2 * width + at : 2 * width + at + pair]
        do = both_heads(grad_mix[:, at : at + pair])
        prob = probs[g]
        grad_probs = dot_t(do, v)
        rho = jnp.sum(prob * grad_probs, axis=-1, keepdims=True)
        grad_scores = (prob * (grad_probs - rho)).astype(LOW)
        turned = dot(flip, jnp.concatenate([grad_scores[:rows], grad_scores[rows:]], axis=1))
        for side in range(2):
            part = turned[:, side * rows : (side + 1) * rows]
            part = pltpu.roll(part, 0, axis=1, stride=1, stride_axis=0)
            head = 3 + 2 * g + side
            small[head : head + 1, :rows] = jnp.sum(part, axis=0, keepdims=True)
        parts[0].append((pick_rows(dot(grad_scores, k)) * HEAD ** (-0.5)).astype(LOW))
        parts[1].append(outer_sum(grad_scores, q).astype(LOW))
        parts[2].append(outer_sum(prob.astype(LOW), do).astype(LOW))
    joined = jnp.concatenate(parts[0] + parts[1] + parts[2], axis=1)
    grad_p1[...] = joined
    grad = dot_t(joined, proj[...])
    unit, factor = rms_unit(x[...].astype(FULL))
    small[0:1, :] = jnp.sum(grad * unit, axis=0, keepdims=True)
    grad_x[...] = (dx1 + norm_back(grad, unit, factor, gains[0:1, :])).astype(LOW)


def feed_total_kernel(here, parts, contract, *refs):
    outs, rows = refs[:-1], refs[-1]
    total = tree([parts[z].astype(FULL) for z in range(parts.shape[0])])
    slab = contract.shape[0]
    contract[...] = total[:slab]
    rows[...] = total[slab:]
    share = outs[0].shape[0]
    for r, out in enumerate(outs):
        out[...] = rows[pl.ds(pl.multiple_of((here[CHIP] ^ r) * share, 8), share)].astype(LOW)


def expand_total_kernel(pb, here, *refs):
    parts, out = [ref[...].astype(FULL) for ref in refs[:-1]], refs[-1]
    step = 1
    while step < len(parts):
        flip = (here[CHIP] & step) != 0
        parts = [jnp.where(flip, parts[i ^ step], parts[i]) for i in range(len(parts))]
        step *= 2
    units = parts[0].shape[1] // pb
    out[...] = jnp.concatenate(
        [part[:, q * units : (q + 1) * units] for q in range(pb) for part in parts], axis=1
    )


def attention_grad_kernel(
    count,
    here,
    mix_mine,
    mix_other,
    low_cross,
    h2,
    cq_mine,
    cq_other,
    mix1,
    low_self,
    h1,
    grad_p1,
    small,
    *refs,
):
    pieces, out, choose, sums = refs[:count], *refs[count:]
    first = here[CORE] == 0
    pb = out.shape[0]
    width = mix1.shape[1]
    share = sums.shape[0] // pb
    lane = lax.broadcasted_iota(jnp.int32, choose.shape, 1)
    row = lax.broadcasted_iota(jnp.int32, choose.shape, 0)
    mine = lane // share * (width // pb) + here[CTX] * share + lane % share
    choose[...] = jnp.where(row == mine, 1.0, 0.0).astype(LOW)

    def owned(left, right):
        return outer_sum(dot(left, choose[...]).astype(LOW), right)

    sums[:, : 3 * width] = owned(h1[...], grad_p1[...])
    sums[:, 3 * width : 4 * width] = owned(mix1[...], low_self[...])
    cq = join(first, cq_mine[...], cq_other[...])
    sums[:, 4 * width : 5 * width] = owned(h2[...], cq)
    mix2 = join(first, mix_mine[...], mix_other[...])
    sums[:, 5 * width :] = owned(mix2, low_cross[...])
    total = tree([piece[...].astype(FULL) for piece in pieces])
    both = 2 * share
    for z in range(pb):
        rows = sums[z * share : (z + 1) * share]
        blocks = [rows[:, a : a + width] for a in range(0, 6 * width, width)]
        blocks += [total[z * both : (z + 1) * both], small[...]]
        out[z] = jnp.concatenate(blocks, axis=0).astype(LOW)


def attention_total_kernel(
    here, parts, hot, proj_grad, out_grad, query_grad, cross_grad, mine, other, gain_grad, table
):
    total = tree([parts[z].astype(FULL) for z in range(parts.shape[0])])
    first = here[CORE] == 0
    share, width = out_grad.shape
    blocks = [total[a : a + share] for a in range(0, 8 * share, share)]
    proj_grad[...] = jnp.concatenate(blocks[:3], axis=1)
    out_grad[...] = blocks[3]
    query_grad[...] = blocks[4]
    cross_grad[...] = blocks[5]
    mine[...] = jnp.where(first, blocks[6], blocks[7])
    other[...] = jnp.where(first, blocks[7], blocks[6])
    small = total[8 * share :]
    gains = gain_grad.shape[0]
    rows = hot.shape[1]
    shape = (width, share)
    place_of = lax.broadcasted_iota(jnp.int32, shape, 1) + (here[PB] * here[4] + here[CTX]) * share
    chosen = jnp.where(lax.broadcasted_iota(jnp.int32, shape, 0) == place_of, 1.0, 0.0)
    highest = lax.Precision.HIGHEST
    gain_grad[...] = jnp.dot(small, chosen, precision=highest, preferred_element_type=FULL)[:gains]
    heads = table.shape[0]
    whole = lax.dot_general(
        small[:, :rows],
        hot[...].astype(FULL),
        (((1,), (1,)), ((), ())),
        precision=highest,
        preferred_element_type=FULL,
    )
    table[...] = whole[gains : gains + heads]


def fast_body(
    decoder_in,
    encoder_out,
    self_projection,
    self_output,
    cross_query,
    cross_memory,
    cross_output,
    expand_weight,
    contract_weight,
    norm_gains,
    bias_table,
    bucket_index,
    passage_mask,
    target_length,
    task_group,
    cotangent,
):
    pb, ctx = lax.axis_size("pb"), lax.axis_size("ctx")
    mine_pb, mine_ctx = lax.axis_index("pb"), lax.axis_index("ctx")
    here = jnp.stack([mine_ctx & 1, mine_ctx >> 1, mine_pb, mine_ctx, jnp.int32(ctx)])
    here = here.astype(jnp.int32)
    rows, width = decoder_in.shape[1:]
    half = width // 2
    passage = encoder_out.shape[1]
    buckets, heads = bias_table.shape
    share = self_projection.shape[0]
    hidden = expand_weight.shape[1]
    slab = contract_weight.shape[0]
    units = pb * slab
    chips = ctx // 2
    x, e, cot = decoder_in[0], encoder_out[0], cotangent[0]

    (columns,) = call(
        prepare_kernel,
        [((share, 5 * width + 128), LOW)],
        [self_projection, self_output, cross_query, norm_gains],
    )
    along = first_hops(columns)
    far = jnp.stack(all_pb(columns)[1:])
    mixed = expand_weight.reshape(share, pb, chips, 2 * slab).transpose(2, 0, 1, 3)
    mixed = mixed.reshape(chips, share, 2 * units)
    chip = mine_ctx >> 1
    mixed = [lax.dynamic_index_in_dim(mixed, chip ^ r, 0, False) for r in range(chips)]
    mixed = jnp.concatenate([mixed[0]] + [swap_ctx(mixed[r], 2 * r) for r in range(1, chips)])
    e_other = swap_ctx(e, 1)
    visible = jnp.concatenate([passage_mask, swap_ctx(passage_mask, 1)], axis=1)
    others = jnp.concatenate([cross_memory, cross_output], axis=1)
    others_along = first_hops(after(others, along))
    far_along = first_hops(after(far, (e_other, visible, mixed, others_along)))
    proj_blocks, _ = gather_rows(columns, along, far, far_along)
    others_far = jnp.stack(all_pb(after(others, far))[1:])
    others_far_along = first_hops(after(others_far, far_along))
    others_blocks, last = gather_rows(others, others_along, others_far, others_far_along)
    x = after(x, others_far_along)
    feed = jnp.concatenate([contract_weight, mixed], axis=1)
    feed = jnp.broadcast_to(after(feed, others_far)[None], (pb,) + feed.shape)
    feed = exchange(feed, "pb")

    hot = (jnp.arange(buckets)[:, None] == bucket_index[::-1][None, :]).astype(LOW)
    table = outer_sum(bias_table, hot)

    proj, self_out, cross_in, gains, p1, probs, mix1, x1, h1, h2, cq = call(
        functools.partial(self_kernel, ctx),
        [
            ((width, 3 * width), LOW),
            ((width, width), LOW),
            ((width, width), LOW),
            ((norm_gains.shape[0], width), FULL),
            ((rows, 3 * width), LOW),
            ((heads // 2, 2 * rows, rows), FULL),
            ((rows, width), LOW),
            ((rows, width), FULL),
            ((rows, width), LOW),
            ((rows, width), LOW),
            ((rows, half), LOW),
        ],
        [here, target_length, x, table] + proj_blocks,
        scalars=2,
        scratch=[pltpu.VMEM((width, 128), LOW)],
        spare=5 * SPARE_BYTES,
    )
    def part(size, index):
        return [(b, b.shape[:2] + (size * width,), (0, 0, index)) for b in others_blocks]

    feed = after(feed, cq)
    feed_other = swap_ctx(feed, 1)
    memory_in, memory = call(
        functools.partial(memory_kernel, ctx),
        [((width, 2 * width), LOW), ((2 * passage, width), LOW)],
        [here, e, e_other] + part(2, 0),
        scalars=1,
    )
    (packed,) = call(cross_kernel, [((rows, half + 128), LOW)], [cq, memory, visible])
    mix2, stats = call(
        merge_kernel,
        [((rows, half), LOW), ((rows, 128), FULL)],
        [here] + all_chips(packed),
        scalars=1,
    )
    mix2_other = swap_ctx(mix2, 1)

    cross_out, x2, h3, active, low_out, grad_hidden, partial, part_out = call(
        functools.partial(feed_kernel, ctx),
        [
            ((width, width), LOW),
            ((rows, width), FULL),
            ((rows, width), LOW),
            ((rows, 2 * units), LOW),
            ((rows, width), LOW),
            ((rows, 2 * units), LOW),
            ((rows, half), LOW),
            ((rows, half), LOW),
        ],
        [
            here,
            target_length,
            task_group,
            mix2,
            mix2_other,
            x1,
            gains,
            feed,
            feed_other,
            cot,
        ]
        + part(1, 2),
        scalars=3,
        scratch=[pltpu.VMEM((width, 2 * units), LOW), pltpu.VMEM((2 * units, width), LOW)],
    )
    sums = sum_chips(partial)
    sums_other = swap_ctx(sums, 1)
    (feed_grads,) = call(
        functools.partial(feed_grad_kernel, share),
        [((pb, 2 * slab, width), LOW)],
        [here, active, low_out, h3, grad_hidden],
        scalars=1,
        scratch=[pltpu.VMEM((2 * units, width), FULL), pltpu.VMEM((width, 2 * units), FULL)],
    )
    feed_grads = exchange(feed_grads, "pb")

    dx2, low_cross, grad_cq, grad_mine, grad_other, gain_grad = call(
        cross_back_kernel,
        [
            ((rows, width), FULL),
            ((rows, width), LOW),
            ((rows, half), LOW),
            ((passage, width), LOW),
            ((passage, width), LOW),
            ((1, width), FULL),
        ],
        [
            here,
            target_length,
            task_group,
            sums,
            sums_other,
            x2,
            gains,
            cot,
            cross_out,
            cq,
            memory,
            visible,
            stats,
            mix2,
        ],
        scalars=3,
    )
    grad_cq = sum_chips(grad_cq)
    cq_other = swap_ctx(grad_cq, 1)
    pieces = call(
        functools.partial(memory_grad_kernel, pb),
        [((pb * 2 * share, width), LOW)] * chips,
        [here, e, e_other, grad_mine, grad_other],
        scalars=1,
        scratch=[pltpu.VMEM((width, width), FULL)],
    )
    pieces = [pieces[0]] + [swap_ctx(pieces[r], 2 * r) for r in range(1, chips)]
    memory_other = swap_ctx(grad_other, 1)

    low_self, grad_p1, grad_x, small = call(
        self_back_kernel,
        [
            ((rows, width), LOW),
            ((rows, 3 * width), LOW),
            ((rows, width), LOW),
            ((16, width), FULL),
        ],
        [
            here,
            grad_cq,
            cq_other,
            cross_in,
            x1,
            gains,
            dx2,
            self_out,
            p1,
            probs,
            x,
            proj,
            gain_grad,
        ],
        scalars=1,
    )

    (grads,) = call(
        functools.partial(attention_grad_kernel, chips),
        [((pb, 8 * share + 16, width), LOW)],
        [
            here,
            mix2,
            mix2_other,
            low_cross,
            h2,
            grad_cq,
            cq_other,
            mix1,
            low_self,
            h1,
            grad_p1,
            small,
        ]
        + pieces,
        scalars=1,
        scratch=[pltpu.VMEM((width, pb * share), LOW), pltpu.VMEM((pb * share, 6 * width), FULL)],
    )
    output = sum_chips(after(part_out, grads))
    grads = exchange(grads, "pb")
    (grad_encoder,) = call(
        encoder_grad_kernel,
        [((passage, width), LOW)],
        [here, after(grad_mine, grad_p1), memory_other, memory_in],
        scalars=1,
    )
    grad_contract, *expand_rows = call(
        feed_total_kernel,
        [((slab, width), FULL)] + [((share, 2 * units), LOW)] * chips,
        [here, after(feed_grads, grad_p1)],
        scalars=1,
        scratch=[pltpu.VMEM((chips * share, 2 * units), FULL)],
    )
    expand_rows = [expand_rows[0]] + [swap_ctx(expand_rows[r], 2 * r) for r in range(1, chips)]
    (grad_expand,) = call(
        functools.partial(expand_total_kernel, pb),
        [((share, hidden), FULL)],
        [here] + expand_rows,
        scalars=1,
    )
    first = (mine_ctx & 1) == 0
    block_output = (x2 + join(first, output, swap_ctx(output, 1)).astype(FULL)).astype(LOW)
    (
        grad_self_projection,
        grad_self_output,
        grad_cross_query,
        grad_cross_output,
        mine,
        other,
        grad_norm_gains,
        grad_table,
    ) = call(
        attention_total_kernel,
        [((share, 3 * width), FULL)]
        + [((share, width), FULL)] * 5
        + [(norm_gains.shape[:1] + (share,), FULL), ((heads, buckets), FULL)],
        [here, grads, hot],
        scalars=1,
    )
    other = swap_ctx(other, 1)
    grad_cross_memory = jnp.concatenate(
        [join(first, mine[:, :half], other[:, :half]), join(first, mine[:, half:], other[:, half:])],
        axis=1,
    )
    return (
        block_output[None],
        grad_x[None],
        grad_encoder[None],
        grad_self_projection,
        grad_self_output,
        grad_cross_query,
        grad_cross_memory,
        grad_cross_output,
        grad_expand,
        grad_contract,
        grad_norm_gains,
        grad_table.T,
    )


def body(*args):
    decoder_in, encoder_out, self_projection = args[:3]
    contract_weight = args[8]
    fits = (
        lax.axis_size("ctx") == 8
        and lax.axis_size("pb") == 4
        and decoder_in.shape[0] == 1
        and decoder_in.shape[1] == 128
        and self_projection.shape[0] % 8 == 0
        and contract_weight.shape[0] * 2 == self_projection.shape[0] * lax.axis_size("ctx")
        and encoder_out.shape[1] % 16 == 0
    )
    return (fast_body if fits else plain_body)(*args)


def solution(mesh):
    return jax.shard_map(
        body,
        mesh=mesh,
        in_specs=(
            P("pb", None, None),
            P("pb", "ctx", None),
            P(("pb", "ctx"), None),
            P(("pb", "ctx"), None),
            P(("pb", "ctx"), None),
            P(("pb", "ctx"), None),
            P(("pb", "ctx"), None),
            P(("pb", "ctx"), None),
            P(("pb", "ctx"), None),
            P(None, ("pb", "ctx")),
            P(),
            P(),
            P("pb", "ctx"),
            P("pb"),
            P("pb"),
            P("pb", None, None),
        ),
        out_specs=(
            P("pb", None, None),
            P("pb", None, None),
            P("pb", "ctx", None),
            P(("pb", "ctx"), None),
            P(("pb", "ctx"), None),
            P(("pb", "ctx"), None),
            P(("pb", "ctx"), None),
            P(("pb", "ctx"), None),
            P(("pb", "ctx"), None),
            P(("pb", "ctx"), None),
            P(None, ("pb", "ctx")),
            P(),
        ),
        check_vma=False,
    )
```

```python
import functools
import math

import jax
import jax.numpy as jnp
from jax import lax
from jax.experimental import pallas as pl
from jax.experimental.pallas import tpu as pltpu
from jax.sharding import PartitionSpec as P

LOW, FULL = jnp.bfloat16, jnp.float32
MASKED = -1000000000.0
EPS = 1e-06
HEAD = 64
ALL_BYTES = 58 * 1024 * 1024
SPARE_BYTES = 6 * 1024 * 1024


def dot(left, right, left_axis=1, right_axis=0):
    return lax.dot_general(
        left,
        right,
        (((left_axis,), (right_axis,)), ((), ())),
        preferred_element_type=FULL,
    )


def dot_t(left, right):
    return dot(left, right, 1, 1)


def outer_sum(left, right):
    return dot(left, right, 0, 0)


def rms_unit(values):
    factor = lax.rsqrt(jnp.mean(values * values, axis=-1, keepdims=True) + EPS)
    return values * factor, factor


def norm_back(grad, unit, factor, gain):
    scaled = grad * gain
    return factor * (scaled - unit * jnp.mean(scaled * unit, axis=-1, keepdims=True))


class Far:
    def __init__(self, array):
        self.array, self.shape, self.dtype = array, array.shape, array.dtype


class Arriving:
    def __init__(self, source, held, sem):
        self.held, self.shape, self.dtype = held, held.shape, held.dtype
        self.copy = pltpu.make_async_copy(source, held, sem)
        self.copy.start()

    def wait(self):
        if self.copy is not None:
            self.copy.wait()
            self.copy = None

    def __getitem__(self, index):
        self.wait()
        return self.held[index]


class Leaving:
    def __init__(self, held, target, sem):
        self.held, self.shape, self.dtype = held, held.shape, held.dtype
        self.copy = pltpu.make_async_copy(held, target, sem)
        self.left = False

    def leave(self):
        if not self.left:
            self.copy.start()
            self.left = True

    def __getitem__(self, index):
        return self.held[index]

    def __setitem__(self, index, values):
        self.held[index] = values


def place_of_device():
    mine_pb, mine_ctx = lax.axis_index("pb"), lax.axis_index("ctx")
    return mine_ctx & 1, mine_ctx >> 1, mine_pb, mine_ctx, lax.axis_size("ctx")


def call(kernel, outs, args, scalars=0, scratch=(), limit=None):
    placed = args[0] is None
    if placed:
        args, scalars = args[1:], scalars - 1
    arrays, specs, grid, held = [], [], (), []
    far_ins = [index for index, arg in enumerate(args) if isinstance(arg, Far)]
    far_outs = [index for index, out in enumerate(outs) if len(out) == 3]
    for index, arg in enumerate(args):
        if isinstance(arg, tuple):
            arg, shape, place = arg
            specs.append(pl.BlockSpec(shape, lambda i, place=place: place))
            grid = (1,)
            held.append((shape, arg.dtype))
        elif isinstance(arg, Far):
            specs.append(pl.BlockSpec(memory_space=pltpu.HBM))
            held.append((arg.shape, arg.dtype))
            arg = arg.array
        else:
            specs.append(pl.BlockSpec(memory_space=pltpu.SMEM if index < scalars else pltpu.VMEM))
            held.append((arg.shape, arg.dtype))
        arrays.append(arg)
    held += [out[:2] for out in outs] + [(one.shape, one.dtype) for one in scratch]
    size = sum(math.prod(shape) * jnp.dtype(dtype).itemsize for shape, dtype in held)
    buffers = [pltpu.VMEM(args[i].shape, args[i].dtype) for i in far_ins]
    buffers += [pltpu.VMEM(*outs[i][:2]) for i in far_outs]
    if buffers:
        buffers.append(pltpu.SemaphoreType.DMA((len(buffers),)))

    def run(*refs):
        ins, results = list(refs[: len(args)]), list(refs[len(args) : len(args) + len(outs)])
        rest = refs[len(args) + len(outs) :]
        own, extra = rest[: len(scratch)], rest[len(scratch) :]
        moved = []
        for k, i in enumerate(far_ins):
            ins[i] = Arriving(ins[i], extra[k], extra[-1].at[k])
            moved.append(ins[i])
        for k, i in enumerate(far_outs, len(far_ins)):
            results[i] = Leaving(extra[k], results[i], extra[-1].at[k])
            moved.append(results[i])
        kernel(*([place_of_device()] if placed else []), *ins, *results, *own)
        for one in moved:
            if isinstance(one, Leaving):
                one.leave()
                one.copy.wait()
            else:
                one.wait()

    return pl.pallas_call(
        run,
        grid=grid,
        out_shape=[jax.ShapeDtypeStruct(out[0], out[1]) for out in outs],
        in_specs=specs,
        out_specs=[
            pl.BlockSpec(memory_space=pltpu.HBM if len(out) == 3 else pltpu.VMEM) for out in outs
        ],
        scratch_shapes=list(scratch) + buffers,
        compiler_params=pltpu.CompilerParams(vmem_limit_bytes=limit or size + SPARE_BYTES),
    )(*arrays)


def to_low(values):
    return values.astype(jnp.bfloat16)


def normalize(values, scale):
    factor = lax.rsqrt(jnp.mean(values * values, axis=-1, keepdims=True) + 1e-06)
    return (values * factor * scale, values * factor, factor)


def gelu_tanh(values):
    return jax.nn.gelu(values, approximate=True)


def fetch(shards):
    return (
        lax.all_gather(shards[0], ("pb", "ctx"), axis=0, tiled=True),
        lax.all_gather(shards[1], ("pb", "ctx"), axis=0, tiled=True),
        lax.all_gather(shards[2], ("pb", "ctx"), axis=0, tiled=True),
        lax.all_gather(shards[3], ("pb", "ctx"), axis=0, tiled=True),
        lax.all_gather(shards[4], ("pb", "ctx"), axis=0, tiled=True),
        lax.all_gather(shards[5], ("pb", "ctx"), axis=0, tiled=True),
        lax.all_gather(shards[6], ("pb", "ctx"), axis=0, tiled=True),
        lax.all_gather(shards[7], ("pb", "ctx"), axis=1, tiled=True),
    )


def run_forward(params, decoder, encoder, allowed, visible, rel_bias):
    projection, self_out, cross_in, memory_in, cross_out, expand, contract, gains = params
    scale_gain = gains.astype(jnp.float32)
    count, length, width = decoder.shape
    heads = rel_bias.shape[0]
    head_dim = width // heads
    inverse = head_dim ** (-0.5)
    residual = decoder.astype(jnp.float32).reshape(count * length, width)
    normed_a, unit_a, factor_a = normalize(residual, scale_gain[0])
    normed_a = to_low(normed_a)
    joined = to_low(dot(normed_a, projection)).reshape(count, length, 3, heads, head_dim)
    query_rows, key_rows, value_rows = (joined[:, :, 0], joined[:, :, 1], joined[:, :, 2])
    self_scores = (
        jnp.einsum("nihd,njhd->nhij", query_rows, key_rows, preferred_element_type=jnp.float32)
        * inverse
        + rel_bias[None]
    )
    self_probs = jax.nn.softmax(jnp.where(allowed, self_scores, -1000000000.0), axis=-1)
    self_mixed = jnp.einsum(
        "nhij,njhd->nihd", to_low(self_probs), value_rows, preferred_element_type=jnp.float32
    )
    self_mix = to_low(self_mixed.reshape(count * length, width))
    after_self = residual + dot(self_mix, self_out)
    normed_b, unit_b, factor_b = normalize(after_self, scale_gain[1])
    normed_b = to_low(normed_b)
    cross_rows = to_low(dot(normed_b, cross_in)).reshape(count, length, heads, head_dim)
    ctx_rows = encoder.shape[1]
    memory = to_low(dot(encoder.reshape(count * ctx_rows, width), memory_in)).reshape(
        count, ctx_rows, 2, heads, head_dim
    )
    cross_keys, cross_vals = (memory[:, :, 0], memory[:, :, 1])
    cross_scores = (
        jnp.einsum("nihd,njhd->nhij", cross_rows, cross_keys, preferred_element_type=jnp.float32)
        * inverse
    )
    masked = jnp.where(visible, cross_scores, -1000000000.0)
    highest_score = lax.pmax(jnp.max(masked, axis=-1), "ctx")
    total = lax.psum(
        jnp.sum(jnp.where(visible, jnp.exp(masked - highest_score[..., None]), 0.0), axis=-1), "ctx"
    )
    cross_probs = (
        jnp.where(visible, jnp.exp(masked - highest_score[..., None]), 0.0) / total[..., None]
    )
    partial_mix = jnp.einsum(
        "nhij,njhd->nihd", to_low(cross_probs), cross_vals, preferred_element_type=jnp.float32
    )
    cross_mixed = lax.psum(partial_mix, "ctx")
    cross_mix = to_low(cross_mixed.reshape(count * length, width))
    after_cross = after_self + dot(cross_mix, cross_out)
    normed_c, unit_c, factor_c = normalize(after_cross, scale_gain[2])
    normed_c = to_low(normed_c)
    hidden = dot(normed_c, expand)
    active = to_low(gelu_tanh(hidden))
    output = after_cross + dot(active, contract)
    saved = (
        normed_a,
        unit_a,
        factor_a,
        query_rows,
        key_rows,
        value_rows,
        self_probs,
        self_mix,
        normed_b,
        unit_b,
        factor_b,
        cross_rows,
        cross_keys,
        cross_vals,
        cross_probs,
        cross_mix,
        normed_c,
        unit_c,
        factor_c,
        hidden,
        active,
        scale_gain,
    )
    return (output, saved)


def plain_body(
    decoder_in,
    encoder_out,
    self_projection,
    self_output,
    cross_query,
    cross_memory,
    cross_output,
    expand_weight,
    contract_weight,
    norm_gains,
    bias_table,
    bucket_index,
    passage_mask,
    target_length,
    task_group,
    cotangent,
):
    shards = (
        self_projection,
        self_output,
        cross_query,
        cross_memory,
        cross_output,
        expand_weight,
        contract_weight,
        norm_gains,
    )
    count, length, width = decoder_in.shape
    ctx_rows = encoder_out.shape[1]
    buckets, heads = bias_table.shape
    head_dim = width // heads
    inverse = head_dim ** (-0.5)
    positions = jnp.arange(length)
    offsets = jnp.clip(positions[:, None] - positions[None, :], 0, length - 1)
    pair_bucket = jnp.take(bucket_index, offsets.reshape(-1))
    one_hot = (pair_bucket[:, None] == jnp.arange(buckets)[None, :]).astype(jnp.bfloat16)
    rel_bias = dot(one_hot, bias_table).T.reshape(heads, length, length)
    causal = positions[None, :] <= positions[:, None]
    allowed = (causal[None] & (positions[None, None, :] < target_length[:, None, None]))[:, None]
    visible = (passage_mask > 0)[:, None, None, :]
    params = fetch(shards)
    output, saved = run_forward(params, decoder_in, encoder_out, allowed, visible, rel_bias)
    projection, self_out, cross_in, memory_in, cross_out, expand, contract, gains = params
    (
        normed_a,
        unit_a,
        factor_a,
        query_rows,
        key_rows,
        value_rows,
        self_probs,
        self_mix,
        normed_b,
        unit_b,
        factor_b,
        cross_rows,
        cross_keys,
        cross_vals,
        cross_probs,
        cross_mix,
        normed_c,
        unit_c,
        factor_c,
        hidden,
        active,
        scale_gain,
    ) = saved
    rows_total = count * length
    share = rows_total // lax.axis_size("ctx")
    start = lax.axis_index("ctx") * share

    def sliced(values):
        return lax.dynamic_slice_in_dim(values, start, share, 0)

    task_scale = jnp.where(task_group == 0, 1.0, jnp.where(task_group == 1, 0.5, 2.0)).astype(
        jnp.float32
    )
    row_live = (positions[None, :] < target_length[:, None]).astype(jnp.float32)
    grad_out = (
        cotangent.astype(jnp.float32) * (task_scale[:, None] * row_live)[:, :, None]
    ).reshape(rows_total, width)
    low_out = to_low(grad_out)
    grad_active = dot_t(low_out, contract)
    unused_value, gelu_pull = jax.vjp(gelu_tanh, hidden)
    grad_hidden = to_low(gelu_pull(grad_active)[0])
    grad_normed_c = dot_t(grad_hidden, expand)
    gain_c = jnp.sum(sliced(grad_normed_c * unit_c), axis=0)
    grad_after_cross = grad_out + norm_back(grad_normed_c, unit_c, factor_c, scale_gain[2])
    low_cross = to_low(grad_after_cross)
    grad_mix = to_low(dot_t(low_cross, cross_out)).reshape(count, length, heads, head_dim)
    grad_probs = jnp.einsum(
        "nihd,njhd->nhij", grad_mix, cross_vals, preferred_element_type=jnp.float32
    )
    row_dot = lax.psum(jnp.sum(grad_probs * cross_probs, axis=-1), "ctx")
    grad_scores = to_low(cross_probs * (grad_probs - row_dot[..., None]))
    partial_query = (
        jnp.einsum("nhij,njhd->nihd", grad_scores, cross_keys, preferred_element_type=jnp.float32)
        * inverse
    )
    grad_query = to_low(lax.psum(partial_query, "ctx")).reshape(rows_total, width)
    grad_key = (
        jnp.einsum("nhij,nihd->njhd", grad_scores, cross_rows, preferred_element_type=jnp.float32)
        * inverse
    )
    grad_value = jnp.einsum(
        "nhij,nihd->njhd", to_low(cross_probs), grad_mix, preferred_element_type=jnp.float32
    )
    grad_memory = to_low(jnp.stack([grad_key, grad_value], axis=2)).reshape(
        count * ctx_rows, 2 * width
    )
    encoder_rows = encoder_out.reshape(count * ctx_rows, width)
    grad_cross_memory = outer_sum(encoder_rows, grad_memory)
    grad_encoder = to_low(dot_t(grad_memory, memory_in)).reshape(count, ctx_rows, width)
    grad_normed_b = dot_t(grad_query, cross_in)
    gain_b = jnp.sum(sliced(grad_normed_b * unit_b), axis=0)
    grad_after_self = grad_after_cross + norm_back(grad_normed_b, unit_b, factor_b, scale_gain[1])
    low_self = to_low(grad_after_self)
    grad_self_mix = to_low(dot_t(low_self, self_out)).reshape(count, length, heads, head_dim)
    grad_probs_self = jnp.einsum(
        "nihd,njhd->nhij", grad_self_mix, value_rows, preferred_element_type=jnp.float32
    )
    self_dot = jnp.sum(grad_probs_self * self_probs, axis=-1, keepdims=True)
    grad_scores_self = to_low(self_probs * (grad_probs_self - self_dot))
    pair_grad = jnp.sum(grad_scores_self.astype(jnp.float32), axis=0).reshape(
        heads, length * length
    )
    pair_count = length * length // lax.axis_size("ctx")
    pair_start = lax.axis_index("ctx") * pair_count
    pair_slice = lax.dynamic_slice_in_dim(pair_grad, pair_start, pair_count, 1)
    hot_slice = lax.dynamic_slice_in_dim(one_hot.astype(jnp.float32), pair_start, pair_count, 0)
    table_term = lax.dot_general(
        hot_slice,
        pair_slice,
        (((0,), (1,)), ((), ())),
        precision=lax.Precision.HIGHEST,
        preferred_element_type=jnp.float32,
    )
    grad_table = lax.psum(table_term, ("pb", "ctx"))
    grad_q = (
        jnp.einsum(
            "nhij,njhd->nihd", grad_scores_self, key_rows, preferred_element_type=jnp.float32
        )
        * inverse
    )
    grad_k = (
        jnp.einsum(
            "nhij,nihd->njhd", grad_scores_self, query_rows, preferred_element_type=jnp.float32
        )
        * inverse
    )
    grad_v = jnp.einsum(
        "nhij,nihd->njhd", to_low(self_probs), grad_self_mix, preferred_element_type=jnp.float32
    )
    grad_joined = to_low(jnp.stack([grad_q, grad_k, grad_v], axis=2)).reshape(rows_total, 3 * width)
    grad_normed_a = dot_t(grad_joined, projection)
    gain_a = jnp.sum(sliced(grad_normed_a * unit_a), axis=0)
    grad_decoder = to_low(
        grad_after_self + norm_back(grad_normed_a, unit_a, factor_a, scale_gain[0])
    ).reshape(count, length, width)
    gain_grads = jnp.stack([gain_a, gain_b, gain_c])
    pairs = (
        (normed_a, grad_joined),
        (self_mix, low_self),
        (normed_b, grad_query),
        (cross_mix, low_cross),
        (normed_c, grad_hidden),
        (active, low_out),
    )
    partials = tuple((outer_sum(sliced(left), sliced(right)) for left, right in pairs))
    summed = (
        lax.psum_scatter(partials[0], ("pb", "ctx"), scatter_dimension=0, tiled=True),
        lax.psum_scatter(partials[1], ("pb", "ctx"), scatter_dimension=0, tiled=True),
        lax.psum_scatter(partials[2], ("pb", "ctx"), scatter_dimension=0, tiled=True),
        lax.psum_scatter(grad_cross_memory, ("pb", "ctx"), scatter_dimension=0, tiled=True),
        lax.psum_scatter(partials[3], ("pb", "ctx"), scatter_dimension=0, tiled=True),
        lax.psum_scatter(partials[4], ("pb", "ctx"), scatter_dimension=0, tiled=True),
        lax.psum_scatter(partials[5], ("pb", "ctx"), scatter_dimension=0, tiled=True),
        lax.psum_scatter(gain_grads, ("pb", "ctx"), scatter_dimension=1, tiled=True),
    )
    block_output = to_low(output).reshape(count, length, width)
    return (
        block_output,
        grad_decoder,
        grad_encoder,
        summed[0],
        summed[1],
        summed[2],
        summed[3],
        summed[4],
        summed[5],
        summed[6],
        summed[7],
        grad_table,
    )


def swap_ctx(values, mask):
    size = lax.axis_size("ctx")
    return lax.ppermute(values, "ctx", [(i, i ^ mask) for i in range(size)])


def swap_pb(values, mask):
    size = lax.axis_size("pb")
    return lax.ppermute(values, "pb", [(i, i ^ mask) for i in range(size)])


def exchange(values, axis):
    return lax.all_to_all(values, axis, 0, 0, tiled=True)


def all_pb(values):
    size = lax.axis_size("pb")
    return [values] + [swap_pb(values, r) for r in range(1, size)]


def after(values, earlier):
    return lax.optimization_barrier((values, earlier))[0]


def all_chips(values):
    return [values] + [swap_ctx(values, mask) for mask in range(2, lax.axis_size("ctx"), 2)]


def tree(terms):
    while len(terms) > 1:
        terms = [a + b for a, b in zip(terms[0::2], terms[1::2])]
    return terms[0]


def add_chips(parts):
    return tree([part.astype(FULL) for part in parts]).astype(LOW)


def to_owners(parts):
    return [parts[0]] + [swap_pb(part, r) for r, part in enumerate(parts) if r]


def pick(low, high):
    lanes = lax.broadcasted_iota(jnp.int32, low.shape, 1)
    return jnp.where(lanes < low.shape[1] // 2, low, high)


def lane_mask(values, side):
    zeros = jnp.zeros_like(values)
    return pick(values, zeros) if side == 0 else pick(zeros, values)


def both_heads(values):
    return jnp.concatenate([lane_mask(values, 0), lane_mask(values, 1)], axis=0)


def pick_rows(values):
    middle = values.shape[0] // 2
    return pick(values[:middle], values[middle:])


def join(first, mine, other, axis=1):
    return jnp.where(
        first,
        jnp.concatenate([mine, other], axis=axis),
        jnp.concatenate([other, mine], axis=axis),
    )


def half_of(first, values, axis=1):
    middle = values.shape[axis] // 2
    if axis == 0:
        return jnp.where(first, values[:middle], values[middle:])
    return jnp.where(first, values[:, :middle], values[:, middle:])


CORE, CHIP, PB, CTX = range(4)


def prepare_kernel(proj, self_out, cross_in, gains, out):
    count = gains.shape[0]
    row = lax.broadcasted_iota(jnp.int32, (count, 128), 0)
    lane = lax.broadcasted_iota(jnp.int32, (count, 128), 1)
    columns = outer_sum(gains[...], jnp.where(row == lane, 1.0, 0.0).astype(LOW)).astype(LOW)
    at = 0
    for part in (proj[...], self_out[...], cross_in[...], columns):
        out[:, at : at + part.shape[1]] = part
        at += part.shape[1]


def block_places(pb):
    middle = pb // 2
    return [
        [(0, 0), (0, 1), (0, 2)],
        [(r, 0) for r in range(1, pb)],
        [(r, 1) for r in range(1, pb)],
        [(r, 2) for r in range(1, pb)],
        [(r, 3) for r in range(middle)],
        [(r, 3) for r in range(middle, pb)],
    ]


def place(here, ins, outs, ctx):
    first = here[CORE] == 0
    pb = ins[2].shape[0] + 1
    rows = ins[0].shape[1]
    for i, places in enumerate(block_places(pb)):
        mine, other = ins[2 * i], ins[2 * i + 1]
        for k, (z, flip) in enumerate(places):
            both = join(first, mine[k], other[k], 0)
            owner = (z ^ here[PB]) * (ctx // 2) + (here[CHIP] ^ flip)
            slot = pl.multiple_of(owner * 2 * rows, 16)
            at = 0
            for out in outs:
                width = out.shape[1]
                out[pl.ds(slot, 2 * rows), :] = both[:, at : at + width]
                at += width


def first_hops(own):
    return swap_ctx(own, 2), swap_ctx(own, 4)


def gather_rows(own, along, far, far_along):
    middle = (far.shape[0] + 1) // 2
    low = jnp.concatenate([along[0][None], far_along[0][: middle - 1]])
    low = swap_ctx(low, 4)
    high = swap_ctx(far_along[1][middle - 1 :], 2)
    blocks = []
    for array in (jnp.stack([own, *along]), far, *far_along, low, high):
        blocks += [array, swap_ctx(array, 1)]
    return blocks, (low, high)


def self_kernel(ctx, here, length, x, table, *refs):
    blocks, refs = refs[:-12], refs[-12:]
    proj, self_out, cross_in, gains_out, p1, probs, mix, x1, h1, h2, cq, columns = refs
    rows, width = x.shape
    heads = width // HEAD
    pair = 2 * HEAD
    inverse = jnp.asarray(HEAD ** (-0.5), LOW)
    place(here, blocks, [proj, self_out, cross_in, columns], ctx)
    for one in (proj, self_out, cross_in):
        one.leave()
    gains = columns[...].astype(FULL).T
    gains_out[...] = gains[: gains_out.shape[0]]
    xf = x[...].astype(FULL)
    unit, _ = rms_unit(xf)
    normed = (unit * gains[0:1, :]).astype(LOW)
    h1[...] = normed
    joined = dot(normed, proj[...]).astype(LOW)
    p1[...] = joined
    p1.leave()
    row = lax.broadcasted_iota(jnp.int32, (rows, rows), 0)
    col = lax.broadcasted_iota(jnp.int32, (rows, rows), 1)
    allowed = (col <= row) & (col < length[0])
    barred = jnp.where(allowed, 0.0, MASKED)
    mixes = []
    for g in range(heads // 2):
        at = g * pair
        q = both_heads(joined[:, at : at + pair] * inverse)
        k = joined[:, width + at : width + at + pair]
        v = joined[:, 2 * width + at : 2 * width + at + pair]
        bias = [
            pltpu.roll(
                jnp.broadcast_to(table[head : head + 1, :], (rows, rows)),
                1,
                axis=1,
                stride=1,
                stride_axis=0,
            )
            + barred
            for head in (2 * g, 2 * g + 1)
        ]
        scores = dot_t(q, k) + jnp.concatenate(bias, axis=0)
        powers = jnp.exp(scores - jnp.max(scores, axis=-1, keepdims=True))
        prob = powers * (1.0 / jnp.sum(powers, axis=-1, keepdims=True))
        probs[g] = prob
        mixes.append(pick_rows(dot(prob.astype(LOW), v)).astype(LOW))
    probs.leave()
    mixes = jnp.concatenate(mixes, axis=1)
    mix[...] = mixes
    after_self = xf + dot(mixes, self_out[...])
    x1[...] = after_self
    unit, _ = rms_unit(after_self)
    normed = (unit * gains[1:2, :]).astype(LOW)
    h2[...] = normed
    cq[...] = dot(normed, half_of(here[CORE] == 0, cross_in[...])).astype(LOW)


def memory_kernel(ctx, here, mine, other, *refs):
    blocks, (memory_in, memory) = refs[:-2], refs[-2:]
    place(here, blocks, [memory_in], ctx)
    memory_in.leave()
    first = here[CORE] == 0
    width = mine.shape[1]
    keys = half_of(first, memory_in[:, :width])
    values = half_of(first, memory_in[:, width:])
    weight = jnp.concatenate([keys, values], axis=1)
    rows = mine.shape[0]
    memory[:rows] = dot(mine[...], weight).astype(LOW)
    memory[rows:] = dot(other[...], weight).astype(LOW)


def pack_stats(tops, totals):
    rows = tops[0].shape[0]
    lanes = lax.broadcasted_iota(jnp.int32, (rows, 128), 1)
    columns = jnp.zeros((rows, 128), FULL)
    for index, column in enumerate(tops + totals):
        columns = jnp.where(lanes // 3 == index, column, columns)
    high = columns.astype(LOW).astype(FULL)
    middle = (columns - high).astype(LOW).astype(FULL)
    kind = lanes % 3
    return jnp.where(kind == 0, high, jnp.where(kind == 1, middle, columns - high - middle)).astype(
        LOW
    )


def read_stats(packed):
    values = packed.astype(FULL)
    return values + pltpu.roll(values, 127, axis=1) + pltpu.roll(values, 126, axis=1)


def cross_kernel(cq, memory, visible, packed):
    rows, half = cq.shape
    pair = 2 * HEAD
    inverse = jnp.asarray(HEAD ** (-0.5), LOW)
    barred = jnp.where(visible[...] > 0, 0.0, MASKED)
    tops, totals, mixes = [], [], []
    for at in range(0, half, pair):
        q = both_heads(cq[:, at : at + pair] * inverse)
        k = memory[:, at : at + pair]
        v = memory[:, half + at : half + at + pair]
        scores = dot_t(q, k) + barred
        top = jnp.max(scores, axis=-1, keepdims=True)
        powers = jnp.exp(scores - top)
        total = jnp.sum(powers, axis=-1, keepdims=True)
        tops += [top[:rows], top[rows:]]
        totals += [total[:rows], total[rows:]]
        mixes.append(pick_rows(dot(powers.astype(LOW), v)).astype(LOW))
    packed[...] = jnp.concatenate(mixes + [pack_stats(tops, totals)], axis=1)


def spread(columns):
    shape = (columns[0].shape[0], 2 * HEAD)
    return jnp.concatenate(
        [
            pick(jnp.broadcast_to(a, shape), jnp.broadcast_to(b, shape))
            for a, b in zip(columns[0::2], columns[1::2])
        ],
        axis=1,
    )


def merge_kernel(here, *refs):
    ins, mix, stats = refs[:-2], refs[-2], refs[-1]
    half = mix.shape[1]
    heads = half // HEAD
    packed = [ref[...] for ref in ins]
    step = 1
    while step < len(packed):
        flip = (here[CHIP] & step) != 0
        packed = [jnp.where(flip, packed[i ^ step], packed[i]) for i in range(len(packed))]
        step *= 2
    read = [read_stats(p[:, half:]) for p in packed]
    top = read[0]
    for other in read[1:]:
        top = jnp.maximum(top, other)
    lanes = lax.broadcasted_iota(jnp.int32, top.shape, 1)
    is_top = lanes < 3 * heads
    scales = [jnp.exp(jnp.where(is_top, r - top, 0.0)) for r in read]
    total = tree([r * pltpu.roll(w, 3 * heads, axis=1) for r, w in zip(read, scales)])
    share = 1.0 / pltpu.roll(total, 128 - 3 * heads, axis=1)
    weights = [w * share for w in scales]
    terms = [
        p[:, :half].astype(FULL) * spread([w[:, 3 * h : 3 * h + 1] for h in range(heads)])
        for p, w in zip(packed, weights)
    ]
    mix[...] = tree(terms).astype(LOW)
    stats[...] = jnp.where(is_top, top, total)


def gelu_parts(values):
    slope = (2.0 / jnp.pi) ** 0.5
    square = values * values
    bent = jnp.tanh(slope * (values + 0.044715 * values * square))
    active = 0.5 * values * (1.0 + bent)
    inner = slope * (1.0 + 3 * 0.044715 * square)
    return active, 0.5 * (1.0 + bent) + 0.5 * values * (1.0 - bent * bent) * inner


def task_rows(length, task, cot):
    rows = lax.broadcasted_iota(jnp.int32, cot.shape, 0)
    weight = jnp.where(task[0] == 0, 1.0, jnp.where(task[0] == 1, 0.5, 2.0)).astype(FULL)
    return jnp.where(rows < length[0], cot[...].astype(FULL) * weight, 0.0)


def feed_weights(here, mine, other, expand, contract):
    first = here[CORE] == 0
    width = contract.shape[1]
    slab = mine.shape[1]
    share = slab // 4
    for z in range(mine.shape[0]):
        owner = z
        contract[pl.ds(pl.multiple_of(2 * owner * slab, 16), 2 * slab), :] = join(
            first, mine[z, :, :width], other[z, :, :width], 0
        )
        for r in range(4):
            rows = slice(r * share, (r + 1) * share)
            both = join(first, mine[z, rows, width:], other[z, rows, width:], 0)
            at = pl.multiple_of((owner * 4 + (here[CHIP] ^ r)) * 2 * share, 16)
            expand[pl.ds(at, 2 * share), :] = both


def feed_kernel(
    ctx,
    here,
    length,
    task,
    mix_mine,
    mix_other,
    x1,
    gains,
    feed_mine,
    feed_other,
    cot,
    *refs,
):
    blocks, outs = refs[:-10], refs[-10:]
    place(here, blocks, [outs[0]], ctx)
    outs[0].leave()
    feed_step(
        here, length, task, mix_mine, mix_other, x1, gains, feed_mine, feed_other, cot, *outs
    )


def feed_step(
    here,
    length,
    task,
    mix_mine,
    mix_other,
    x1,
    gains,
    feed_mine,
    feed_other,
    cot,
    cross_out,
    x2,
    h3,
    active,
    low_out,
    grad_hidden,
    partial,
    part_out,
    expand,
    contract,
):
    first = here[CORE] == 0
    after_cross = x1[...] + dot(join(first, mix_mine[...], mix_other[...]), cross_out[...])
    x2[...] = after_cross
    x2.leave()
    unit, _ = rms_unit(after_cross)
    normed = (unit * gains[2:3, :]).astype(LOW)
    h3[...] = normed
    low = task_rows(length, task, cot).astype(LOW)
    low_out[...] = low
    feed_weights(here, feed_mine, feed_other, expand, contract)
    value, slope = gelu_parts(dot(normed, expand[...]))
    value = value.astype(LOW)
    grad = (dot_t(low, contract[...]) * slope).astype(LOW)
    active[...] = value
    grad_hidden[...] = grad
    partial[...] = dot_t(grad, half_of(first, expand[...], 0)).astype(LOW)
    part_out[...] = dot(value, half_of(first, contract[...])).astype(LOW)


def feed_grad_kernel(share, here, active, low_out, h3, grad_hidden, out, contract, expand):
    contract[...] = outer_sum(active[...], low_out[...])
    expand[...] = outer_sum(h3[...], grad_hidden[...])
    pb = out.shape[0]
    slab = contract.shape[0] // pb // 2
    block = expand.shape[0] // pb
    for z in range(pb):
        at = pl.multiple_of((2 * z + here[CORE]) * slab, 16)
        out[z, :slab] = contract[pl.ds(at, slab)].astype(LOW)
        rows = [
            expand[pl.ds(pl.multiple_of(z * block + at + here[CORE] * share, 8), share)]
            for at in range(0, block, 2 * share)
        ]
        out[z, slab:] = jnp.concatenate(rows, axis=0).astype(LOW)


def cross_back_kernel(
    here,
    length,
    task,
    sums_mine,
    sums_other,
    x2,
    gains,
    cot,
    cross_out,
    cq,
    memory,
    visible,
    stats,
    mix,
    dx2,
    low_cross,
    grad_cq,
    grad_mine,
    grad_other,
    gain_grad,
):
    first = here[CORE] == 0
    half = mix.shape[1]
    heads = half // HEAD
    pair = 2 * HEAD
    inverse = jnp.asarray(HEAD ** (-0.5), LOW)
    unit, factor = rms_unit(x2[...])
    grad = join(first, sums_mine[...], sums_other[...]).astype(FULL)
    gain_grad[...] = jnp.sum(grad * unit, axis=0, keepdims=True)
    back = task_rows(length, task, cot) + norm_back(grad, unit, factor, gains[2:3, :])
    dx2[...] = back
    low = back.astype(LOW)
    low_cross[...] = low
    grad_mix = dot_t(low, half_of(first, cross_out[...], 0)).astype(LOW)
    barred = jnp.where(visible[...] > 0, 0.0, MASKED)
    shares = 1.0 / stats[...]
    passage = grad_mine.shape[0]
    for g in range(heads // 2):
        at = g * pair
        q = both_heads(cq[:, at : at + pair] * inverse)
        do = both_heads(grad_mix[:, at : at + pair])
        k = memory[:, at : at + pair]
        v = memory[:, half + at : half + at + pair]
        mixed = mix[:, at : at + pair].astype(FULL)
        top, scale = [
            jnp.concatenate([a[:, c : c + 1], a[:, c + 3 : c + 4]], axis=0)
            for a, c in ((stats, 6 * g), (shares, 3 * heads + 6 * g))
        ]
        rho = jnp.sum(
            do.astype(FULL) * jnp.concatenate([mixed, mixed], axis=0), axis=-1, keepdims=True
        )
        prob = jnp.exp(dot_t(q, k) + barred - top) * scale
        grad_scores = (prob * (dot_t(do, v) - rho)).astype(LOW)
        grad_cq[:, at : at + pair] = (pick_rows(dot(grad_scores, k)) * HEAD ** (-0.5)).astype(LOW)
        keys = outer_sum(grad_scores, q).astype(LOW)
        values = outer_sum(prob.astype(LOW), do).astype(LOW)
        for ref, begin in ((grad_mine, 0), (grad_other, passage)):
            ref[:, at : at + pair] = keys[begin : begin + passage]
            ref[:, half + at : half + at + pair] = values[begin : begin + passage]


def memory_grad_kernel(pb, here, mine, other, grad_mine, grad_other, *refs):
    outs, whole = refs[:-1], refs[-1]
    whole[...] = outer_sum(mine[...], grad_mine[...]) + outer_sum(other[...], grad_other[...])
    share = whole.shape[0] // pb // len(outs)
    for r, out in enumerate(outs):
        chip = here[CHIP] ^ r
        for z in range(pb):
            at = pl.multiple_of((z * len(outs) + chip) * share, 16)
            out[z * share : (z + 1) * share] = whole[pl.ds(at, share)].astype(LOW)


def encoder_grad_kernel(here, mine, other, memory_in, grad):
    first = here[CORE] == 0
    half = mine.shape[1] // 2
    keys = join(first, mine[:, :half], other[:, :half])
    values = join(first, mine[:, half:], other[:, half:])
    grad[...] = dot_t(jnp.concatenate([keys, values], axis=1), memory_in[...]).astype(LOW)


def owned(left, choose):
    return dot(left, choose).astype(LOW)


def self_back_kernel(
    here,
    cq_mine,
    cq_other,
    cross_in,
    x1,
    gains,
    dx2,
    self_out,
    p1,
    probs,
    x,
    proj,
    gain_grad,
    low_self,
    grad_p1,
    grad_x,
    small,
):
    rows, width = x.shape
    heads = width // HEAD
    pair = 2 * HEAD
    inverse = jnp.asarray(HEAD ** (-0.5), LOW)
    grad = dot_t(join(here[CORE] == 0, cq_mine[...], cq_other[...]), cross_in[...])
    unit, factor = rms_unit(x1[...])
    small[...] = jnp.zeros_like(small)
    small[1:2, :] = jnp.sum(grad * unit, axis=0, keepdims=True)
    small[2:3, :] = gain_grad[...]
    dx1 = dx2[...] + norm_back(grad, unit, factor, gains[1:2, :])
    low = dx1.astype(LOW)
    low_self[...] = low
    row = lax.broadcasted_iota(jnp.int32, (rows, rows), 0)
    col = lax.broadcasted_iota(jnp.int32, (rows, rows), 1)
    flip = jnp.where(row + col == rows - 1, 1.0, 0.0).astype(LOW)
    grad_mix = dot_t(low, self_out[...]).astype(LOW)
    parts = [[], [], []]
    for g in range(heads // 2):
        at = g * pair
        q = both_heads(p1[:, at : at + pair] * inverse)
        k = p1[:, width + at : width + at + pair]
        v = p1[:, 2 * width + at : 2 * width + at + pair]
        do = both_heads(grad_mix[:, at : at + pair])
        prob = probs[g]
        grad_probs = dot_t(do, v)
        rho = jnp.sum(prob * grad_probs, axis=-1, keepdims=True)
        grad_scores = (prob * (grad_probs - rho)).astype(LOW)
        turned = dot(flip, jnp.concatenate([grad_scores[:rows], grad_scores[rows:]], axis=1))
        for side in range(2):
            part = turned[:, side * rows : (side + 1) * rows]
            part = pltpu.roll(part, 0, axis=1, stride=1, stride_axis=0)
            head = 3 + 2 * g + side
            small[head : head + 1, :rows] = jnp.sum(part, axis=0, keepdims=True)
        parts[0].append((pick_rows(dot(grad_scores, k)) * HEAD ** (-0.5)).astype(LOW))
        parts[1].append(outer_sum(grad_scores, q).astype(LOW))
        parts[2].append(outer_sum(prob.astype(LOW), do).astype(LOW))
    joined = jnp.concatenate(parts[0] + parts[1] + parts[2], axis=1)
    grad_p1[...] = joined
    grad = dot_t(joined, proj[...])
    unit, factor = rms_unit(x[...].astype(FULL))
    small[0:1, :] = jnp.sum(grad * unit, axis=0, keepdims=True)
    grad_x[...] = (dx1 + norm_back(grad, unit, factor, gains[0:1, :])).astype(LOW)


def feed_total_kernel(here, parts, contract, *refs):
    outs, rows = refs[:-1], refs[-1]
    total = tree([parts[z].astype(FULL) for z in range(parts.shape[0])])
    slab = contract.shape[0]
    contract[...] = total[:slab]
    rows[...] = total[slab:]
    share = outs[0].shape[0]
    for r, out in enumerate(outs):
        out[...] = rows[pl.ds(pl.multiple_of((here[CHIP] ^ r) * share, 8), share)].astype(LOW)


def expand_total_kernel(pb, here, *refs):
    parts, out = [ref[...].astype(FULL) for ref in refs[:-1]], refs[-1]
    step = 1
    while step < len(parts):
        flip = (here[CHIP] & step) != 0
        parts = [jnp.where(flip, parts[i ^ step], parts[i]) for i in range(len(parts))]
        step *= 2
    units = parts[0].shape[1] // pb
    out[...] = jnp.concatenate(
        [part[:, q * units : (q + 1) * units] for q in range(pb) for part in parts], axis=1
    )


def attention_grad_kernel(
    count,
    here,
    mix_mine,
    mix_other,
    low_cross,
    h2,
    cq_mine,
    cq_other,
    mix1,
    low_self,
    h1,
    grad_p1,
    small,
    *refs,
):
    pieces, out, choose, sums = refs[:count], *refs[count:]
    first = here[CORE] == 0
    pb = out.shape[0]
    width = mix1.shape[1]
    share = sums.shape[0] // pb
    lane = lax.broadcasted_iota(jnp.int32, choose.shape, 1)
    row = lax.broadcasted_iota(jnp.int32, choose.shape, 0)
    mine = lane // share * (width // pb) + here[CTX] * share + lane % share
    choose[...] = jnp.where(row == mine, 1.0, 0.0).astype(LOW)

    def owned(left, right):
        return outer_sum(dot(left, choose[...]).astype(LOW), right)

    sums[:, : 3 * width] = owned(h1[...], grad_p1[...])
    sums[:, 3 * width : 4 * width] = owned(mix1[...], low_self[...])
    cq = join(first, cq_mine[...], cq_other[...])
    sums[:, 4 * width : 5 * width] = owned(h2[...], cq)
    mix2 = join(first, mix_mine[...], mix_other[...])
    sums[:, 5 * width :] = owned(mix2, low_cross[...])
    total = tree([piece[...].astype(FULL) for piece in pieces])
    both = 2 * share
    for z in range(pb):
        rows = sums[z * share : (z + 1) * share]
        blocks = [rows[:, a : a + width] for a in range(0, 6 * width, width)]
        blocks += [total[z * both : (z + 1) * both], small[...]]
        out[z] = jnp.concatenate(blocks, axis=0).astype(LOW)


def attention_total_kernel(
    here, parts, hot, proj_grad, out_grad, query_grad, cross_grad, mine, other, gain_grad, table
):
    total = tree([parts[z].astype(FULL) for z in range(parts.shape[0])])
    first = here[CORE] == 0
    share, width = out_grad.shape
    blocks = [total[a : a + share] for a in range(0, 8 * share, share)]
    proj_grad[...] = jnp.concatenate(blocks[:3], axis=1)
    out_grad[...] = blocks[3]
    query_grad[...] = blocks[4]
    cross_grad[...] = blocks[5]
    mine[...] = jnp.where(first, blocks[6], blocks[7])
    other[...] = jnp.where(first, blocks[7], blocks[6])
    small = total[8 * share :]
    gains = gain_grad.shape[0]
    rows = hot.shape[1]
    shape = (width, share)
    place_of = lax.broadcasted_iota(jnp.int32, shape, 1) + (here[PB] * here[4] + here[CTX]) * share
    chosen = jnp.where(lax.broadcasted_iota(jnp.int32, shape, 0) == place_of, 1.0, 0.0)
    highest = lax.Precision.HIGHEST
    gain_grad[...] = jnp.dot(small, chosen, precision=highest, preferred_element_type=FULL)[:gains]
    heads = table.shape[0]
    whole = lax.dot_general(
        small[:, :rows],
        hot[...].astype(FULL),
        (((1,), (1,)), ((), ())),
        precision=highest,
        preferred_element_type=FULL,
    )
    table[...] = whole[gains : gains + heads]


def fast_body(
    decoder_in,
    encoder_out,
    self_projection,
    self_output,
    cross_query,
    cross_memory,
    cross_output,
    expand_weight,
    contract_weight,
    norm_gains,
    bias_table,
    bucket_index,
    passage_mask,
    target_length,
    task_group,
    cotangent,
):
    pb, ctx = lax.axis_size("pb"), lax.axis_size("ctx")
    mine_pb, mine_ctx = lax.axis_index("pb"), lax.axis_index("ctx")
    here = None
    rows, width = decoder_in.shape[1:]
    half = width // 2
    passage = encoder_out.shape[1]
    buckets, heads = bias_table.shape
    share = self_projection.shape[0]
    hidden = expand_weight.shape[1]
    slab = contract_weight.shape[0]
    units = pb * slab
    chips = ctx // 2
    x, e, cot = decoder_in[0], encoder_out[0], cotangent[0]

    (columns,) = call(
        prepare_kernel,
        [((share, 5 * width + 128), LOW)],
        [self_projection, self_output, cross_query, norm_gains],
    )
    along = first_hops(columns)
    far = jnp.stack(all_pb(columns)[1:])
    mixed = expand_weight.reshape(share, pb, chips, 2 * slab).transpose(2, 0, 1, 3)
    mixed = mixed.reshape(chips, share, 2 * units)
    chip = mine_ctx >> 1
    mixed = [lax.dynamic_index_in_dim(mixed, chip ^ r, 0, False) for r in range(chips)]
    mixed = jnp.concatenate([mixed[0]] + [swap_ctx(mixed[r], 2 * r) for r in range(1, chips)])
    e_other = swap_ctx(e, 1)
    visible = jnp.concatenate([passage_mask, swap_ctx(passage_mask, 1)], axis=1)
    others = jnp.concatenate([cross_memory, cross_output], axis=1)
    others_along = first_hops(after(others, along))
    far_along = first_hops(after(far, (e_other, visible, mixed, others_along)))
    proj_blocks, _ = gather_rows(columns, along, far, far_along)
    others_far = jnp.stack(all_pb(after(others, far))[1:])
    others_far_along = first_hops(after(others_far, far_along))
    others_blocks, last = gather_rows(others, others_along, others_far, others_far_along)
    x = after(x, others_far_along)
    feed = jnp.concatenate([contract_weight, mixed], axis=1)
    feed = jnp.broadcast_to(after(feed, others_far)[None], (pb,) + feed.shape)
    feed = exchange(feed, "pb")

    hot = (jnp.arange(buckets)[:, None] == bucket_index[::-1][None, :]).astype(LOW)
    table = outer_sum(bias_table, hot)

    proj, self_out, cross_in, gains, p1, probs, mix1, x1, h1, h2, cq = call(
        functools.partial(self_kernel, ctx),
        [
            ((width, 3 * width), LOW, True),
            ((width, width), LOW, True),
            ((width, width), LOW, True),
            ((norm_gains.shape[0], width), FULL),
            ((rows, 3 * width), LOW, True),
            ((heads // 2, 2 * rows, rows), FULL, True),
            ((rows, width), LOW),
            ((rows, width), FULL),
            ((rows, width), LOW),
            ((rows, width), LOW),
            ((rows, half), LOW),
        ],
        [here, target_length, x, table] + proj_blocks,
        scalars=2,
        scratch=[pltpu.VMEM((width, 128), LOW)],
        limit=ALL_BYTES,
    )
    def part(size, index):
        return [(b, b.shape[:2] + (size * width,), (0, 0, index)) for b in others_blocks]

    feed = after(feed, cq)
    feed_other = swap_ctx(feed, 1)
    memory_in, memory = call(
        functools.partial(memory_kernel, ctx),
        [((width, 2 * width), LOW, True), ((2 * passage, width), LOW)],
        [here, e, e_other] + part(2, 0),
        scalars=1,
    )
    (packed,) = call(cross_kernel, [((rows, half + 128), LOW)], [cq, memory, visible])
    mix2, stats = call(
        merge_kernel,
        [((rows, half), LOW), ((rows, 128), FULL)],
        [here] + all_chips(packed),
        scalars=1,
    )
    mix2_other = swap_ctx(mix2, 1)

    cross_out, x2, h3, active, low_out, grad_hidden, partial, part_out = call(
        functools.partial(feed_kernel, ctx),
        [
            ((width, width), LOW, True),
            ((rows, width), FULL, True),
            ((rows, width), LOW),
            ((rows, 2 * units), LOW),
            ((rows, width), LOW),
            ((rows, 2 * units), LOW),
            ((rows, half), LOW),
            ((rows, half), LOW),
        ],
        [
            here,
            target_length,
            task_group,
            mix2,
            mix2_other,
            x1,
            gains,
            feed,
            feed_other,
            cot,
        ]
        + part(1, 2),
        scalars=3,
        scratch=[pltpu.VMEM((width, 2 * units), LOW), pltpu.VMEM((2 * units, width), LOW)],
    )
    partials = all_chips(partial)
    sums = add_chips(partials)
    sums_other = swap_ctx(sums, 1)
    (feed_grads,) = call(
        functools.partial(feed_grad_kernel, share),
        [((pb, 2 * slab, width), LOW)],
        [here, after(active, partials), low_out, h3, grad_hidden],
        scalars=1,
        scratch=[pltpu.VMEM((2 * units, width), FULL), pltpu.VMEM((width, 2 * units), FULL)],
    )
    feed_grads = exchange(feed_grads, "pb")

    dx2, low_cross, grad_cq, grad_mine, grad_other, gain_grad = call(
        cross_back_kernel,
        [
            ((rows, width), FULL),
            ((rows, width), LOW),
            ((rows, half), LOW),
            ((passage, width), LOW),
            ((passage, width), LOW),
            ((1, width), FULL),
        ],
        [
            here,
            target_length,
            task_group,
            sums,
            sums_other,
            Far(x2),
            gains,
            cot,
            Far(cross_out),
            cq,
            memory,
            visible,
            stats,
            mix2,
        ],
        scalars=3,
    )
    grad_cq = add_chips(all_chips(grad_cq))
    cq_other = swap_ctx(grad_cq, 1)
    pieces = call(
        functools.partial(memory_grad_kernel, pb),
        [((pb * 2 * share, width), LOW)] * chips,
        [here, e, e_other, grad_mine, grad_other],
        scalars=1,
        scratch=[pltpu.VMEM((width, width), FULL)],
    )
    pieces = [pieces[0]] + [swap_ctx(pieces[r], 2 * r) for r in range(1, chips)]
    memory_other = swap_ctx(grad_other, 1)

    low_self, grad_p1, grad_x, small = call(
        self_back_kernel,
        [
            ((rows, width), LOW),
            ((rows, 3 * width), LOW),
            ((rows, width), LOW),
            ((16, width), FULL),
        ],
        [
            here,
            grad_cq,
            cq_other,
            Far(cross_in),
            x1,
            gains,
            dx2,
            Far(self_out),
            Far(p1),
            Far(probs),
            x,
            Far(proj),
            gain_grad,
        ],
        scalars=1,
    )

    (grads,) = call(
        functools.partial(attention_grad_kernel, chips),
        [((pb, 8 * share + 16, width), LOW)],
        [
            here,
            mix2,
            mix2_other,
            low_cross,
            h2,
            grad_cq,
            cq_other,
            mix1,
            low_self,
            h1,
            grad_p1,
            small,
        ]
        + pieces,
        scalars=1,
        scratch=[pltpu.VMEM((width, pb * share), LOW), pltpu.VMEM((pb * share, 6 * width), FULL)],
    )
    output = add_chips(all_chips(after(part_out, grads)))
    grads = exchange(grads, "pb")
    (grad_encoder,) = call(
        encoder_grad_kernel,
        [((passage, width), LOW)],
        [here, after(grad_mine, grad_p1), memory_other, Far(memory_in)],
        scalars=1,
    )
    grad_contract, *expand_rows = call(
        feed_total_kernel,
        [((slab, width), FULL)] + [((share, 2 * units), LOW)] * chips,
        [here, after(feed_grads, grad_p1)],
        scalars=1,
        scratch=[pltpu.VMEM((chips * share, 2 * units), FULL)],
    )
    expand_rows = [expand_rows[0]] + [swap_ctx(expand_rows[r], 2 * r) for r in range(1, chips)]
    (grad_expand,) = call(
        functools.partial(expand_total_kernel, pb),
        [((share, hidden), FULL)],
        [here] + expand_rows,
        scalars=1,
    )
    first = (mine_ctx & 1) == 0
    block_output = (x2 + join(first, output, swap_ctx(output, 1)).astype(FULL)).astype(LOW)
    (
        grad_self_projection,
        grad_self_output,
        grad_cross_query,
        grad_cross_output,
        mine,
        other,
        grad_norm_gains,
        grad_table,
    ) = call(
        attention_total_kernel,
        [((share, 3 * width), FULL)]
        + [((share, width), FULL)] * 5
        + [(norm_gains.shape[:1] + (share,), FULL), ((heads, buckets), FULL)],
        [here, grads, hot],
        scalars=1,
    )
    other = swap_ctx(other, 1)
    grad_cross_memory = jnp.concatenate(
        [join(first, mine[:, :half], other[:, :half]), join(first, mine[:, half:], other[:, half:])],
        axis=1,
    )
    return (
        block_output[None],
        grad_x[None],
        grad_encoder[None],
        grad_self_projection,
        grad_self_output,
        grad_cross_query,
        grad_cross_memory,
        grad_cross_output,
        grad_expand,
        grad_contract,
        grad_norm_gains,
        grad_table.T,
    )


def body(*args):
    decoder_in, encoder_out, self_projection = args[:3]
    contract_weight = args[8]
    fits = (
        lax.axis_size("ctx") == 8
        and lax.axis_size("pb") == 4
        and decoder_in.shape[0] == 1
        and decoder_in.shape[1] == 128
        and self_projection.shape[0] % 8 == 0
        and contract_weight.shape[0] * 2 == self_projection.shape[0] * lax.axis_size("ctx")
        and encoder_out.shape[1] % 16 == 0
    )
    return (fast_body if fits else plain_body)(*args)


def solution(mesh):
    return jax.shard_map(
        body,
        mesh=mesh,
        in_specs=(
            P("pb", None, None),
            P("pb", "ctx", None),
            P(("pb", "ctx"), None),
            P(("pb", "ctx"), None),
            P(("pb", "ctx"), None),
            P(("pb", "ctx"), None),
            P(("pb", "ctx"), None),
            P(("pb", "ctx"), None),
            P(("pb", "ctx"), None),
            P(None, ("pb", "ctx")),
            P(),
            P(),
            P("pb", "ctx"),
            P("pb"),
            P("pb"),
            P("pb", None, None),
        ),
        out_specs=(
            P("pb", None, None),
            P("pb", None, None),
            P("pb", "ctx", None),
            P(("pb", "ctx"), None),
            P(("pb", "ctx"), None),
            P(("pb", "ctx"), None),
            P(("pb", "ctx"), None),
            P(("pb", "ctx"), None),
            P(("pb", "ctx"), None),
            P(("pb", "ctx"), None),
            P(None, ("pb", "ctx")),
            P(),
        ),
        check_vma=False,
    )
```

```python
import functools
import math

import jax
import jax.numpy as jnp
from jax import lax
from jax.experimental import pallas as pl
from jax.experimental.pallas import tpu as pltpu
from jax.sharding import PartitionSpec as P

LOW, FULL = jnp.bfloat16, jnp.float32
MASKED = -1000000000.0
EPS = 1e-06
HEAD = 64
ALL_BYTES = 58 * 1024 * 1024
SPARE_BYTES = 6 * 1024 * 1024


def dot(left, right, left_axis=1, right_axis=0):
    return lax.dot_general(
        left,
        right,
        (((left_axis,), (right_axis,)), ((), ())),
        preferred_element_type=FULL,
    )


def dot_t(left, right):
    return dot(left, right, 1, 1)


def outer_sum(left, right):
    return dot(left, right, 0, 0)


def rms_unit(values):
    factor = lax.rsqrt(jnp.mean(values * values, axis=-1, keepdims=True) + EPS)
    return values * factor, factor


def norm_back(grad, unit, factor, gain):
    scaled = grad * gain
    return factor * (scaled - unit * jnp.mean(scaled * unit, axis=-1, keepdims=True))


class Leaving:
    def __init__(self, held, target, sem):
        self.held, self.shape, self.dtype = held, held.shape, held.dtype
        self.copy = pltpu.make_async_copy(held, target, sem)
        self.left = False

    def leave(self):
        if not self.left:
            self.copy.start()
            self.left = True

    def __getitem__(self, index):
        return self.held[index]

    def __setitem__(self, index, values):
        self.held[index] = values


def place_of_device():
    mine_pb, mine_ctx = lax.axis_index("pb"), lax.axis_index("ctx")
    return mine_ctx & 1, mine_ctx >> 1, mine_pb, mine_ctx, lax.axis_size("ctx")


def call(kernel, outs, args, scalars=0, scratch=(), limit=None):
    placed = args[0] is None
    if placed:
        args, scalars = args[1:], scalars - 1
    arrays, specs, grid, held = [], [], (), []
    far_outs = [index for index, out in enumerate(outs) if len(out) == 3]
    for index, arg in enumerate(args):
        if isinstance(arg, tuple):
            arg, shape, place = arg
            specs.append(pl.BlockSpec(shape, lambda i, place=place: place))
            grid = (1,)
            held.append((shape, arg.dtype))
        else:
            specs.append(pl.BlockSpec(memory_space=pltpu.SMEM if index < scalars else pltpu.VMEM))
            held.append((arg.shape, arg.dtype))
        arrays.append(arg)
    held += [out[:2] for out in outs] + [(one.shape, one.dtype) for one in scratch]
    size = sum(math.prod(shape) * jnp.dtype(dtype).itemsize for shape, dtype in held)
    buffers = [pltpu.VMEM(*outs[i][:2]) for i in far_outs]
    if buffers:
        buffers.append(pltpu.SemaphoreType.DMA((len(buffers),)))

    def run(*refs):
        ins, results = list(refs[: len(args)]), list(refs[len(args) : len(args) + len(outs)])
        rest = refs[len(args) + len(outs) :]
        own, extra = rest[: len(scratch)], rest[len(scratch) :]
        moved = []
        for k, i in enumerate(far_outs):
            results[i] = Leaving(extra[k], results[i], extra[-1].at[k])
            moved.append(results[i])
        kernel(*([place_of_device()] if placed else []), *ins, *results, *own)
        for one in moved:
            one.leave()
            one.copy.wait()

    return pl.pallas_call(
        run,
        grid=grid,
        out_shape=[
            pltpu.HBM(*out[:2]) if len(out) == 3 else jax.ShapeDtypeStruct(*out) for out in outs
        ],
        in_specs=specs,
        out_specs=[
            pl.BlockSpec(memory_space=pltpu.HBM if len(out) == 3 else pltpu.VMEM) for out in outs
        ],
        scratch_shapes=list(scratch) + buffers,
        compiler_params=pltpu.CompilerParams(vmem_limit_bytes=limit or size + SPARE_BYTES),
    )(*arrays)


def to_low(values):
    return values.astype(jnp.bfloat16)


def normalize(values, scale):
    factor = lax.rsqrt(jnp.mean(values * values, axis=-1, keepdims=True) + 1e-06)
    return (values * factor * scale, values * factor, factor)


def gelu_tanh(values):
    return jax.nn.gelu(values, approximate=True)


def fetch(shards):
    return (
        lax.all_gather(shards[0], ("pb", "ctx"), axis=0, tiled=True),
        lax.all_gather(shards[1], ("pb", "ctx"), axis=0, tiled=True),
        lax.all_gather(shards[2], ("pb", "ctx"), axis=0, tiled=True),
        lax.all_gather(shards[3], ("pb", "ctx"), axis=0, tiled=True),
        lax.all_gather(shards[4], ("pb", "ctx"), axis=0, tiled=True),
        lax.all_gather(shards[5], ("pb", "ctx"), axis=0, tiled=True),
        lax.all_gather(shards[6], ("pb", "ctx"), axis=0, tiled=True),
        lax.all_gather(shards[7], ("pb", "ctx"), axis=1, tiled=True),
    )


def run_forward(params, decoder, encoder, allowed, visible, rel_bias):
    projection, self_out, cross_in, memory_in, cross_out, expand, contract, gains = params
    scale_gain = gains.astype(jnp.float32)
    count, length, width = decoder.shape
    heads = rel_bias.shape[0]
    head_dim = width // heads
    inverse = head_dim ** (-0.5)
    residual = decoder.astype(jnp.float32).reshape(count * length, width)
    normed_a, unit_a, factor_a = normalize(residual, scale_gain[0])
    normed_a = to_low(normed_a)
    joined = to_low(dot(normed_a, projection)).reshape(count, length, 3, heads, head_dim)
    query_rows, key_rows, value_rows = (joined[:, :, 0], joined[:, :, 1], joined[:, :, 2])
    self_scores = (
        jnp.einsum("nihd,njhd->nhij", query_rows, key_rows, preferred_element_type=jnp.float32)
        * inverse
        + rel_bias[None]
    )
    self_probs = jax.nn.softmax(jnp.where(allowed, self_scores, -1000000000.0), axis=-1)
    self_mixed = jnp.einsum(
        "nhij,njhd->nihd", to_low(self_probs), value_rows, preferred_element_type=jnp.float32
    )
    self_mix = to_low(self_mixed.reshape(count * length, width))
    after_self = residual + dot(self_mix, self_out)
    normed_b, unit_b, factor_b = normalize(after_self, scale_gain[1])
    normed_b = to_low(normed_b)
    cross_rows = to_low(dot(normed_b, cross_in)).reshape(count, length, heads, head_dim)
    ctx_rows = encoder.shape[1]
    memory = to_low(dot(encoder.reshape(count * ctx_rows, width), memory_in)).reshape(
        count, ctx_rows, 2, heads, head_dim
    )
    cross_keys, cross_vals = (memory[:, :, 0], memory[:, :, 1])
    cross_scores = (
        jnp.einsum("nihd,njhd->nhij", cross_rows, cross_keys, preferred_element_type=jnp.float32)
        * inverse
    )
    masked = jnp.where(visible, cross_scores, -1000000000.0)
    highest_score = lax.pmax(jnp.max(masked, axis=-1), "ctx")
    total = lax.psum(
        jnp.sum(jnp.where(visible, jnp.exp(masked - highest_score[..., None]), 0.0), axis=-1), "ctx"
    )
    cross_probs = (
        jnp.where(visible, jnp.exp(masked - highest_score[..., None]), 0.0) / total[..., None]
    )
    partial_mix = jnp.einsum(
        "nhij,njhd->nihd", to_low(cross_probs), cross_vals, preferred_element_type=jnp.float32
    )
    cross_mixed = lax.psum(partial_mix, "ctx")
    cross_mix = to_low(cross_mixed.reshape(count * length, width))
    after_cross = after_self + dot(cross_mix, cross_out)
    normed_c, unit_c, factor_c = normalize(after_cross, scale_gain[2])
    normed_c = to_low(normed_c)
    hidden = dot(normed_c, expand)
    active = to_low(gelu_tanh(hidden))
    output = after_cross + dot(active, contract)
    saved = (
        normed_a,
        unit_a,
        factor_a,
        query_rows,
        key_rows,
        value_rows,
        self_probs,
        self_mix,
        normed_b,
        unit_b,
        factor_b,
        cross_rows,
        cross_keys,
        cross_vals,
        cross_probs,
        cross_mix,
        normed_c,
        unit_c,
        factor_c,
        hidden,
        active,
        scale_gain,
    )
    return (output, saved)


def plain_body(
    decoder_in,
    encoder_out,
    self_projection,
    self_output,
    cross_query,
    cross_memory,
    cross_output,
    expand_weight,
    contract_weight,
    norm_gains,
    bias_table,
    bucket_index,
    passage_mask,
    target_length,
    task_group,
    cotangent,
):
    shards = (
        self_projection,
        self_output,
        cross_query,
        cross_memory,
        cross_output,
        expand_weight,
        contract_weight,
        norm_gains,
    )
    count, length, width = decoder_in.shape
    ctx_rows = encoder_out.shape[1]
    buckets, heads = bias_table.shape
    head_dim = width // heads
    inverse = head_dim ** (-0.5)
    positions = jnp.arange(length)
    offsets = jnp.clip(positions[:, None] - positions[None, :], 0, length - 1)
    pair_bucket = jnp.take(bucket_index, offsets.reshape(-1))
    one_hot = (pair_bucket[:, None] == jnp.arange(buckets)[None, :]).astype(jnp.bfloat16)
    rel_bias = dot(one_hot, bias_table).T.reshape(heads, length, length)
    causal = positions[None, :] <= positions[:, None]
    allowed = (causal[None] & (positions[None, None, :] < target_length[:, None, None]))[:, None]
    visible = (passage_mask > 0)[:, None, None, :]
    params = fetch(shards)
    output, saved = run_forward(params, decoder_in, encoder_out, allowed, visible, rel_bias)
    projection, self_out, cross_in, memory_in, cross_out, expand, contract, gains = params
    (
        normed_a,
        unit_a,
        factor_a,
        query_rows,
        key_rows,
        value_rows,
        self_probs,
        self_mix,
        normed_b,
        unit_b,
        factor_b,
        cross_rows,
        cross_keys,
        cross_vals,
        cross_probs,
        cross_mix,
        normed_c,
        unit_c,
        factor_c,
        hidden,
        active,
        scale_gain,
    ) = saved
    rows_total = count * length
    share = rows_total // lax.axis_size("ctx")
    start = lax.axis_index("ctx") * share

    def sliced(values):
        return lax.dynamic_slice_in_dim(values, start, share, 0)

    task_scale = jnp.where(task_group == 0, 1.0, jnp.where(task_group == 1, 0.5, 2.0)).astype(
        jnp.float32
    )
    row_live = (positions[None, :] < target_length[:, None]).astype(jnp.float32)
    grad_out = (
        cotangent.astype(jnp.float32) * (task_scale[:, None] * row_live)[:, :, None]
    ).reshape(rows_total, width)
    low_out = to_low(grad_out)
    grad_active = dot_t(low_out, contract)
    unused_value, gelu_pull = jax.vjp(gelu_tanh, hidden)
    grad_hidden = to_low(gelu_pull(grad_active)[0])
    grad_normed_c = dot_t(grad_hidden, expand)
    gain_c = jnp.sum(sliced(grad_normed_c * unit_c), axis=0)
    grad_after_cross = grad_out + norm_back(grad_normed_c, unit_c, factor_c, scale_gain[2])
    low_cross = to_low(grad_after_cross)
    grad_mix = to_low(dot_t(low_cross, cross_out)).reshape(count, length, heads, head_dim)
    grad_probs = jnp.einsum(
        "nihd,njhd->nhij", grad_mix, cross_vals, preferred_element_type=jnp.float32
    )
    row_dot = lax.psum(jnp.sum(grad_probs * cross_probs, axis=-1), "ctx")
    grad_scores = to_low(cross_probs * (grad_probs - row_dot[..., None]))
    partial_query = (
        jnp.einsum("nhij,njhd->nihd", grad_scores, cross_keys, preferred_element_type=jnp.float32)
        * inverse
    )
    grad_query = to_low(lax.psum(partial_query, "ctx")).reshape(rows_total, width)
    grad_key = (
        jnp.einsum("nhij,nihd->njhd", grad_scores, cross_rows, preferred_element_type=jnp.float32)
        * inverse
    )
    grad_value = jnp.einsum(
        "nhij,nihd->njhd", to_low(cross_probs), grad_mix, preferred_element_type=jnp.float32
    )
    grad_memory = to_low(jnp.stack([grad_key, grad_value], axis=2)).reshape(
        count * ctx_rows, 2 * width
    )
    encoder_rows = encoder_out.reshape(count * ctx_rows, width)
    grad_cross_memory = outer_sum(encoder_rows, grad_memory)
    grad_encoder = to_low(dot_t(grad_memory, memory_in)).reshape(count, ctx_rows, width)
    grad_normed_b = dot_t(grad_query, cross_in)
    gain_b = jnp.sum(sliced(grad_normed_b * unit_b), axis=0)
    grad_after_self = grad_after_cross + norm_back(grad_normed_b, unit_b, factor_b, scale_gain[1])
    low_self = to_low(grad_after_self)
    grad_self_mix = to_low(dot_t(low_self, self_out)).reshape(count, length, heads, head_dim)
    grad_probs_self = jnp.einsum(
        "nihd,njhd->nhij", grad_self_mix, value_rows, preferred_element_type=jnp.float32
    )
    self_dot = jnp.sum(grad_probs_self * self_probs, axis=-1, keepdims=True)
    grad_scores_self = to_low(self_probs * (grad_probs_self - self_dot))
    pair_grad = jnp.sum(grad_scores_self.astype(jnp.float32), axis=0).reshape(
        heads, length * length
    )
    pair_count = length * length // lax.axis_size("ctx")
    pair_start = lax.axis_index("ctx") * pair_count
    pair_slice = lax.dynamic_slice_in_dim(pair_grad, pair_start, pair_count, 1)
    hot_slice = lax.dynamic_slice_in_dim(one_hot.astype(jnp.float32), pair_start, pair_count, 0)
    table_term = lax.dot_general(
        hot_slice,
        pair_slice,
        (((0,), (1,)), ((), ())),
        precision=lax.Precision.HIGHEST,
        preferred_element_type=jnp.float32,
    )
    grad_table = lax.psum(table_term, ("pb", "ctx"))
    grad_q = (
        jnp.einsum(
            "nhij,njhd->nihd", grad_scores_self, key_rows, preferred_element_type=jnp.float32
        )
        * inverse
    )
    grad_k = (
        jnp.einsum(
            "nhij,nihd->njhd", grad_scores_self, query_rows, preferred_element_type=jnp.float32
        )
        * inverse
    )
    grad_v = jnp.einsum(
        "nhij,nihd->njhd", to_low(self_probs), grad_self_mix, preferred_element_type=jnp.float32
    )
    grad_joined = to_low(jnp.stack([grad_q, grad_k, grad_v], axis=2)).reshape(rows_total, 3 * width)
    grad_normed_a = dot_t(grad_joined, projection)
    gain_a = jnp.sum(sliced(grad_normed_a * unit_a), axis=0)
    grad_decoder = to_low(
        grad_after_self + norm_back(grad_normed_a, unit_a, factor_a, scale_gain[0])
    ).reshape(count, length, width)
    gain_grads = jnp.stack([gain_a, gain_b, gain_c])
    pairs = (
        (normed_a, grad_joined),
        (self_mix, low_self),
        (normed_b, grad_query),
        (cross_mix, low_cross),
        (normed_c, grad_hidden),
        (active, low_out),
    )
    partials = tuple((outer_sum(sliced(left), sliced(right)) for left, right in pairs))
    summed = (
        lax.psum_scatter(partials[0], ("pb", "ctx"), scatter_dimension=0, tiled=True),
        lax.psum_scatter(partials[1], ("pb", "ctx"), scatter_dimension=0, tiled=True),
        lax.psum_scatter(partials[2], ("pb", "ctx"), scatter_dimension=0, tiled=True),
        lax.psum_scatter(grad_cross_memory, ("pb", "ctx"), scatter_dimension=0, tiled=True),
        lax.psum_scatter(partials[3], ("pb", "ctx"), scatter_dimension=0, tiled=True),
        lax.psum_scatter(partials[4], ("pb", "ctx"), scatter_dimension=0, tiled=True),
        lax.psum_scatter(partials[5], ("pb", "ctx"), scatter_dimension=0, tiled=True),
        lax.psum_scatter(gain_grads, ("pb", "ctx"), scatter_dimension=1, tiled=True),
    )
    block_output = to_low(output).reshape(count, length, width)
    return (
        block_output,
        grad_decoder,
        grad_encoder,
        summed[0],
        summed[1],
        summed[2],
        summed[3],
        summed[4],
        summed[5],
        summed[6],
        summed[7],
        grad_table,
    )


def swap_ctx(values, mask):
    size = lax.axis_size("ctx")
    return lax.ppermute(values, "ctx", [(i, i ^ mask) for i in range(size)])


def swap_pb(values, mask):
    size = lax.axis_size("pb")
    return lax.ppermute(values, "pb", [(i, i ^ mask) for i in range(size)])


def exchange(values, axis):
    return lax.all_to_all(values, axis, 0, 0, tiled=True)


def all_pb(values):
    size = lax.axis_size("pb")
    return [values] + [swap_pb(values, r) for r in range(1, size)]


def after(values, earlier):
    return lax.optimization_barrier((values, earlier))[0]


def all_chips(values):
    return [values] + [swap_ctx(values, mask) for mask in range(2, lax.axis_size("ctx"), 2)]


def tree(terms):
    while len(terms) > 1:
        terms = [a + b for a, b in zip(terms[0::2], terms[1::2])]
    return terms[0]


def add_chips(parts):
    return tree([part.astype(FULL) for part in parts]).astype(LOW)


def to_owners(parts):
    return [parts[0]] + [swap_pb(part, r) for r, part in enumerate(parts) if r]


def pick(low, high):
    lanes = lax.broadcasted_iota(jnp.int32, low.shape, 1)
    return jnp.where(lanes < low.shape[1] // 2, low, high)


def lane_mask(values, side):
    zeros = jnp.zeros_like(values)
    return pick(values, zeros) if side == 0 else pick(zeros, values)


def both_heads(values):
    return jnp.concatenate([lane_mask(values, 0), lane_mask(values, 1)], axis=0)


def pick_rows(values):
    middle = values.shape[0] // 2
    return pick(values[:middle], values[middle:])


def join(first, mine, other, axis=1):
    return jnp.where(
        first,
        jnp.concatenate([mine, other], axis=axis),
        jnp.concatenate([other, mine], axis=axis),
    )


def half_of(first, values, axis=1):
    middle = values.shape[axis] // 2
    if axis == 0:
        return jnp.where(first, values[:middle], values[middle:])
    return jnp.where(first, values[:, :middle], values[:, middle:])


CORE, CHIP, PB, CTX = range(4)


def prepare_kernel(proj, self_out, cross_in, gains, out):
    count = gains.shape[0]
    row = lax.broadcasted_iota(jnp.int32, (count, 128), 0)
    lane = lax.broadcasted_iota(jnp.int32, (count, 128), 1)
    columns = outer_sum(gains[...], jnp.where(row == lane, 1.0, 0.0).astype(LOW)).astype(LOW)
    at = 0
    for part in (proj[...], self_out[...], cross_in[...], columns):
        out[:, at : at + part.shape[1]] = part
        at += part.shape[1]


def block_places(pb):
    middle = pb // 2
    return [
        [(0, 0), (0, 1), (0, 2)],
        [(r, 0) for r in range(1, pb)],
        [(r, 1) for r in range(1, pb)],
        [(r, 2) for r in range(1, pb)],
        [(r, 3) for r in range(middle)],
        [(r, 3) for r in range(middle, pb)],
    ]


def place(here, ins, outs, ctx):
    first = here[CORE] == 0
    pb = ins[2].shape[0] + 1
    rows = ins[0].shape[1]
    for i, places in enumerate(block_places(pb)):
        mine, other = ins[2 * i], ins[2 * i + 1]
        for k, (z, flip) in enumerate(places):
            both = join(first, mine[k], other[k], 0)
            owner = (z ^ here[PB]) * (ctx // 2) + (here[CHIP] ^ flip)
            slot = pl.multiple_of(owner * 2 * rows, 16)
            at = 0
            for out in outs:
                width = out.shape[1]
                out[pl.ds(slot, 2 * rows), :] = both[:, at : at + width]
                at += width


def first_hops(own):
    return swap_ctx(own, 2), swap_ctx(own, 4)


def gather_rows(own, along, far, far_along):
    middle = (far.shape[0] + 1) // 2
    low = jnp.concatenate([along[0][None], far_along[0][: middle - 1]])
    low = swap_ctx(low, 4)
    high = swap_ctx(far_along[1][middle - 1 :], 2)
    blocks = []
    for array in (jnp.stack([own, *along]), far, *far_along, low, high):
        blocks += [array, swap_ctx(array, 1)]
    return blocks, (low, high)


def self_kernel(ctx, here, length, x, table, *refs):
    blocks, refs = refs[:-12], refs[-12:]
    proj, self_out, cross_in, gains_out, p1, probs, mix, x1, h1, h2, cq, columns = refs
    rows, width = x.shape
    heads = width // HEAD
    pair = 2 * HEAD
    inverse = jnp.asarray(HEAD ** (-0.5), LOW)
    place(here, blocks, [proj, self_out, cross_in, columns], ctx)
    for one in (proj, self_out, cross_in):
        one.leave()
    gains = columns[...].astype(FULL).T
    gains_out[...] = gains[: gains_out.shape[0]]
    xf = x[...].astype(FULL)
    unit, _ = rms_unit(xf)
    normed = (unit * gains[0:1, :]).astype(LOW)
    h1[...] = normed
    joined = dot(normed, proj[...]).astype(LOW)
    p1[...] = joined
    p1.leave()
    row = lax.broadcasted_iota(jnp.int32, (rows, rows), 0)
    col = lax.broadcasted_iota(jnp.int32, (rows, rows), 1)
    allowed = (col <= row) & (col < length[0])
    barred = jnp.where(allowed, 0.0, MASKED)
    mixes = []
    for g in range(heads // 2):
        at = g * pair
        q = both_heads(joined[:, at : at + pair] * inverse)
        k = joined[:, width + at : width + at + pair]
        v = joined[:, 2 * width + at : 2 * width + at + pair]
        bias = [
            pltpu.roll(
                jnp.broadcast_to(table[head : head + 1, :], (rows, rows)),
                1,
                axis=1,
                stride=1,
                stride_axis=0,
            )
            + barred
            for head in (2 * g, 2 * g + 1)
        ]
        scores = dot_t(q, k) + jnp.concatenate(bias, axis=0)
        powers = jnp.exp(scores - jnp.max(scores, axis=-1, keepdims=True))
        prob = powers * (1.0 / jnp.sum(powers, axis=-1, keepdims=True))
        probs[g] = prob
        mixes.append(pick_rows(dot(prob.astype(LOW), v)).astype(LOW))
    probs.leave()
    mixes = jnp.concatenate(mixes, axis=1)
    mix[...] = mixes
    after_self = xf + dot(mixes, self_out[...])
    x1[...] = after_self
    unit, _ = rms_unit(after_self)
    normed = (unit * gains[1:2, :]).astype(LOW)
    h2[...] = normed
    cq[...] = dot(normed, half_of(here[CORE] == 0, cross_in[...])).astype(LOW)


def memory_kernel(ctx, here, mine, other, *refs):
    blocks, (memory_in, memory) = refs[:-2], refs[-2:]
    place(here, blocks, [memory_in], ctx)
    memory_in.leave()
    first = here[CORE] == 0
    width = mine.shape[1]
    keys = half_of(first, memory_in[:, :width])
    values = half_of(first, memory_in[:, width:])
    weight = jnp.concatenate([keys, values], axis=1)
    rows = mine.shape[0]
    memory[:rows] = dot(mine[...], weight).astype(LOW)
    memory[rows:] = dot(other[...], weight).astype(LOW)


def pack_stats(tops, totals):
    rows = tops[0].shape[0]
    lanes = lax.broadcasted_iota(jnp.int32, (rows, 128), 1)
    columns = jnp.zeros((rows, 128), FULL)
    for index, column in enumerate(tops + totals):
        columns = jnp.where(lanes // 3 == index, column, columns)
    high = columns.astype(LOW).astype(FULL)
    middle = (columns - high).astype(LOW).astype(FULL)
    kind = lanes % 3
    return jnp.where(kind == 0, high, jnp.where(kind == 1, middle, columns - high - middle)).astype(
        LOW
    )


def read_stats(packed):
    values = packed.astype(FULL)
    return values + pltpu.roll(values, 127, axis=1) + pltpu.roll(values, 126, axis=1)


def cross_kernel(cq, memory, visible, packed):
    rows, half = cq.shape
    pair = 2 * HEAD
    inverse = jnp.asarray(HEAD ** (-0.5), LOW)
    barred = jnp.where(visible[...] > 0, 0.0, MASKED)
    tops, totals, mixes = [], [], []
    for at in range(0, half, pair):
        q = both_heads(cq[:, at : at + pair] * inverse)
        k = memory[:, at : at + pair]
        v = memory[:, half + at : half + at + pair]
        scores = dot_t(q, k) + barred
        top = jnp.max(scores, axis=-1, keepdims=True)
        powers = jnp.exp(scores - top)
        total = jnp.sum(powers, axis=-1, keepdims=True)
        tops += [top[:rows], top[rows:]]
        totals += [total[:rows], total[rows:]]
        mixes.append(pick_rows(dot(powers.astype(LOW), v)).astype(LOW))
    packed[...] = jnp.concatenate(mixes + [pack_stats(tops, totals)], axis=1)


def spread(columns):
    shape = (columns[0].shape[0], 2 * HEAD)
    return jnp.concatenate(
        [
            pick(jnp.broadcast_to(a, shape), jnp.broadcast_to(b, shape))
            for a, b in zip(columns[0::2], columns[1::2])
        ],
        axis=1,
    )


def merge_kernel(here, *refs):
    ins, mix, stats = refs[:-2], refs[-2], refs[-1]
    half = mix.shape[1]
    heads = half // HEAD
    packed = [ref[...] for ref in ins]
    step = 1
    while step < len(packed):
        flip = (here[CHIP] & step) != 0
        packed = [jnp.where(flip, packed[i ^ step], packed[i]) for i in range(len(packed))]
        step *= 2
    read = [read_stats(p[:, half:]) for p in packed]
    top = read[0]
    for other in read[1:]:
        top = jnp.maximum(top, other)
    lanes = lax.broadcasted_iota(jnp.int32, top.shape, 1)
    is_top = lanes < 3 * heads
    scales = [jnp.exp(jnp.where(is_top, r - top, 0.0)) for r in read]
    total = tree([r * pltpu.roll(w, 3 * heads, axis=1) for r, w in zip(read, scales)])
    share = 1.0 / pltpu.roll(total, 128 - 3 * heads, axis=1)
    weights = [w * share for w in scales]
    terms = [
        p[:, :half].astype(FULL) * spread([w[:, 3 * h : 3 * h + 1] for h in range(heads)])
        for p, w in zip(packed, weights)
    ]
    mix[...] = tree(terms).astype(LOW)
    stats[...] = jnp.where(is_top, top, total)


def gelu_parts(values):
    slope = (2.0 / jnp.pi) ** 0.5
    square = values * values
    bent = jnp.tanh(slope * (values + 0.044715 * values * square))
    active = 0.5 * values * (1.0 + bent)
    inner = slope * (1.0 + 3 * 0.044715 * square)
    return active, 0.5 * (1.0 + bent) + 0.5 * values * (1.0 - bent * bent) * inner


def task_rows(length, task, cot):
    rows = lax.broadcasted_iota(jnp.int32, cot.shape, 0)
    weight = jnp.where(task[0] == 0, 1.0, jnp.where(task[0] == 1, 0.5, 2.0)).astype(FULL)
    return jnp.where(rows < length[0], cot[...].astype(FULL) * weight, 0.0)


def feed_weights(here, mine, other, expand, contract):
    first = here[CORE] == 0
    width = contract.shape[1]
    slab = mine.shape[1]
    share = slab // 4
    for z in range(mine.shape[0]):
        owner = z
        contract[pl.ds(pl.multiple_of(2 * owner * slab, 16), 2 * slab), :] = join(
            first, mine[z, :, :width], other[z, :, :width], 0
        )
        for r in range(4):
            rows = slice(r * share, (r + 1) * share)
            both = join(first, mine[z, rows, width:], other[z, rows, width:], 0)
            at = pl.multiple_of((owner * 4 + (here[CHIP] ^ r)) * 2 * share, 16)
            expand[pl.ds(at, 2 * share), :] = both


def feed_kernel(
    ctx,
    here,
    length,
    task,
    mix_mine,
    mix_other,
    x1,
    gains,
    feed_mine,
    feed_other,
    cot,
    *refs,
):
    blocks, outs = refs[:-10], refs[-10:]
    place(here, blocks, [outs[0]], ctx)
    outs[0].leave()
    feed_step(
        here, length, task, mix_mine, mix_other, x1, gains, feed_mine, feed_other, cot, *outs
    )


def feed_step(
    here,
    length,
    task,
    mix_mine,
    mix_other,
    x1,
    gains,
    feed_mine,
    feed_other,
    cot,
    cross_out,
    x2,
    h3,
    active,
    low_out,
    grad_hidden,
    partial,
    part_out,
    expand,
    contract,
):
    first = here[CORE] == 0
    after_cross = x1[...] + dot(join(first, mix_mine[...], mix_other[...]), cross_out[...])
    x2[...] = after_cross
    x2.leave()
    unit, _ = rms_unit(after_cross)
    normed = (unit * gains[2:3, :]).astype(LOW)
    h3[...] = normed
    low = task_rows(length, task, cot).astype(LOW)
    low_out[...] = low
    feed_weights(here, feed_mine, feed_other, expand, contract)
    value, slope = gelu_parts(dot(normed, expand[...]))
    value = value.astype(LOW)
    grad = (dot_t(low, contract[...]) * slope).astype(LOW)
    active[...] = value
    grad_hidden[...] = grad
    partial[...] = dot_t(grad, half_of(first, expand[...], 0)).astype(LOW)
    partial.leave()
    part_out[...] = dot(value, half_of(first, contract[...])).astype(LOW)


def feed_grad_kernel(share, here, active, low_out, h3, grad_hidden, out, contract, expand):
    contract[...] = outer_sum(active[...], low_out[...])
    expand[...] = outer_sum(h3[...], grad_hidden[...])
    pb = out.shape[0]
    slab = contract.shape[0] // pb // 2
    block = expand.shape[0] // pb
    for z in range(pb):
        at = pl.multiple_of((2 * z + here[CORE]) * slab, 16)
        out[z, :slab] = contract[pl.ds(at, slab)].astype(LOW)
        rows = [
            expand[pl.ds(pl.multiple_of(z * block + at + here[CORE] * share, 8), share)]
            for at in range(0, block, 2 * share)
        ]
        out[z, slab:] = jnp.concatenate(rows, axis=0).astype(LOW)


def cross_back_kernel(
    here,
    length,
    task,
    sums_mine,
    sums_other,
    x2,
    gains,
    cot,
    cross_out,
    cq,
    memory,
    visible,
    stats,
    mix,
    dx2,
    low_cross,
    grad_cq,
    grad_mine,
    grad_other,
    gain_grad,
):
    first = here[CORE] == 0
    half = mix.shape[1]
    heads = half // HEAD
    pair = 2 * HEAD
    inverse = jnp.asarray(HEAD ** (-0.5), LOW)
    unit, factor = rms_unit(x2[...])
    grad = join(first, sums_mine[...], sums_other[...]).astype(FULL)
    gain_grad[...] = jnp.sum(grad * unit, axis=0, keepdims=True)
    back = task_rows(length, task, cot) + norm_back(grad, unit, factor, gains[2:3, :])
    dx2[...] = back
    low = back.astype(LOW)
    low_cross[...] = low
    grad_mix = dot_t(low, half_of(first, cross_out[...], 0)).astype(LOW)
    barred = jnp.where(visible[...] > 0, 0.0, MASKED)
    shares = 1.0 / stats[...]
    passage = grad_mine.shape[0]
    for g in range(heads // 2):
        at = g * pair
        q = both_heads(cq[:, at : at + pair] * inverse)
        do = both_heads(grad_mix[:, at : at + pair])
        k = memory[:, at : at + pair]
        v = memory[:, half + at : half + at + pair]
        mixed = mix[:, at : at + pair].astype(FULL)
        top, scale = [
            jnp.concatenate([a[:, c : c + 1], a[:, c + 3 : c + 4]], axis=0)
            for a, c in ((stats, 6 * g), (shares, 3 * heads + 6 * g))
        ]
        rho = jnp.sum(
            do.astype(FULL) * jnp.concatenate([mixed, mixed], axis=0), axis=-1, keepdims=True
        )
        prob = jnp.exp(dot_t(q, k) + barred - top) * scale
        grad_scores = (prob * (dot_t(do, v) - rho)).astype(LOW)
        grad_cq[:, at : at + pair] = (pick_rows(dot(grad_scores, k)) * HEAD ** (-0.5)).astype(LOW)
        keys = outer_sum(grad_scores, q).astype(LOW)
        values = outer_sum(prob.astype(LOW), do).astype(LOW)
        for ref, begin in ((grad_mine, 0), (grad_other, passage)):
            ref[:, at : at + pair] = keys[begin : begin + passage]
            ref[:, half + at : half + at + pair] = values[begin : begin + passage]


def memory_grad_kernel(pb, here, mine, other, grad_mine, grad_other, *refs):
    outs, whole = refs[:-1], refs[-1]
    whole[...] = outer_sum(mine[...], grad_mine[...]) + outer_sum(other[...], grad_other[...])
    share = whole.shape[0] // pb // len(outs)
    for r, out in enumerate(outs):
        chip = here[CHIP] ^ r
        for z in range(pb):
            at = pl.multiple_of((z * len(outs) + chip) * share, 16)
            out[z * share : (z + 1) * share] = whole[pl.ds(at, share)].astype(LOW)


def encoder_grad_kernel(here, mine, other, memory_in, grad):
    first = here[CORE] == 0
    half = mine.shape[1] // 2
    keys = join(first, mine[:, :half], other[:, :half])
    values = join(first, mine[:, half:], other[:, half:])
    grad[...] = dot_t(jnp.concatenate([keys, values], axis=1), memory_in[...]).astype(LOW)


def owned(left, choose):
    return dot(left, choose).astype(LOW)


def self_back_kernel(
    here,
    cq_mine,
    cq_other,
    cross_in,
    x1,
    gains,
    dx2,
    self_out,
    p1,
    probs,
    x,
    proj,
    gain_grad,
    low_self,
    grad_p1,
    grad_x,
    small,
):
    rows, width = x.shape
    heads = width // HEAD
    pair = 2 * HEAD
    inverse = jnp.asarray(HEAD ** (-0.5), LOW)
    grad = dot_t(join(here[CORE] == 0, cq_mine[...], cq_other[...]), cross_in[...])
    unit, factor = rms_unit(x1[...])
    small[...] = jnp.zeros_like(small)
    small[1:2, :] = jnp.sum(grad * unit, axis=0, keepdims=True)
    small[2:3, :] = gain_grad[...]
    dx1 = dx2[...] + norm_back(grad, unit, factor, gains[1:2, :])
    low = dx1.astype(LOW)
    low_self[...] = low
    row = lax.broadcasted_iota(jnp.int32, (rows, rows), 0)
    col = lax.broadcasted_iota(jnp.int32, (rows, rows), 1)
    flip = jnp.where(row + col == rows - 1, 1.0, 0.0).astype(LOW)
    grad_mix = dot_t(low, self_out[...]).astype(LOW)
    parts = [[], [], []]
    for g in range(heads // 2):
        at = g * pair
        q = both_heads(p1[:, at : at + pair] * inverse)
        k = p1[:, width + at : width + at + pair]
        v = p1[:, 2 * width + at : 2 * width + at + pair]
        do = both_heads(grad_mix[:, at : at + pair])
        prob = probs[g]
        grad_probs = dot_t(do, v)
        rho = jnp.sum(prob * grad_probs, axis=-1, keepdims=True)
        grad_scores = (prob * (grad_probs - rho)).astype(LOW)
        turned = dot(flip, jnp.concatenate([grad_scores[:rows], grad_scores[rows:]], axis=1))
        for side in range(2):
            part = turned[:, side * rows : (side + 1) * rows]
            part = pltpu.roll(part, 0, axis=1, stride=1, stride_axis=0)
            head = 3 + 2 * g + side
            small[head : head + 1, :rows] = jnp.sum(part, axis=0, keepdims=True)
        parts[0].append((pick_rows(dot(grad_scores, k)) * HEAD ** (-0.5)).astype(LOW))
        parts[1].append(outer_sum(grad_scores, q).astype(LOW))
        parts[2].append(outer_sum(prob.astype(LOW), do).astype(LOW))
    joined = jnp.concatenate(parts[0] + parts[1] + parts[2], axis=1)
    grad_p1[...] = joined
    grad = dot_t(joined, proj[...])
    unit, factor = rms_unit(x[...].astype(FULL))
    small[0:1, :] = jnp.sum(grad * unit, axis=0, keepdims=True)
    grad_x[...] = (dx1 + norm_back(grad, unit, factor, gains[0:1, :])).astype(LOW)


def feed_total_kernel(here, parts, contract, *refs):
    outs, rows = refs[:-1], refs[-1]
    total = tree([parts[z].astype(FULL) for z in range(parts.shape[0])])
    slab = contract.shape[0]
    contract[...] = total[:slab]
    rows[...] = total[slab:]
    share = outs[0].shape[0]
    for r, out in enumerate(outs):
        out[...] = rows[pl.ds(pl.multiple_of((here[CHIP] ^ r) * share, 8), share)].astype(LOW)


def expand_total_kernel(pb, here, *refs):
    parts, out = [ref[...].astype(FULL) for ref in refs[:-1]], refs[-1]
    step = 1
    while step < len(parts):
        flip = (here[CHIP] & step) != 0
        parts = [jnp.where(flip, parts[i ^ step], parts[i]) for i in range(len(parts))]
        step *= 2
    units = parts[0].shape[1] // pb
    out[...] = jnp.concatenate(
        [part[:, q * units : (q + 1) * units] for q in range(pb) for part in parts], axis=1
    )


def attention_grad_kernel(
    count,
    here,
    mix_mine,
    mix_other,
    low_cross,
    h2,
    cq_mine,
    cq_other,
    mix1,
    low_self,
    h1,
    grad_p1,
    small,
    *refs,
):
    pieces, out, choose, sums = refs[:count], *refs[count:]
    first = here[CORE] == 0
    pb = out.shape[0]
    width = mix1.shape[1]
    share = sums.shape[0] // pb
    lane = lax.broadcasted_iota(jnp.int32, choose.shape, 1)
    row = lax.broadcasted_iota(jnp.int32, choose.shape, 0)
    mine = lane // share * (width // pb) + here[CTX] * share + lane % share
    choose[...] = jnp.where(row == mine, 1.0, 0.0).astype(LOW)

    def owned(left, right):
        return outer_sum(dot(left, choose[...]).astype(LOW), right)

    sums[:, : 3 * width] = owned(h1[...], grad_p1[...])
    sums[:, 3 * width : 4 * width] = owned(mix1[...], low_self[...])
    cq = join(first, cq_mine[...], cq_other[...])
    sums[:, 4 * width : 5 * width] = owned(h2[...], cq)
    mix2 = join(first, mix_mine[...], mix_other[...])
    sums[:, 5 * width :] = owned(mix2, low_cross[...])
    total = tree([piece[...].astype(FULL) for piece in pieces])
    both = 2 * share
    for z in range(pb):
        rows = sums[z * share : (z + 1) * share]
        blocks = [rows[:, a : a + width] for a in range(0, 6 * width, width)]
        blocks += [total[z * both : (z + 1) * both], small[...]]
        out[z] = jnp.concatenate(blocks, axis=0).astype(LOW)


def attention_total_kernel(
    here, parts, hot, proj_grad, out_grad, query_grad, cross_grad, mine, other, gain_grad, table
):
    total = tree([parts[z].astype(FULL) for z in range(parts.shape[0])])
    first = here[CORE] == 0
    share, width = out_grad.shape
    blocks = [total[a : a + share] for a in range(0, 8 * share, share)]
    proj_grad[...] = jnp.concatenate(blocks[:3], axis=1)
    out_grad[...] = blocks[3]
    query_grad[...] = blocks[4]
    cross_grad[...] = blocks[5]
    mine[...] = jnp.where(first, blocks[6], blocks[7])
    other[...] = jnp.where(first, blocks[7], blocks[6])
    small = total[8 * share :]
    gains = gain_grad.shape[0]
    rows = hot.shape[1]
    shape = (width, share)
    place_of = lax.broadcasted_iota(jnp.int32, shape, 1) + (here[PB] * here[4] + here[CTX]) * share
    chosen = jnp.where(lax.broadcasted_iota(jnp.int32, shape, 0) == place_of, 1.0, 0.0)
    highest = lax.Precision.HIGHEST
    gain_grad[...] = jnp.dot(small, chosen, precision=highest, preferred_element_type=FULL)[:gains]
    heads = table.shape[0]
    whole = lax.dot_general(
        small[:, :rows],
        hot[...].astype(FULL),
        (((1,), (1,)), ((), ())),
        precision=highest,
        preferred_element_type=FULL,
    )
    table[...] = whole[gains : gains + heads]


def fast_body(
    decoder_in,
    encoder_out,
    self_projection,
    self_output,
    cross_query,
    cross_memory,
    cross_output,
    expand_weight,
    contract_weight,
    norm_gains,
    bias_table,
    bucket_index,
    passage_mask,
    target_length,
    task_group,
    cotangent,
):
    pb, ctx = lax.axis_size("pb"), lax.axis_size("ctx")
    mine_pb, mine_ctx = lax.axis_index("pb"), lax.axis_index("ctx")
    here = None
    rows, width = decoder_in.shape[1:]
    half = width // 2
    passage = encoder_out.shape[1]
    buckets, heads = bias_table.shape
    share = self_projection.shape[0]
    hidden = expand_weight.shape[1]
    slab = contract_weight.shape[0]
    units = pb * slab
    chips = ctx // 2
    x, e, cot = decoder_in[0], encoder_out[0], cotangent[0]

    (columns,) = call(
        prepare_kernel,
        [((share, 5 * width + 128), LOW)],
        [self_projection, self_output, cross_query, norm_gains],
    )
    along = first_hops(columns)
    far = jnp.stack(all_pb(columns)[1:])
    mixed = expand_weight.reshape(share, pb, chips, 2 * slab).transpose(2, 0, 1, 3)
    mixed = mixed.reshape(chips, share, 2 * units)
    chip = mine_ctx >> 1
    mixed = [lax.dynamic_index_in_dim(mixed, chip ^ r, 0, False) for r in range(chips)]
    mixed = jnp.concatenate([mixed[0]] + [swap_ctx(mixed[r], 2 * r) for r in range(1, chips)])
    e_other = swap_ctx(e, 1)
    visible = jnp.concatenate([passage_mask, swap_ctx(passage_mask, 1)], axis=1)
    others = jnp.concatenate([cross_memory, cross_output], axis=1)
    others_along = first_hops(after(others, along))
    far_along = first_hops(after(far, (e_other, visible, mixed, others_along)))
    proj_blocks, _ = gather_rows(columns, along, far, far_along)
    others_far = jnp.stack(all_pb(after(others, far))[1:])
    others_far_along = first_hops(after(others_far, far_along))
    others_blocks, last = gather_rows(others, others_along, others_far, others_far_along)
    x = after(x, others_far_along)
    feed = jnp.concatenate([contract_weight, mixed], axis=1)
    feed = jnp.broadcast_to(after(feed, others_far)[None], (pb,) + feed.shape)
    feed = exchange(feed, "pb")

    hot = (jnp.arange(buckets)[:, None] == bucket_index[::-1][None, :]).astype(LOW)
    table = outer_sum(bias_table, hot)

    proj, self_out, cross_in, gains, p1, probs, mix1, x1, h1, h2, cq = call(
        functools.partial(self_kernel, ctx),
        [
            ((width, 3 * width), LOW, True),
            ((width, width), LOW, True),
            ((width, width), LOW, True),
            ((norm_gains.shape[0], width), FULL),
            ((rows, 3 * width), LOW, True),
            ((heads // 2, 2 * rows, rows), FULL, True),
            ((rows, width), LOW),
            ((rows, width), FULL),
            ((rows, width), LOW),
            ((rows, width), LOW),
            ((rows, half), LOW),
        ],
        [here, target_length, x, table] + proj_blocks,
        scalars=2,
        scratch=[pltpu.VMEM((width, 128), LOW)],
        limit=ALL_BYTES,
    )
    def part(size, index):
        return [(b, b.shape[:2] + (size * width,), (0, 0, index)) for b in others_blocks]

    feed = after(feed, cq)
    feed_other = swap_ctx(feed, 1)
    memory_in, memory = call(
        functools.partial(memory_kernel, ctx),
        [((width, 2 * width), LOW, True), ((2 * passage, width), LOW)],
        [here, e, e_other] + part(2, 0),
        scalars=1,
    )
    (packed,) = call(cross_kernel, [((rows, half + 128), LOW)], [cq, memory, visible])
    mix2, stats = call(
        merge_kernel,
        [((rows, half), LOW), ((rows, 128), FULL)],
        [here] + all_chips(packed),
        scalars=1,
    )
    mix2_other = swap_ctx(mix2, 1)

    cross_out, x2, h3, active, low_out, grad_hidden, partial, part_out = call(
        functools.partial(feed_kernel, ctx),
        [
            ((width, width), LOW, True),
            ((rows, width), FULL, True),
            ((rows, width), LOW),
            ((rows, 2 * units), LOW),
            ((rows, width), LOW),
            ((rows, 2 * units), LOW),
            ((rows, half), LOW, True),
            ((rows, half), LOW),
        ],
        [
            here,
            target_length,
            task_group,
            mix2,
            mix2_other,
            x1,
            gains,
            feed,
            feed_other,
            cot,
        ]
        + part(1, 2),
        scalars=3,
        scratch=[pltpu.VMEM((width, 2 * units), LOW), pltpu.VMEM((2 * units, width), LOW)],
    )
    partials = all_chips(partial)
    sums = add_chips(partials)
    sums_other = swap_ctx(sums, 1)
    (feed_grads,) = call(
        functools.partial(feed_grad_kernel, share),
        [((pb, 2 * slab, width), LOW)],
        [here, after(active, partials), low_out, h3, grad_hidden],
        scalars=1,
        scratch=[pltpu.VMEM((2 * units, width), FULL), pltpu.VMEM((width, 2 * units), FULL)],
    )
    feed_grads = exchange(feed_grads, "pb")

    dx2, low_cross, grad_cq, grad_mine, grad_other, gain_grad = call(
        cross_back_kernel,
        [
            ((rows, width), FULL),
            ((rows, width), LOW),
            ((rows, half), LOW),
            ((passage, width), LOW),
            ((passage, width), LOW),
            ((1, width), FULL),
        ],
        [
            here,
            target_length,
            task_group,
            sums,
            sums_other,
            x2,
            gains,
            cot,
            cross_out,
            cq,
            memory,
            visible,
            stats,
            mix2,
        ],
        scalars=3,
    )
    grad_cq = add_chips(all_chips(grad_cq))
    cq_other = swap_ctx(grad_cq, 1)
    pieces = call(
        functools.partial(memory_grad_kernel, pb),
        [((pb * 2 * share, width), LOW)] * chips,
        [here, e, e_other, grad_mine, grad_other],
        scalars=1,
        scratch=[pltpu.VMEM((width, width), FULL)],
    )
    pieces = [pieces[0]] + [swap_ctx(pieces[r], 2 * r) for r in range(1, chips)]
    memory_other = swap_ctx(grad_other, 1)

    low_self, grad_p1, grad_x, small = call(
        self_back_kernel,
        [
            ((rows, width), LOW),
            ((rows, 3 * width), LOW),
            ((rows, width), LOW),
            ((16, width), FULL),
        ],
        [
            here,
            grad_cq,
            cq_other,
            (cross_in, (width, width), (0, 0)),
            x1,
            gains,
            dx2,
            (self_out, (width, width), (0, 0)),
            (p1, (rows, 3 * width), (0, 0)),
            probs,
            x,
            (proj, (width, 3 * width), (0, 0)),
            gain_grad,
        ],
        scalars=1,
    )

    (grads,) = call(
        functools.partial(attention_grad_kernel, chips),
        [((pb, 8 * share + 16, width), LOW)],
        [
            here,
            mix2,
            mix2_other,
            low_cross,
            h2,
            grad_cq,
            cq_other,
            mix1,
            low_self,
            h1,
            grad_p1,
            small,
        ]
        + pieces,
        scalars=1,
        scratch=[pltpu.VMEM((width, pb * share), LOW), pltpu.VMEM((pb * share, 6 * width), FULL)],
    )
    output = add_chips(all_chips(after(part_out, grads)))
    grads = exchange(grads, "pb")
    (grad_encoder,) = call(
        encoder_grad_kernel,
        [((passage, width), LOW)],
        [here, after(grad_mine, grad_p1), memory_other, memory_in],
        scalars=1,
    )
    grad_contract, *expand_rows = call(
        feed_total_kernel,
        [((slab, width), FULL)] + [((share, 2 * units), LOW)] * chips,
        [here, after(feed_grads, grad_p1)],
        scalars=1,
        scratch=[pltpu.VMEM((chips * share, 2 * units), FULL)],
    )
    expand_rows = [expand_rows[0]] + [swap_ctx(expand_rows[r], 2 * r) for r in range(1, chips)]
    (grad_expand,) = call(
        functools.partial(expand_total_kernel, pb),
        [((share, hidden), FULL)],
        [here] + expand_rows,
        scalars=1,
    )
    first = (mine_ctx & 1) == 0
    block_output = (x2 + join(first, output, swap_ctx(output, 1)).astype(FULL)).astype(LOW)
    (
        grad_self_projection,
        grad_self_output,
        grad_cross_query,
        grad_cross_output,
        mine,
        other,
        grad_norm_gains,
        grad_table,
    ) = call(
        attention_total_kernel,
        [((share, 3 * width), FULL)]
        + [((share, width), FULL)] * 5
        + [(norm_gains.shape[:1] + (share,), FULL), ((heads, buckets), FULL)],
        [here, grads, hot],
        scalars=1,
    )
    other = swap_ctx(other, 1)
    grad_cross_memory = jnp.concatenate(
        [join(first, mine[:, :half], other[:, :half]), join(first, mine[:, half:], other[:, half:])],
        axis=1,
    )
    return (
        block_output[None],
        grad_x[None],
        grad_encoder[None],
        grad_self_projection,
        grad_self_output,
        grad_cross_query,
        grad_cross_memory,
        grad_cross_output,
        grad_expand,
        grad_contract,
        grad_norm_gains,
        grad_table.T,
    )


def body(*args):
    decoder_in, encoder_out, self_projection = args[:3]
    contract_weight = args[8]
    fits = (
        lax.axis_size("ctx") == 8
        and lax.axis_size("pb") == 4
        and decoder_in.shape[0] == 1
        and decoder_in.shape[1] == 128
        and self_projection.shape[0] % 8 == 0
        and contract_weight.shape[0] * 2 == self_projection.shape[0] * lax.axis_size("ctx")
        and encoder_out.shape[1] % 16 == 0
    )
    return (fast_body if fits else plain_body)(*args)


def solution(mesh):
    return jax.shard_map(
        body,
        mesh=mesh,
        in_specs=(
            P("pb", None, None),
            P("pb", "ctx", None),
            P(("pb", "ctx"), None),
            P(("pb", "ctx"), None),
            P(("pb", "ctx"), None),
            P(("pb", "ctx"), None),
            P(("pb", "ctx"), None),
            P(("pb", "ctx"), None),
            P(("pb", "ctx"), None),
            P(None, ("pb", "ctx")),
            P(),
            P(),
            P("pb", "ctx"),
            P("pb"),
            P("pb"),
            P("pb", None, None),
        ),
        out_specs=(
            P("pb", None, None),
            P("pb", None, None),
            P("pb", "ctx", None),
            P(("pb", "ctx"), None),
            P(("pb", "ctx"), None),
            P(("pb", "ctx"), None),
            P(("pb", "ctx"), None),
            P(("pb", "ctx"), None),
            P(("pb", "ctx"), None),
            P(("pb", "ctx"), None),
            P(None, ("pb", "ctx")),
            P(),
        ),
        check_vma=False,
    )
```

```python
import functools
import math

import jax
import jax.numpy as jnp
from jax import lax
from jax.experimental import pallas as pl
from jax.experimental.pallas import tpu as pltpu
from jax.sharding import PartitionSpec as P

LOW, FULL = jnp.bfloat16, jnp.float32
MASKED = -1000000000.0
EPS = 1e-06
HEAD = 64
ALL_BYTES = 58 * 1024 * 1024
SPARE_BYTES = 6 * 1024 * 1024


def dot(left, right, left_axis=1, right_axis=0):
    return lax.dot_general(
        left,
        right,
        (((left_axis,), (right_axis,)), ((), ())),
        preferred_element_type=FULL,
    )


def dot_t(left, right):
    return dot(left, right, 1, 1)


def outer_sum(left, right):
    return dot(left, right, 0, 0)


def rms_unit(values):
    factor = lax.rsqrt(jnp.mean(values * values, axis=-1, keepdims=True) + EPS)
    return values * factor, factor


def norm_back(grad, unit, factor, gain):
    scaled = grad * gain
    return factor * (scaled - unit * jnp.mean(scaled * unit, axis=-1, keepdims=True))


class Leaving:
    def __init__(self, held, target, sem):
        self.held, self.shape, self.dtype = held, held.shape, held.dtype
        self.copy = pltpu.make_async_copy(held, target, sem)
        self.left = False

    def leave(self):
        if not self.left:
            self.copy.start()
            self.left = True

    def __getitem__(self, index):
        return self.held[index]

    def __setitem__(self, index, values):
        self.held[index] = values


def place_of_device():
    mine_pb, mine_ctx = lax.axis_index("pb"), lax.axis_index("ctx")
    return mine_ctx & 1, mine_ctx >> 1, mine_pb, mine_ctx, lax.axis_size("ctx")


def call(kernel, outs, args, scalars=0, scratch=(), limit=None):
    placed = args[0] is None
    if placed:
        args, scalars = args[1:], scalars - 1
    arrays, specs, grid, held = [], [], (), []
    far_outs = [index for index, out in enumerate(outs) if len(out) == 3]
    for index, arg in enumerate(args):
        if isinstance(arg, tuple):
            arg, shape, place = arg
            specs.append(pl.BlockSpec(shape, lambda i, place=place: place))
            grid = (1,)
            held.append((shape, arg.dtype))
        else:
            specs.append(pl.BlockSpec(memory_space=pltpu.SMEM if index < scalars else pltpu.VMEM))
            held.append((arg.shape, arg.dtype))
        arrays.append(arg)
    held += [out[:2] for out in outs] + [(one.shape, one.dtype) for one in scratch]
    size = sum(math.prod(shape) * jnp.dtype(dtype).itemsize for shape, dtype in held)
    buffers = [pltpu.VMEM(*outs[i][:2]) for i in far_outs]
    if buffers:
        buffers.append(pltpu.SemaphoreType.DMA((len(buffers),)))

    def run(*refs):
        ins, results = list(refs[: len(args)]), list(refs[len(args) : len(args) + len(outs)])
        rest = refs[len(args) + len(outs) :]
        own, extra = rest[: len(scratch)], rest[len(scratch) :]
        moved = []
        for k, i in enumerate(far_outs):
            results[i] = Leaving(extra[k], results[i], extra[-1].at[k])
            moved.append(results[i])
        kernel(*([place_of_device()] if placed else []), *ins, *results, *own)
        for one in moved:
            one.leave()
            one.copy.wait()

    return pl.pallas_call(
        run,
        grid=grid,
        out_shape=[
            pltpu.HBM(*out[:2]) if len(out) == 3 else jax.ShapeDtypeStruct(*out) for out in outs
        ],
        in_specs=specs,
        out_specs=[
            pl.BlockSpec(memory_space=pltpu.HBM if len(out) == 3 else pltpu.VMEM) for out in outs
        ],
        scratch_shapes=list(scratch) + buffers,
        compiler_params=pltpu.CompilerParams(vmem_limit_bytes=limit or size + SPARE_BYTES),
    )(*arrays)


def to_low(values):
    return values.astype(jnp.bfloat16)


def normalize(values, scale):
    factor = lax.rsqrt(jnp.mean(values * values, axis=-1, keepdims=True) + 1e-06)
    return (values * factor * scale, values * factor, factor)


def gelu_tanh(values):
    return jax.nn.gelu(values, approximate=True)


def fetch(shards):
    return (
        lax.all_gather(shards[0], ("pb", "ctx"), axis=0, tiled=True),
        lax.all_gather(shards[1], ("pb", "ctx"), axis=0, tiled=True),
        lax.all_gather(shards[2], ("pb", "ctx"), axis=0, tiled=True),
        lax.all_gather(shards[3], ("pb", "ctx"), axis=0, tiled=True),
        lax.all_gather(shards[4], ("pb", "ctx"), axis=0, tiled=True),
        lax.all_gather(shards[5], ("pb", "ctx"), axis=0, tiled=True),
        lax.all_gather(shards[6], ("pb", "ctx"), axis=0, tiled=True),
        lax.all_gather(shards[7], ("pb", "ctx"), axis=1, tiled=True),
    )


def run_forward(params, decoder, encoder, allowed, visible, rel_bias):
    projection, self_out, cross_in, memory_in, cross_out, expand, contract, gains = params
    scale_gain = gains.astype(jnp.float32)
    count, length, width = decoder.shape
    heads = rel_bias.shape[0]
    head_dim = width // heads
    inverse = head_dim ** (-0.5)
    residual = decoder.astype(jnp.float32).reshape(count * length, width)
    normed_a, unit_a, factor_a = normalize(residual, scale_gain[0])
    normed_a = to_low(normed_a)
    joined = to_low(dot(normed_a, projection)).reshape(count, length, 3, heads, head_dim)
    query_rows, key_rows, value_rows = (joined[:, :, 0], joined[:, :, 1], joined[:, :, 2])
    self_scores = (
        jnp.einsum("nihd,njhd->nhij", query_rows, key_rows, preferred_element_type=jnp.float32)
        * inverse
        + rel_bias[None]
    )
    self_probs = jax.nn.softmax(jnp.where(allowed, self_scores, -1000000000.0), axis=-1)
    self_mixed = jnp.einsum(
        "nhij,njhd->nihd", to_low(self_probs), value_rows, preferred_element_type=jnp.float32
    )
    self_mix = to_low(self_mixed.reshape(count * length, width))
    after_self = residual + dot(self_mix, self_out)
    normed_b, unit_b, factor_b = normalize(after_self, scale_gain[1])
    normed_b = to_low(normed_b)
    cross_rows = to_low(dot(normed_b, cross_in)).reshape(count, length, heads, head_dim)
    ctx_rows = encoder.shape[1]
    memory = to_low(dot(encoder.reshape(count * ctx_rows, width), memory_in)).reshape(
        count, ctx_rows, 2, heads, head_dim
    )
    cross_keys, cross_vals = (memory[:, :, 0], memory[:, :, 1])
    cross_scores = (
        jnp.einsum("nihd,njhd->nhij", cross_rows, cross_keys, preferred_element_type=jnp.float32)
        * inverse
    )
    masked = jnp.where(visible, cross_scores, -1000000000.0)
    highest_score = lax.pmax(jnp.max(masked, axis=-1), "ctx")
    total = lax.psum(
        jnp.sum(jnp.where(visible, jnp.exp(masked - highest_score[..., None]), 0.0), axis=-1), "ctx"
    )
    cross_probs = (
        jnp.where(visible, jnp.exp(masked - highest_score[..., None]), 0.0) / total[..., None]
    )
    partial_mix = jnp.einsum(
        "nhij,njhd->nihd", to_low(cross_probs), cross_vals, preferred_element_type=jnp.float32
    )
    cross_mixed = lax.psum(partial_mix, "ctx")
    cross_mix = to_low(cross_mixed.reshape(count * length, width))
    after_cross = after_self + dot(cross_mix, cross_out)
    normed_c, unit_c, factor_c = normalize(after_cross, scale_gain[2])
    normed_c = to_low(normed_c)
    hidden = dot(normed_c, expand)
    active = to_low(gelu_tanh(hidden))
    output = after_cross + dot(active, contract)
    saved = (
        normed_a,
        unit_a,
        factor_a,
        query_rows,
        key_rows,
        value_rows,
        self_probs,
        self_mix,
        normed_b,
        unit_b,
        factor_b,
        cross_rows,
        cross_keys,
        cross_vals,
        cross_probs,
        cross_mix,
        normed_c,
        unit_c,
        factor_c,
        hidden,
        active,
        scale_gain,
    )
    return (output, saved)


def plain_body(
    decoder_in,
    encoder_out,
    self_projection,
    self_output,
    cross_query,
    cross_memory,
    cross_output,
    expand_weight,
    contract_weight,
    norm_gains,
    bias_table,
    bucket_index,
    passage_mask,
    target_length,
    task_group,
    cotangent,
):
    shards = (
        self_projection,
        self_output,
        cross_query,
        cross_memory,
        cross_output,
        expand_weight,
        contract_weight,
        norm_gains,
    )
    count, length, width = decoder_in.shape
    ctx_rows = encoder_out.shape[1]
    buckets, heads = bias_table.shape
    head_dim = width // heads
    inverse = head_dim ** (-0.5)
    positions = jnp.arange(length)
    offsets = jnp.clip(positions[:, None] - positions[None, :], 0, length - 1)
    pair_bucket = jnp.take(bucket_index, offsets.reshape(-1))
    one_hot = (pair_bucket[:, None] == jnp.arange(buckets)[None, :]).astype(jnp.bfloat16)
    rel_bias = dot(one_hot, bias_table).T.reshape(heads, length, length)
    causal = positions[None, :] <= positions[:, None]
    allowed = (causal[None] & (positions[None, None, :] < target_length[:, None, None]))[:, None]
    visible = (passage_mask > 0)[:, None, None, :]
    params = fetch(shards)
    output, saved = run_forward(params, decoder_in, encoder_out, allowed, visible, rel_bias)
    projection, self_out, cross_in, memory_in, cross_out, expand, contract, gains = params
    (
        normed_a,
        unit_a,
        factor_a,
        query_rows,
        key_rows,
        value_rows,
        self_probs,
        self_mix,
        normed_b,
        unit_b,
        factor_b,
        cross_rows,
        cross_keys,
        cross_vals,
        cross_probs,
        cross_mix,
        normed_c,
        unit_c,
        factor_c,
        hidden,
        active,
        scale_gain,
    ) = saved
    rows_total = count * length
    share = rows_total // lax.axis_size("ctx")
    start = lax.axis_index("ctx") * share

    def sliced(values):
        return lax.dynamic_slice_in_dim(values, start, share, 0)

    task_scale = jnp.where(task_group == 0, 1.0, jnp.where(task_group == 1, 0.5, 2.0)).astype(
        jnp.float32
    )
    row_live = (positions[None, :] < target_length[:, None]).astype(jnp.float32)
    grad_out = (
        cotangent.astype(jnp.float32) * (task_scale[:, None] * row_live)[:, :, None]
    ).reshape(rows_total, width)
    low_out = to_low(grad_out)
    grad_active = dot_t(low_out, contract)
    unused_value, gelu_pull = jax.vjp(gelu_tanh, hidden)
    grad_hidden = to_low(gelu_pull(grad_active)[0])
    grad_normed_c = dot_t(grad_hidden, expand)
    gain_c = jnp.sum(sliced(grad_normed_c * unit_c), axis=0)
    grad_after_cross = grad_out + norm_back(grad_normed_c, unit_c, factor_c, scale_gain[2])
    low_cross = to_low(grad_after_cross)
    grad_mix = to_low(dot_t(low_cross, cross_out)).reshape(count, length, heads, head_dim)
    grad_probs = jnp.einsum(
        "nihd,njhd->nhij", grad_mix, cross_vals, preferred_element_type=jnp.float32
    )
    row_dot = lax.psum(jnp.sum(grad_probs * cross_probs, axis=-1), "ctx")
    grad_scores = to_low(cross_probs * (grad_probs - row_dot[..., None]))
    partial_query = (
        jnp.einsum("nhij,njhd->nihd", grad_scores, cross_keys, preferred_element_type=jnp.float32)
        * inverse
    )
    grad_query = to_low(lax.psum(partial_query, "ctx")).reshape(rows_total, width)
    grad_key = (
        jnp.einsum("nhij,nihd->njhd", grad_scores, cross_rows, preferred_element_type=jnp.float32)
        * inverse
    )
    grad_value = jnp.einsum(
        "nhij,nihd->njhd", to_low(cross_probs), grad_mix, preferred_element_type=jnp.float32
    )
    grad_memory = to_low(jnp.stack([grad_key, grad_value], axis=2)).reshape(
        count * ctx_rows, 2 * width
    )
    encoder_rows = encoder_out.reshape(count * ctx_rows, width)
    grad_cross_memory = outer_sum(encoder_rows, grad_memory)
    grad_encoder = to_low(dot_t(grad_memory, memory_in)).reshape(count, ctx_rows, width)
    grad_normed_b = dot_t(grad_query, cross_in)
    gain_b = jnp.sum(sliced(grad_normed_b * unit_b), axis=0)
    grad_after_self = grad_after_cross + norm_back(grad_normed_b, unit_b, factor_b, scale_gain[1])
    low_self = to_low(grad_after_self)
    grad_self_mix = to_low(dot_t(low_self, self_out)).reshape(count, length, heads, head_dim)
    grad_probs_self = jnp.einsum(
        "nihd,njhd->nhij", grad_self_mix, value_rows, preferred_element_type=jnp.float32
    )
    self_dot = jnp.sum(grad_probs_self * self_probs, axis=-1, keepdims=True)
    grad_scores_self = to_low(self_probs * (grad_probs_self - self_dot))
    pair_grad = jnp.sum(grad_scores_self.astype(jnp.float32), axis=0).reshape(
        heads, length * length
    )
    pair_count = length * length // lax.axis_size("ctx")
    pair_start = lax.axis_index("ctx") * pair_count
    pair_slice = lax.dynamic_slice_in_dim(pair_grad, pair_start, pair_count, 1)
    hot_slice = lax.dynamic_slice_in_dim(one_hot.astype(jnp.float32), pair_start, pair_count, 0)
    table_term = lax.dot_general(
        hot_slice,
        pair_slice,
        (((0,), (1,)), ((), ())),
        precision=lax.Precision.HIGHEST,
        preferred_element_type=jnp.float32,
    )
    grad_table = lax.psum(table_term, ("pb", "ctx"))
    grad_q = (
        jnp.einsum(
            "nhij,njhd->nihd", grad_scores_self, key_rows, preferred_element_type=jnp.float32
        )
        * inverse
    )
    grad_k = (
        jnp.einsum(
            "nhij,nihd->njhd", grad_scores_self, query_rows, preferred_element_type=jnp.float32
        )
        * inverse
    )
    grad_v = jnp.einsum(
        "nhij,nihd->njhd", to_low(self_probs), grad_self_mix, preferred_element_type=jnp.float32
    )
    grad_joined = to_low(jnp.stack([grad_q, grad_k, grad_v], axis=2)).reshape(rows_total, 3 * width)
    grad_normed_a = dot_t(grad_joined, projection)
    gain_a = jnp.sum(sliced(grad_normed_a * unit_a), axis=0)
    grad_decoder = to_low(
        grad_after_self + norm_back(grad_normed_a, unit_a, factor_a, scale_gain[0])
    ).reshape(count, length, width)
    gain_grads = jnp.stack([gain_a, gain_b, gain_c])
    pairs = (
        (normed_a, grad_joined),
        (self_mix, low_self),
        (normed_b, grad_query),
        (cross_mix, low_cross),
        (normed_c, grad_hidden),
        (active, low_out),
    )
    partials = tuple((outer_sum(sliced(left), sliced(right)) for left, right in pairs))
    summed = (
        lax.psum_scatter(partials[0], ("pb", "ctx"), scatter_dimension=0, tiled=True),
        lax.psum_scatter(partials[1], ("pb", "ctx"), scatter_dimension=0, tiled=True),
        lax.psum_scatter(partials[2], ("pb", "ctx"), scatter_dimension=0, tiled=True),
        lax.psum_scatter(grad_cross_memory, ("pb", "ctx"), scatter_dimension=0, tiled=True),
        lax.psum_scatter(partials[3], ("pb", "ctx"), scatter_dimension=0, tiled=True),
        lax.psum_scatter(partials[4], ("pb", "ctx"), scatter_dimension=0, tiled=True),
        lax.psum_scatter(partials[5], ("pb", "ctx"), scatter_dimension=0, tiled=True),
        lax.psum_scatter(gain_grads, ("pb", "ctx"), scatter_dimension=1, tiled=True),
    )
    block_output = to_low(output).reshape(count, length, width)
    return (
        block_output,
        grad_decoder,
        grad_encoder,
        summed[0],
        summed[1],
        summed[2],
        summed[3],
        summed[4],
        summed[5],
        summed[6],
        summed[7],
        grad_table,
    )


def swap_ctx(values, mask):
    size = lax.axis_size("ctx")
    return lax.ppermute(values, "ctx", [(i, i ^ mask) for i in range(size)])


def swap_pb(values, mask):
    size = lax.axis_size("pb")
    return lax.ppermute(values, "pb", [(i, i ^ mask) for i in range(size)])


def exchange(values, axis):
    return lax.all_to_all(values, axis, 0, 0, tiled=True)


def all_pb(values):
    size = lax.axis_size("pb")
    return [values] + [swap_pb(values, r) for r in range(1, size)]


def after(values, earlier):
    return lax.optimization_barrier((values, earlier))[0]


def all_chips(values):
    return [values] + [swap_ctx(values, mask) for mask in range(2, lax.axis_size("ctx"), 2)]


def tree(terms):
    while len(terms) > 1:
        terms = [a + b for a, b in zip(terms[0::2], terms[1::2])]
    return terms[0]


def add_chips(parts):
    return tree([part.astype(FULL) for part in parts]).astype(LOW)


def to_owners(parts):
    return [parts[0]] + [swap_pb(part, r) for r, part in enumerate(parts) if r]


def pick(low, high):
    lanes = lax.broadcasted_iota(jnp.int32, low.shape, 1)
    return jnp.where(lanes < low.shape[1] // 2, low, high)


def lane_mask(values, side):
    zeros = jnp.zeros_like(values)
    return pick(values, zeros) if side == 0 else pick(zeros, values)


def both_heads(values):
    return jnp.concatenate([lane_mask(values, 0), lane_mask(values, 1)], axis=0)


def pick_rows(values):
    middle = values.shape[0] // 2
    return pick(values[:middle], values[middle:])


def join(first, mine, other, axis=1):
    return jnp.where(
        first,
        jnp.concatenate([mine, other], axis=axis),
        jnp.concatenate([other, mine], axis=axis),
    )


def half_of(first, values, axis=1):
    middle = values.shape[axis] // 2
    if axis == 0:
        return jnp.where(first, values[:middle], values[middle:])
    return jnp.where(first, values[:, :middle], values[:, middle:])


CORE, CHIP, PB, CTX = range(4)


def prepare_kernel(proj, self_out, cross_in, gains, out):
    count = gains.shape[0]
    row = lax.broadcasted_iota(jnp.int32, (count, 128), 0)
    lane = lax.broadcasted_iota(jnp.int32, (count, 128), 1)
    columns = outer_sum(gains[...], jnp.where(row == lane, 1.0, 0.0).astype(LOW)).astype(LOW)
    at = 0
    for part in (proj[...], self_out[...], cross_in[...], columns):
        out[:, at : at + part.shape[1]] = part
        at += part.shape[1]


def block_places(pb):
    middle = pb // 2
    return [
        [(0, 0), (0, 1), (0, 2)],
        [(r, 0) for r in range(1, pb)],
        [(r, 1) for r in range(1, pb)],
        [(r, 2) for r in range(1, pb)],
        [(r, 3) for r in range(middle)],
        [(r, 3) for r in range(middle, pb)],
    ]


def place(here, ins, outs, ctx):
    first = here[CORE] == 0
    pb = ins[2].shape[0] + 1
    rows = ins[0].shape[1]
    for i, places in enumerate(block_places(pb)):
        mine, other = ins[2 * i], ins[2 * i + 1]
        for k, (z, flip) in enumerate(places):
            both = join(first, mine[k], other[k], 0)
            owner = (z ^ here[PB]) * (ctx // 2) + (here[CHIP] ^ flip)
            slot = pl.multiple_of(owner * 2 * rows, 16)
            at = 0
            for out in outs:
                width = out.shape[1]
                out[pl.ds(slot, 2 * rows), :] = both[:, at : at + width]
                at += width


def first_hops(own):
    return swap_ctx(own, 2), swap_ctx(own, 4)


def gather_rows(own, along, far, far_along):
    middle = (far.shape[0] + 1) // 2
    low = jnp.concatenate([along[0][None], far_along[0][: middle - 1]])
    low = swap_ctx(low, 4)
    high = swap_ctx(far_along[1][middle - 1 :], 2)
    blocks = []
    for array in (jnp.stack([own, *along]), far, *far_along, low, high):
        blocks += [array, swap_ctx(array, 1)]
    return blocks, (low, high)


def self_kernel(ctx, here, length, x, table, *refs):
    blocks, refs = refs[:-12], refs[-12:]
    proj, self_out, cross_in, gains_out, p1, probs, mix, x1, h1, h2, cq, columns = refs
    rows, width = x.shape
    heads = width // HEAD
    pair = 2 * HEAD
    inverse = jnp.asarray(HEAD ** (-0.5), LOW)
    place(here, blocks, [proj, self_out, cross_in, columns], ctx)
    for one in (proj, self_out, cross_in):
        one.leave()
    gains = columns[...].astype(FULL).T
    gains_out[...] = gains[: gains_out.shape[0]]
    xf = x[...].astype(FULL)
    unit, _ = rms_unit(xf)
    normed = (unit * gains[0:1, :]).astype(LOW)
    h1[...] = normed
    joined = dot(normed, proj[...]).astype(LOW)
    p1[...] = joined
    p1.leave()
    row = lax.broadcasted_iota(jnp.int32, (rows, rows), 0)
    col = lax.broadcasted_iota(jnp.int32, (rows, rows), 1)
    allowed = (col <= row) & (col < length[0])
    barred = jnp.where(allowed, 0.0, MASKED)
    mixes = []
    for g in range(heads // 2):
        at = g * pair
        q = both_heads(joined[:, at : at + pair] * inverse)
        k = joined[:, width + at : width + at + pair]
        v = joined[:, 2 * width + at : 2 * width + at + pair]
        bias = [
            pltpu.roll(
                jnp.broadcast_to(table[head : head + 1, :], (rows, rows)),
                1,
                axis=1,
                stride=1,
                stride_axis=0,
            )
            + barred
            for head in (2 * g, 2 * g + 1)
        ]
        scores = dot_t(q, k) + jnp.concatenate(bias, axis=0)
        powers = jnp.exp(scores - jnp.max(scores, axis=-1, keepdims=True))
        prob = powers * (1.0 / jnp.sum(powers, axis=-1, keepdims=True))
        probs[g] = prob
        mixes.append(pick_rows(dot(prob.astype(LOW), v)).astype(LOW))
    probs.leave()
    mixes = jnp.concatenate(mixes, axis=1)
    mix[...] = mixes
    after_self = xf + dot(mixes, self_out[...])
    x1[...] = after_self
    unit, _ = rms_unit(after_self)
    normed = (unit * gains[1:2, :]).astype(LOW)
    h2[...] = normed
    cq[...] = dot(normed, half_of(here[CORE] == 0, cross_in[...])).astype(LOW)


def memory_kernel(ctx, here, mine, other, *refs):
    blocks, (memory_in, memory) = refs[:-2], refs[-2:]
    place(here, blocks, [memory_in], ctx)
    memory_in.leave()
    first = here[CORE] == 0
    width = mine.shape[1]
    keys = half_of(first, memory_in[:, :width])
    values = half_of(first, memory_in[:, width:])
    weight = jnp.concatenate([keys, values], axis=1)
    rows = mine.shape[0]
    memory[:rows] = dot(mine[...], weight).astype(LOW)
    memory[rows:] = dot(other[...], weight).astype(LOW)


def pack_stats(tops, totals):
    rows = tops[0].shape[0]
    lanes = lax.broadcasted_iota(jnp.int32, (rows, 128), 1)
    columns = jnp.zeros((rows, 128), FULL)
    for index, column in enumerate(tops + totals):
        columns = jnp.where(lanes // 3 == index, column, columns)
    high = columns.astype(LOW).astype(FULL)
    middle = (columns - high).astype(LOW).astype(FULL)
    kind = lanes % 3
    return jnp.where(kind == 0, high, jnp.where(kind == 1, middle, columns - high - middle)).astype(
        LOW
    )


def read_stats(packed):
    values = packed.astype(FULL)
    return values + pltpu.roll(values, 127, axis=1) + pltpu.roll(values, 126, axis=1)


def cross_kernel(cq, memory, visible, packed):
    rows, half = cq.shape
    pair = 2 * HEAD
    inverse = jnp.asarray(HEAD ** (-0.5), LOW)
    barred = jnp.where(visible[...] > 0, 0.0, MASKED)
    tops, totals, mixes = [], [], []
    for at in range(0, half, pair):
        q = both_heads(cq[:, at : at + pair] * inverse)
        k = memory[:, at : at + pair]
        v = memory[:, half + at : half + at + pair]
        scores = dot_t(q, k) + barred
        top = jnp.max(scores, axis=-1, keepdims=True)
        powers = jnp.exp(scores - top)
        total = jnp.sum(powers, axis=-1, keepdims=True)
        tops += [top[:rows], top[rows:]]
        totals += [total[:rows], total[rows:]]
        mixes.append(pick_rows(dot(powers.astype(LOW), v)).astype(LOW))
    packed[...] = jnp.concatenate(mixes + [pack_stats(tops, totals)], axis=1)


def spread(columns):
    shape = (columns[0].shape[0], 2 * HEAD)
    return jnp.concatenate(
        [
            pick(jnp.broadcast_to(a, shape), jnp.broadcast_to(b, shape))
            for a, b in zip(columns[0::2], columns[1::2])
        ],
        axis=1,
    )


def merge_kernel(here, *refs):
    ins, mix, stats = refs[:-2], refs[-2], refs[-1]
    half = mix.shape[1]
    heads = half // HEAD
    packed = [ref[...] for ref in ins]
    step = 1
    while step < len(packed):
        flip = (here[CHIP] & step) != 0
        packed = [jnp.where(flip, packed[i ^ step], packed[i]) for i in range(len(packed))]
        step *= 2
    read = [read_stats(p[:, half:]) for p in packed]
    top = read[0]
    for other in read[1:]:
        top = jnp.maximum(top, other)
    lanes = lax.broadcasted_iota(jnp.int32, top.shape, 1)
    is_top = lanes < 3 * heads
    scales = [jnp.exp(jnp.where(is_top, r - top, 0.0)) for r in read]
    total = tree([r * pltpu.roll(w, 3 * heads, axis=1) for r, w in zip(read, scales)])
    share = 1.0 / pltpu.roll(total, 128 - 3 * heads, axis=1)
    weights = [w * share for w in scales]
    terms = [
        p[:, :half].astype(FULL) * spread([w[:, 3 * h : 3 * h + 1] for h in range(heads)])
        for p, w in zip(packed, weights)
    ]
    mix[...] = tree(terms).astype(LOW)
    stats[...] = jnp.where(is_top, top, total)


def gelu_parts(values):
    slope = (2.0 / jnp.pi) ** 0.5
    square = values * values
    bent = jnp.tanh(slope * (values + 0.044715 * values * square))
    active = 0.5 * values * (1.0 + bent)
    inner = slope * (1.0 + 3 * 0.044715 * square)
    return active, 0.5 * (1.0 + bent) + 0.5 * values * (1.0 - bent * bent) * inner


def task_rows(length, task, cot):
    rows = lax.broadcasted_iota(jnp.int32, cot.shape, 0)
    weight = jnp.where(task[0] == 0, 1.0, jnp.where(task[0] == 1, 0.5, 2.0)).astype(FULL)
    return jnp.where(rows < length[0], cot[...].astype(FULL) * weight, 0.0)


def feed_weights(here, mine, other, expand, contract):
    first = here[CORE] == 0
    width = contract.shape[1]
    slab = mine.shape[1]
    share = slab // 4
    for z in range(mine.shape[0]):
        owner = z
        contract[pl.ds(pl.multiple_of(2 * owner * slab, 16), 2 * slab), :] = join(
            first, mine[z, :, :width], other[z, :, :width], 0
        )
        for r in range(4):
            rows = slice(r * share, (r + 1) * share)
            both = join(first, mine[z, rows, width:], other[z, rows, width:], 0)
            at = pl.multiple_of((owner * 4 + (here[CHIP] ^ r)) * 2 * share, 16)
            expand[pl.ds(at, 2 * share), :] = both


def feed_kernel(
    ctx,
    here,
    length,
    task,
    mix_mine,
    mix_other,
    x1,
    gains,
    feed_mine,
    feed_other,
    cot,
    *refs,
):
    blocks, outs = refs[:-10], refs[-10:]
    place(here, blocks, [outs[0]], ctx)
    outs[0].leave()
    feed_step(
        here, length, task, mix_mine, mix_other, x1, gains, feed_mine, feed_other, cot, *outs
    )


def feed_step(
    here,
    length,
    task,
    mix_mine,
    mix_other,
    x1,
    gains,
    feed_mine,
    feed_other,
    cot,
    cross_out,
    x2,
    h3,
    active,
    low_out,
    grad_hidden,
    partial,
    part_out,
    expand,
    contract,
):
    first = here[CORE] == 0
    after_cross = x1[...] + dot(join(first, mix_mine[...], mix_other[...]), cross_out[...])
    x2[...] = after_cross
    x2.leave()
    unit, _ = rms_unit(after_cross)
    normed = (unit * gains[2:3, :]).astype(LOW)
    h3[...] = normed
    low = task_rows(length, task, cot).astype(LOW)
    low_out[...] = low
    feed_weights(here, feed_mine, feed_other, expand, contract)
    value, slope = gelu_parts(dot(normed, expand[...]))
    value = value.astype(LOW)
    grad = (dot_t(low, contract[...]) * slope).astype(LOW)
    active[...] = value
    grad_hidden[...] = grad
    partial[...] = dot_t(grad, half_of(first, expand[...], 0)).astype(LOW)
    partial.leave()
    part_out[...] = dot(value, half_of(first, contract[...])).astype(LOW)


def feed_grad_kernel(share, here, active, low_out, h3, grad_hidden, out, contract, expand):
    contract[...] = outer_sum(active[...], low_out[...])
    expand[...] = outer_sum(h3[...], grad_hidden[...])
    pb = out.shape[0]
    slab = contract.shape[0] // pb // 2
    block = expand.shape[0] // pb
    for z in range(pb):
        at = pl.multiple_of((2 * z + here[CORE]) * slab, 16)
        out[z, :slab] = contract[pl.ds(at, slab)].astype(LOW)
        rows = [
            expand[pl.ds(pl.multiple_of(z * block + at + here[CORE] * share, 8), share)]
            for at in range(0, block, 2 * share)
        ]
        out[z, slab:] = jnp.concatenate(rows, axis=0).astype(LOW)


def cross_back_kernel(
    here,
    length,
    task,
    sums_mine,
    sums_other,
    x2,
    gains,
    cot,
    cross_out,
    cq,
    memory,
    visible,
    stats,
    mix,
    dx2,
    low_cross,
    grad_cq,
    grad_mine,
    grad_other,
    gain_grad,
):
    first = here[CORE] == 0
    half = mix.shape[1]
    heads = half // HEAD
    pair = 2 * HEAD
    inverse = jnp.asarray(HEAD ** (-0.5), LOW)
    unit, factor = rms_unit(x2[...])
    grad = join(first, sums_mine[...], sums_other[...]).astype(FULL)
    gain_grad[...] = jnp.sum(grad * unit, axis=0, keepdims=True)
    back = task_rows(length, task, cot) + norm_back(grad, unit, factor, gains[2:3, :])
    dx2[...] = back
    low = back.astype(LOW)
    low_cross[...] = low
    grad_mix = dot_t(low, half_of(first, cross_out[...], 0)).astype(LOW)
    barred = jnp.where(visible[...] > 0, 0.0, MASKED)
    shares = 1.0 / stats[...]
    passage = grad_mine.shape[0]
    for g in range(heads // 2):
        at = g * pair
        q = both_heads(cq[:, at : at + pair] * inverse)
        do = both_heads(grad_mix[:, at : at + pair])
        k = memory[:, at : at + pair]
        v = memory[:, half + at : half + at + pair]
        mixed = mix[:, at : at + pair].astype(FULL)
        top, scale = [
            jnp.concatenate([a[:, c : c + 1], a[:, c + 3 : c + 4]], axis=0)
            for a, c in ((stats, 6 * g), (shares, 3 * heads + 6 * g))
        ]
        rho = jnp.sum(
            do.astype(FULL) * jnp.concatenate([mixed, mixed], axis=0), axis=-1, keepdims=True
        )
        prob = jnp.exp(dot_t(q, k) + barred - top) * scale
        grad_scores = (prob * (dot_t(do, v) - rho)).astype(LOW)
        grad_cq[:, at : at + pair] = (pick_rows(dot(grad_scores, k)) * HEAD ** (-0.5)).astype(LOW)
        keys = outer_sum(grad_scores, q).astype(LOW)
        values = outer_sum(prob.astype(LOW), do).astype(LOW)
        for ref, begin in ((grad_mine, 0), (grad_other, passage)):
            ref[:, at : at + pair] = keys[begin : begin + passage]
            ref[:, half + at : half + at + pair] = values[begin : begin + passage]


def memory_grad_kernel(pb, here, mine, other, grad_mine, grad_other, *refs):
    outs, whole = refs[:-1], refs[-1]
    whole[...] = outer_sum(mine[...], grad_mine[...]) + outer_sum(other[...], grad_other[...])
    share = whole.shape[0] // pb // len(outs)
    for r, out in enumerate(outs):
        chip = here[CHIP] ^ r
        for z in range(pb):
            at = pl.multiple_of((z * len(outs) + chip) * share, 16)
            out[z * share : (z + 1) * share] = whole[pl.ds(at, share)].astype(LOW)


def encoder_grad_kernel(here, mine, other, memory_in, grad):
    first = here[CORE] == 0
    half = mine.shape[1] // 2
    keys = join(first, mine[:, :half], other[:, :half])
    values = join(first, mine[:, half:], other[:, half:])
    grad[...] = dot_t(jnp.concatenate([keys, values], axis=1), memory_in[...]).astype(LOW)


def owned(left, choose):
    return dot(left, choose).astype(LOW)


def self_back_kernel(
    here,
    cq_mine,
    cq_other,
    cross_in,
    x1,
    gains,
    dx2,
    self_out,
    p1,
    probs,
    x,
    proj,
    gain_grad,
    low_self,
    grad_p1,
    grad_x,
    small,
):
    rows, width = x.shape
    heads = width // HEAD
    pair = 2 * HEAD
    inverse = jnp.asarray(HEAD ** (-0.5), LOW)
    grad = dot_t(join(here[CORE] == 0, cq_mine[...], cq_other[...]), cross_in[...])
    unit, factor = rms_unit(x1[...])
    small[...] = jnp.zeros_like(small)
    small[1:2, :] = jnp.sum(grad * unit, axis=0, keepdims=True)
    small[2:3, :] = gain_grad[...]
    dx1 = dx2[...] + norm_back(grad, unit, factor, gains[1:2, :])
    low = dx1.astype(LOW)
    low_self[...] = low
    row = lax.broadcasted_iota(jnp.int32, (rows, rows), 0)
    col = lax.broadcasted_iota(jnp.int32, (rows, rows), 1)
    flip = jnp.where(row + col == rows - 1, 1.0, 0.0).astype(LOW)
    grad_mix = dot_t(low, self_out[...]).astype(LOW)
    parts = [[], [], []]
    for g in range(heads // 2):
        at = g * pair
        q = both_heads(p1[:, at : at + pair] * inverse)
        k = p1[:, width + at : width + at + pair]
        v = p1[:, 2 * width + at : 2 * width + at + pair]
        do = both_heads(grad_mix[:, at : at + pair])
        prob = probs[g]
        grad_probs = dot_t(do, v)
        rho = jnp.sum(prob * grad_probs, axis=-1, keepdims=True)
        grad_scores = (prob * (grad_probs - rho)).astype(LOW)
        turned = dot(flip, jnp.concatenate([grad_scores[:rows], grad_scores[rows:]], axis=1))
        for side in range(2):
            part = turned[:, side * rows : (side + 1) * rows]
            part = pltpu.roll(part, 0, axis=1, stride=1, stride_axis=0)
            head = 3 + 2 * g + side
            small[head : head + 1, :rows] = jnp.sum(part, axis=0, keepdims=True)
        parts[0].append((pick_rows(dot(grad_scores, k)) * HEAD ** (-0.5)).astype(LOW))
        parts[1].append(outer_sum(grad_scores, q).astype(LOW))
        parts[2].append(outer_sum(prob.astype(LOW), do).astype(LOW))
    joined = jnp.concatenate(parts[0] + parts[1] + parts[2], axis=1)
    grad_p1[...] = joined
    grad = dot_t(joined, proj[...])
    unit, factor = rms_unit(x[...].astype(FULL))
    small[0:1, :] = jnp.sum(grad * unit, axis=0, keepdims=True)
    grad_x[...] = (dx1 + norm_back(grad, unit, factor, gains[0:1, :])).astype(LOW)


def feed_total_kernel(here, parts, contract, *refs):
    outs, rows = refs[:-1], refs[-1]
    total = tree([parts[z].astype(FULL) for z in range(parts.shape[0])])
    slab = contract.shape[0]
    contract[...] = total[:slab]
    rows[...] = total[slab:]
    share = outs[0].shape[0]
    for r, out in enumerate(outs):
        out[...] = rows[pl.ds(pl.multiple_of((here[CHIP] ^ r) * share, 8), share)].astype(LOW)


def expand_total_kernel(pb, here, *refs):
    parts, out = [ref[...].astype(FULL) for ref in refs[:-1]], refs[-1]
    step = 1
    while step < len(parts):
        flip = (here[CHIP] & step) != 0
        parts = [jnp.where(flip, parts[i ^ step], parts[i]) for i in range(len(parts))]
        step *= 2
    units = parts[0].shape[1] // pb
    out[...] = jnp.concatenate(
        [part[:, q * units : (q + 1) * units] for q in range(pb) for part in parts], axis=1
    )


def attention_grad_kernel(
    count,
    here,
    mix_mine,
    mix_other,
    low_cross,
    h2,
    cq_mine,
    cq_other,
    mix1,
    low_self,
    h1,
    grad_p1,
    small,
    *refs,
):
    pieces, out, choose, sums = refs[:count], *refs[count:]
    first = here[CORE] == 0
    pb = out.shape[0]
    width = mix1.shape[1]
    share = sums.shape[0] // pb
    lane = lax.broadcasted_iota(jnp.int32, choose.shape, 1)
    row = lax.broadcasted_iota(jnp.int32, choose.shape, 0)
    mine = lane // share * (width // pb) + here[CTX] * share + lane % share
    choose[...] = jnp.where(row == mine, 1.0, 0.0).astype(LOW)

    def owned(left, right):
        return outer_sum(dot(left, choose[...]).astype(LOW), right)

    sums[:, : 3 * width] = owned(h1[...], grad_p1[...])
    sums[:, 3 * width : 4 * width] = owned(mix1[...], low_self[...])
    cq = join(first, cq_mine[...], cq_other[...])
    sums[:, 4 * width : 5 * width] = owned(h2[...], cq)
    mix2 = join(first, mix_mine[...], mix_other[...])
    sums[:, 5 * width :] = owned(mix2, low_cross[...])
    total = tree([piece[...].astype(FULL) for piece in pieces])
    both = 2 * share
    for z in range(pb):
        rows = sums[z * share : (z + 1) * share]
        blocks = [rows[:, a : a + width] for a in range(0, 6 * width, width)]
        blocks += [total[z * both : (z + 1) * both], small[...]]
        out[z] = jnp.concatenate(blocks, axis=0).astype(LOW)


def attention_total_kernel(
    here, parts, hot, proj_grad, out_grad, query_grad, cross_grad, mine, other, gain_grad, table
):
    total = tree([parts[z].astype(FULL) for z in range(parts.shape[0])])
    first = here[CORE] == 0
    share, width = out_grad.shape
    blocks = [total[a : a + share] for a in range(0, 8 * share, share)]
    proj_grad[...] = jnp.concatenate(blocks[:3], axis=1)
    out_grad[...] = blocks[3]
    query_grad[...] = blocks[4]
    cross_grad[...] = blocks[5]
    mine[...] = jnp.where(first, blocks[6], blocks[7])
    other[...] = jnp.where(first, blocks[7], blocks[6])
    small = total[8 * share :]
    gains = gain_grad.shape[0]
    rows = hot.shape[1]
    shape = (width, share)
    place_of = lax.broadcasted_iota(jnp.int32, shape, 1) + (here[PB] * here[4] + here[CTX]) * share
    chosen = jnp.where(lax.broadcasted_iota(jnp.int32, shape, 0) == place_of, 1.0, 0.0)
    highest = lax.Precision.HIGHEST
    gain_grad[...] = jnp.dot(small, chosen, precision=highest, preferred_element_type=FULL)[:gains]
    heads = table.shape[0]
    whole = lax.dot_general(
        small[:, :rows],
        hot[...].astype(FULL),
        (((1,), (1,)), ((), ())),
        precision=highest,
        preferred_element_type=FULL,
    )
    table[...] = whole[gains : gains + heads]


def fast_body(
    decoder_in,
    encoder_out,
    self_projection,
    self_output,
    cross_query,
    cross_memory,
    cross_output,
    expand_weight,
    contract_weight,
    norm_gains,
    bias_table,
    bucket_index,
    passage_mask,
    target_length,
    task_group,
    cotangent,
):
    pb, ctx = lax.axis_size("pb"), lax.axis_size("ctx")
    mine_pb, mine_ctx = lax.axis_index("pb"), lax.axis_index("ctx")
    here = None
    rows, width = decoder_in.shape[1:]
    half = width // 2
    passage = encoder_out.shape[1]
    buckets, heads = bias_table.shape
    share = self_projection.shape[0]
    hidden = expand_weight.shape[1]
    slab = contract_weight.shape[0]
    units = pb * slab
    chips = ctx // 2
    x, e, cot = decoder_in[0], encoder_out[0], cotangent[0]

    (columns,) = call(
        prepare_kernel,
        [((share, 5 * width + 128), LOW)],
        [self_projection, self_output, cross_query, norm_gains],
    )
    along = first_hops(columns)
    far = jnp.stack(all_pb(columns)[1:])
    mixed = expand_weight.reshape(share, pb, chips, 2 * slab).transpose(2, 0, 1, 3)
    mixed = mixed.reshape(chips, share, 2 * units)
    chip = mine_ctx >> 1
    mixed = [lax.dynamic_index_in_dim(mixed, chip ^ r, 0, False) for r in range(chips)]
    mixed = jnp.concatenate([mixed[0]] + [swap_ctx(mixed[r], 2 * r) for r in range(1, chips)])
    e_other = swap_ctx(e, 1)
    visible = jnp.concatenate([passage_mask, swap_ctx(passage_mask, 1)], axis=1)
    others = jnp.concatenate([cross_memory, cross_output], axis=1)
    others_along = first_hops(after(others, along))
    far_along = first_hops(after(far, (e_other, visible, mixed, others_along)))
    proj_blocks, _ = gather_rows(columns, along, far, far_along)
    others_far = jnp.stack(all_pb(after(others, far))[1:])
    others_far_along = first_hops(after(others_far, far_along))
    others_blocks, last = gather_rows(others, others_along, others_far, others_far_along)
    x = after(x, others_far_along)
    feed = jnp.concatenate([contract_weight, mixed], axis=1)
    feed = jnp.broadcast_to(after(feed, others_far)[None], (pb,) + feed.shape)
    feed = exchange(feed, "pb")

    hot = (jnp.arange(buckets)[:, None] == bucket_index[::-1][None, :]).astype(LOW)
    table = outer_sum(bias_table, hot)

    proj, self_out, cross_in, gains, p1, probs, mix1, x1, h1, h2, cq = call(
        functools.partial(self_kernel, ctx),
        [
            ((width, 3 * width), LOW, True),
            ((width, width), LOW, True),
            ((width, width), LOW, True),
            ((norm_gains.shape[0], width), FULL),
            ((rows, 3 * width), LOW, True),
            ((heads // 2, 2 * rows, rows), FULL, True),
            ((rows, width), LOW),
            ((rows, width), FULL),
            ((rows, width), LOW),
            ((rows, width), LOW),
            ((rows, half), LOW),
        ],
        [here, target_length, x, table] + proj_blocks,
        scalars=2,
        scratch=[pltpu.VMEM((width, 128), LOW)],
        limit=ALL_BYTES,
    )
    def part(size, index):
        return [(b, b.shape[:2] + (size * width,), (0, 0, index)) for b in others_blocks]

    feed = after(feed, cq)
    feed_other = swap_ctx(feed, 1)
    memory_in, memory = call(
        functools.partial(memory_kernel, ctx),
        [((width, 2 * width), LOW, True), ((2 * passage, width), LOW)],
        [here, e, e_other] + part(2, 0),
        scalars=1,
    )
    (packed,) = call(cross_kernel, [((rows, half + 128), LOW)], [cq, memory, visible])
    mix2, stats = call(
        merge_kernel,
        [((rows, half), LOW), ((rows, 128), FULL)],
        [here] + all_chips(packed),
        scalars=1,
    )
    mix2_other = swap_ctx(mix2, 1)

    cross_out, x2, h3, active, low_out, grad_hidden, partial, part_out = call(
        functools.partial(feed_kernel, ctx),
        [
            ((width, width), LOW, True),
            ((rows, width), FULL, True),
            ((rows, width), LOW),
            ((rows, 2 * units), LOW),
            ((rows, width), LOW),
            ((rows, 2 * units), LOW),
            ((rows, half), LOW, True),
            ((rows, half), LOW),
        ],
        [
            here,
            target_length,
            task_group,
            mix2,
            mix2_other,
            x1,
            gains,
            feed,
            feed_other,
            cot,
        ]
        + part(1, 2),
        scalars=3,
        scratch=[pltpu.VMEM((width, 2 * units), LOW), pltpu.VMEM((2 * units, width), LOW)],
    )
    partials = all_chips(partial)
    sums = add_chips(partials)
    sums_other = swap_ctx(sums, 1)
    (feed_grads,) = call(
        functools.partial(feed_grad_kernel, share),
        [((pb, 2 * slab, width), LOW)],
        [here, after(active, partials), low_out, h3, grad_hidden],
        scalars=1,
        scratch=[pltpu.VMEM((2 * units, width), FULL), pltpu.VMEM((width, 2 * units), FULL)],
    )
    feed_grads = exchange(feed_grads, "pb")

    dx2, low_cross, grad_cq, grad_mine, grad_other, gain_grad = call(
        cross_back_kernel,
        [
            ((rows, width), FULL),
            ((rows, width), LOW),
            ((rows, half), LOW),
            ((passage, width), LOW),
            ((passage, width), LOW),
            ((1, width), FULL),
        ],
        [
            here,
            target_length,
            task_group,
            sums,
            sums_other,
            x2,
            gains,
            cot,
            (cross_out, (width, width), (0, 0)),
            cq,
            memory,
            visible,
            stats,
            mix2,
        ],
        scalars=3,
    )
    grad_cq = add_chips(all_chips(grad_cq))
    cq_other = swap_ctx(grad_cq, 1)
    pieces = call(
        functools.partial(memory_grad_kernel, pb),
        [((pb * 2 * share, width), LOW)] * chips,
        [here, e, e_other, grad_mine, grad_other],
        scalars=1,
        scratch=[pltpu.VMEM((width, width), FULL)],
    )
    pieces = [pieces[0]] + [swap_ctx(pieces[r], 2 * r) for r in range(1, chips)]
    memory_other = swap_ctx(grad_other, 1)

    low_self, grad_p1, grad_x, small = call(
        self_back_kernel,
        [
            ((rows, width), LOW),
            ((rows, 3 * width), LOW),
            ((rows, width), LOW),
            ((16, width), FULL),
        ],
        [
            here,
            (grad_cq, (rows, half), (0, 0)),
            (cq_other, (rows, half), (0, 0)),
            (cross_in, (width, width), (0, 0)),
            x1,
            gains,
            dx2,
            (self_out, (width, width), (0, 0)),
            (p1, (rows, 3 * width), (0, 0)),
            (probs, (heads // 2, 2 * rows, rows), (0, 0, 0)),
            x,
            (proj, (width, 3 * width), (0, 0)),
            gain_grad,
        ],
        scalars=1,
    )

    (grads,) = call(
        functools.partial(attention_grad_kernel, chips),
        [((pb, 8 * share + 16, width), LOW)],
        [
            here,
            mix2,
            mix2_other,
            low_cross,
            h2,
            grad_cq,
            cq_other,
            mix1,
            low_self,
            h1,
            grad_p1,
            small,
        ]
        + pieces,
        scalars=1,
        scratch=[pltpu.VMEM((width, pb * share), LOW), pltpu.VMEM((pb * share, 6 * width), FULL)],
    )
    output = add_chips(all_chips(after(part_out, grads)))
    grads = exchange(grads, "pb")
    (grad_encoder,) = call(
        encoder_grad_kernel,
        [((passage, width), LOW)],
        [here, after(grad_mine, grad_p1), memory_other, memory_in],
        scalars=1,
    )
    grad_contract, *expand_rows = call(
        feed_total_kernel,
        [((slab, width), FULL)] + [((share, 2 * units), LOW)] * chips,
        [here, after(feed_grads, grad_p1)],
        scalars=1,
        scratch=[pltpu.VMEM((chips * share, 2 * units), FULL)],
    )
    expand_rows = [expand_rows[0]] + [swap_ctx(expand_rows[r], 2 * r) for r in range(1, chips)]
    (grad_expand,) = call(
        functools.partial(expand_total_kernel, pb),
        [((share, hidden), FULL)],
        [here] + expand_rows,
        scalars=1,
    )
    first = (mine_ctx & 1) == 0
    block_output = (x2 + join(first, output, swap_ctx(output, 1)).astype(FULL)).astype(LOW)
    (
        grad_self_projection,
        grad_self_output,
        grad_cross_query,
        grad_cross_output,
        mine,
        other,
        grad_norm_gains,
        grad_table,
    ) = call(
        attention_total_kernel,
        [((share, 3 * width), FULL)]
        + [((share, width), FULL)] * 5
        + [(norm_gains.shape[:1] + (share,), FULL), ((heads, buckets), FULL)],
        [here, grads, hot],
        scalars=1,
    )
    other = swap_ctx(other, 1)
    grad_cross_memory = jnp.concatenate(
        [join(first, mine[:, :half], other[:, :half]), join(first, mine[:, half:], other[:, half:])],
        axis=1,
    )
    return (
        block_output[None],
        grad_x[None],
        grad_encoder[None],
        grad_self_projection,
        grad_self_output,
        grad_cross_query,
        grad_cross_memory,
        grad_cross_output,
        grad_expand,
        grad_contract,
        grad_norm_gains,
        grad_table.T,
    )


def body(*args):
    decoder_in, encoder_out, self_projection = args[:3]
    contract_weight = args[8]
    fits = (
        lax.axis_size("ctx") == 8
        and lax.axis_size("pb") == 4
        and decoder_in.shape[0] == 1
        and decoder_in.shape[1] == 128
        and self_projection.shape[0] % 8 == 0
        and contract_weight.shape[0] * 2 == self_projection.shape[0] * lax.axis_size("ctx")
        and encoder_out.shape[1] % 16 == 0
    )
    return (fast_body if fits else plain_body)(*args)


def solution(mesh):
    return jax.shard_map(
        body,
        mesh=mesh,
        in_specs=(
            P("pb", None, None),
            P("pb", "ctx", None),
            P(("pb", "ctx"), None),
            P(("pb", "ctx"), None),
            P(("pb", "ctx"), None),
            P(("pb", "ctx"), None),
            P(("pb", "ctx"), None),
            P(("pb", "ctx"), None),
            P(("pb", "ctx"), None),
            P(None, ("pb", "ctx")),
            P(),
            P(),
            P("pb", "ctx"),
            P("pb"),
            P("pb"),
            P("pb", None, None),
        ),
        out_specs=(
            P("pb", None, None),
            P("pb", None, None),
            P("pb", "ctx", None),
            P(("pb", "ctx"), None),
            P(("pb", "ctx"), None),
            P(("pb", "ctx"), None),
            P(("pb", "ctx"), None),
            P(("pb", "ctx"), None),
            P(("pb", "ctx"), None),
            P(("pb", "ctx"), None),
            P(None, ("pb", "ctx")),
            P(),
        ),
        check_vma=False,
    )
```
